128 devices in a mesh: shard: 2 (over x_lo), context: 16 (over z, x_hi, core), tensor: 4 (over y).
Axes of the slice: x: 4 (x_hi: 2, x_lo: 2; x = x_hi * 2 + x_lo), y: 4, z: 4, core: 2. Of those that a mesh axis runs over, the one named last changes fastest.
Arguments:
- activations: bfloat16 [8192, 1536], P(('shard', 'context')), may hold values from -6 to 6
- gain_attn: bfloat16 [1536], P('shard'), may hold values from 0.5 to 1.5
- w_query: bfloat16 [1536, 1536], P('shard', 'tensor'), may hold values from -0.21875 to 0.21875
- w_key: bfloat16 [1536, 512], P('shard', 'tensor'), may hold values from -0.15625 to 0.15625
- w_value: bfloat16 [1536, 512], P('shard', 'tensor'), may hold values from -0.15625 to 0.15625
- w_out: bfloat16 [1536, 1536], P('tensor', 'shard'), may hold values from -0.625 to 0.625
- gain_moe: bfloat16 [1536], P('shard'), may hold values from 0.5 to 1.5
- expert_gate: bfloat16 [10, 1536, 512], P(None, 'shard', 'tensor'), may hold values from -0.15625 to 0.15625
- expert_up: bfloat16 [10, 1536, 512], P(None, 'shard', 'tensor'), may hold values from -0.15625 to 0.15625
- expert_down: bfloat16 [10, 512, 1536], P(None, 'tensor', 'shard'), may hold values from -0.75 to 0.75
- routes: int32 [8192, 8], P(('shard', 'context')), may hold values from 0 to 9, all different within a row; in each aligned block of 256 rows (0 to 255, 256 to 511, ...) at most 256 rows name the same one
- route_gates: float32 [8192, 8], P(('shard', 'context')), may hold values from 0.06 to 0.2
- layout: int32 [32], replicated, may hold values from 0 to 31, each once
- out_grad: bfloat16 [8192, 1536], P(('shard', 'context')), may hold values from -6 to 6
Outputs:
- output: bfloat16 [8192, 1536], P(('shard', 'context'))
- input_grad: float32 [8192, 1536], P(('shard', 'context'))
- gain_attn_grad: float32 [1536], P('shard')
- w_query_grad: float32 [1536, 1536], P('shard', 'tensor')
- w_key_grad: float32 [1536, 512], P('shard', 'tensor')
- w_value_grad: float32 [1536, 512], P('shard', 'tensor')
- w_out_grad: float32 [1536, 1536], P('tensor', 'shard')
- gain_moe_grad: float32 [1536], P('shard')
- expert_gate_grad: float32 [10, 1536, 512], P(None, 'shard', 'tensor')
- expert_up_grad: float32 [10, 1536, 512], P(None, 'shard', 'tensor')
- expert_down_grad: float32 [10, 512, 1536], P(None, 'tensor', 'shard')
The draws below stay inside these ranges and needn't reach their ends.
Inputs may be any that keep to these rules, and one draw needn't show every extreme that they name: `routes`: in the rows of one device no expert is named by more than 256 rows; some expert reaches 256. Each number once; stored segment j of 128 rows of every sequence holds the sequence's segment layout[j].
All inputs are finite; a program needn't handle non-finite values.
Results may differ from the reference program's by a relative error of at most 0.03.
Values may be sent and summed in bfloat16 or wider, within the bound.
No kernel may reach another device: no remote copies, remote signals or barrier semaphores. Data moves between devices by JAX's collectives and lax.ppermute only.
A program may use at most 256 MiB of HBM per device.

```python
import math
import jax
import jax.numpy as jnp
import numpy as np
from jax import lax

D = 1536
HEADS = 24
KV_HEADS = 8
HD = 64
FF = 512
EXPERTS = 10
TOP = 8
BLK = 256
LENGTH = 4096
TOKENS = 8192
CAP = 256
N_CONTEXT = 16


def block_scale(rng, dims, split, smallest, high):
    def one(position, parts):
        heights = jax.random.uniform(jax.random.fold_in(jax.random.fold_in(rng, 6), position), (parts,), jnp.float32, smallest / len(split), high / len(split))
        return jnp.repeat(jnp.exp(heights), dims[position] // parts).reshape((-1,) + (1,) * (len(dims) - position - 1))

    level = one(*split[0])
    for cut in split[1:]:
        level = level * one(*cut)
    return level


def shared_out(own_key, own, number, rows, number_of, top, limit, lean):
    order = jax.random.permutation(own_key, number_of)
    packed, common = shares(number_of, rows * top, limit, lean, True), shares(number_of, rows * top, limit, lean, False)
    places = jnp.arange(number_of)

    def named(tallies, offset_by):
        used = int((tallies > 0).sum())
        fixed = max(1, used // 4)
        passed = fixed + (places - fixed + offset_by * (used - fixed)) % max(1, number_of - fixed)
        return jnp.zeros((number_of,), jnp.int32).at[order[jnp.where(places < fixed, places, passed)]].set(jnp.asarray(tallies, jnp.int32))

    tallies = jnp.where(number % 4 == 0, named(packed, number // 4), named(common, number - number // 4 - 1))
    mixed = jax.random.permutation(jax.random.fold_in(own, 3), number_of)
    giver, sink = mixed[0:number_of // 2 * 2:2], mixed[1:number_of // 2 * 2:2]
    room = jnp.minimum(tallies[giver] - 1, limit - tallies[sink]) // 2
    room = jnp.where((giver == order[0]) | (sink == order[0]) | (tallies[sink] == 0), 0, jnp.maximum(room, 0))
    passed = jax.random.randint(jax.random.fold_in(own, 4), (number_of // 2,), 0, 1 << 20) % (room + 1)
    tallies = tallies.at[giver].add(-passed).at[sink].add(passed)
    labels = jnp.searchsorted(jnp.cumsum(tallies), jnp.arange(rows * top), side="right").astype(jnp.int32)
    listing = labels.reshape(top, rows).T
    listing = listing[jax.random.permutation(jax.random.fold_in(own, 1), rows)]
    offset_by = jax.random.randint(jax.random.fold_in(own, 2), (rows, 1), 0, top)
    return jnp.take_along_axis(listing, (jnp.arange(top)[None, :] + offset_by) % top, axis=1)


def shares(amount, total, bound, lean, full):
    weights = [(1 << 20) // math.isqrt(rank ** lean) + 1 for rank in range(1, amount + 1)]
    largest = bound if full else min(bound, max(-(-total // amount), total * weights[0] // sum(weights)))
    least = 1 if total - largest >= amount - 1 else 0
    counts, rest = [largest] + [least] * (amount - 1), total - largest - least * (amount - 1)
    while rest > 0:
        free = [i for i in range(1, amount) if counts[i] < largest] or [i for i in range(1, amount) if counts[i] < bound]
        pool, remaining = sum([weights[i] for i in free]), rest
        for i in free:
            more = min(bound - counts[i], max(1, remaining * weights[i] // pool), rest)
            counts[i] = counts[i] + more
            rest = rest - more
    return np.array(counts)


def bell_draw(rng, extent, scale, limit, split=(), kind=jnp.bfloat16):
    factor_of = block_scale(rng, extent, split, -0.22, 0.18) if split else 1.0
    result = jax.random.normal(rng, extent, jnp.float32) * scale * factor_of
    return jnp.minimum(jnp.maximum(result, -limit), limit).astype(kind)


def setup_inputs(seed: int = 0) -> dict:
    seeds = jax.random.split(jax.random.key(seed), 15)
    activations = bell_draw(seeds[0], (TOKENS, D), 1.0, 6.0, ((0, 32),))
    gain_attn = jnp.clip(1.0 + 0.1 * jax.random.normal(seeds[1], (D,), jnp.float32), 0.5, 1.5).astype(jnp.bfloat16)
    w_query = bell_draw(seeds[2], (D, HEADS * HD), (D * 4 // 9) ** -0.5, 0.21875, ((0, 2), (1, 4)))
    w_key = bell_draw(seeds[3], (D, KV_HEADS * HD), D ** -0.5, 0.15625, ((0, 2), (1, 4)))
    w_value = bell_draw(seeds[4], (D, KV_HEADS * HD), D ** -0.5, 0.15625, ((0, 2), (1, 4)))
    w_out = bell_draw(seeds[5], (HEADS * HD, D), (HEADS * HD // 16) ** -0.5, 0.625, ((0, 4), (1, 2)))
    gain_moe = jnp.clip(1.0 + 0.1 * jax.random.normal(seeds[6], (D,), jnp.float32), 0.5, 1.5).astype(jnp.bfloat16)
    expert_gate = bell_draw(seeds[7], (EXPERTS, D, FF), D ** -0.5, 0.15625, ((1, 2), (2, 4)))
    expert_up = bell_draw(seeds[8], (EXPERTS, D, FF), D ** -0.5, 0.15625, ((1, 2), (2, 4)))
    expert_down = bell_draw(seeds[9], (EXPERTS, FF, D), (FF // 8) ** -0.5, 0.75, ((1, 4), (2, 2)))
    routes_keys = jax.random.split(jax.random.fold_in(seeds[10], 1), TOKENS // BLK)
    routes_turns = jax.random.permutation(jax.random.fold_in(seeds[10], 3), TOKENS // BLK)
    routes = jax.vmap(lambda own, number: shared_out(jax.random.fold_in(seeds[10], 2), own, number, BLK, EXPERTS, TOP, CAP, 1))(routes_keys, routes_turns).reshape((TOKENS, TOP))
    route_gates = jnp.clip(jnp.exp(math.log(0.2) - 1.2039728 * jax.random.uniform(seeds[11], (TOKENS, TOP), jnp.float32) ** block_scale(seeds[11], (TOKENS, TOP), ((0, 32),), -0.2, 0.2)), 0.06, 0.2)
    layout = jax.random.permutation(seeds[12], 2 * N_CONTEXT).astype(jnp.int32)
    out_grad = bell_draw(seeds[13], (TOKENS, D), 1.0, 6.0, ((0, 32),))
    return dict(activations=activations, gain_attn=gain_attn, w_query=w_query, w_key=w_key, w_value=w_value, w_out=w_out, gain_moe=gain_moe, expert_gate=expert_gate, expert_up=expert_up, expert_down=expert_down, routes=routes, route_gates=route_gates, layout=layout, out_grad=out_grad)


EPS = 1e-05
HIGH = lax.Precision.HIGHEST

@jax.custom_vjp
def low(v):
    return lax.optimization_barrier(v.astype(jnp.bfloat16)).astype(jnp.float32)

@jax.custom_vjp
def low_back(v):
    return v

def low_keep(v):
    return (low(v), None)

def low_pass(kept, grad):
    return (grad,)

def back_keep(v):
    return (v, None)

def back_low(kept, grad):
    return (low(grad),)
low.defvjp(low_keep, low_pass)
low_back.defvjp(back_keep, back_low)

def rotate_half(vector):
    middle = vector.shape[-1] // 2
    return jnp.concatenate([-vector[..., middle:], vector[..., :middle]], axis=-1)

def rope_tables(positions, width):
    steps_f = jnp.arange(0, width, 2).astype(jnp.float32) / width
    freqs = jnp.power(10000.0, -steps_f)
    angles = positions.astype(jnp.float32)[:, None] * freqs[None, :]
    angles = jnp.concatenate([angles, angles], axis=-1)
    return (jnp.cos(angles), jnp.sin(angles))

def rms_norm(source, gain):
    return source * lax.rsqrt(lax.optimization_barrier(jnp.mean(source * source, axis=-1, keepdims=True)) + EPS) * gain

def slot_places(route_rows, capacity, count):
    flat_ids = route_rows.reshape(-1).astype(jnp.int32)
    onehot = (flat_ids[:, None] == jnp.arange(count, dtype=jnp.int32)[None, :]).astype(jnp.int32)
    earlier = jnp.cumsum(onehot, axis=0) - onehot
    slot = lax.optimization_barrier(jnp.sum(earlier * onehot, axis=1))
    return (flat_ids * capacity + slot).astype(jnp.int32).reshape(route_rows.shape)

def slot_owners(places, capacity, count):
    total = capacity * count
    row_count, top_count = places.shape
    flat = places.reshape(-1)
    owner_ids = jnp.repeat(jnp.arange(row_count, dtype=jnp.int32), top_count)
    owner = jnp.zeros((total,), jnp.int32).at[flat].set(owner_ids)
    filled = jnp.zeros((total,), jnp.float32).at[flat].set(1.0)
    return (owner, filled)

def attention_block(query_block, block_pos, sequence, keys_seq, values_seq, key_pos):
    keys = lax.dynamic_index_in_dim(keys_seq, sequence, 0, keepdims=False)
    values = lax.dynamic_index_in_dim(values_seq, sequence, 0, keepdims=False)
    row_count = query_block.shape[0]
    grouped = query_block.reshape(row_count, KV_HEADS, HEADS // KV_HEADS, HD)
    scores = jnp.einsum('qkgd,lkd->kgql', grouped, keys, precision=HIGH) * float(HD) ** (-0.5)
    scores = low_back(scores)
    allowed = key_pos[None, :] <= block_pos[:, None]
    scores = jnp.where(allowed[None, None], scores, -1e+30)
    probs = low(jax.nn.softmax(scores, axis=-1))
    mixed = jnp.einsum('kgql,lkd->qkgd', probs, values, precision=HIGH)
    return mixed.reshape(row_count, HEADS * HD)

def expert_block(normed_rows, places, gates, w_gate, w_up, w_down):
    owner, filled = slot_owners(places, CAP, EXPERTS)
    tiles = (jnp.take(normed_rows, owner, axis=0) * filled[:, None]).reshape(EXPERTS, CAP, D)
    gate_value = low_back(jnp.einsum('ecd,edf->ecf', tiles, w_gate, precision=HIGH))
    up_value = low_back(jnp.einsum('ecd,edf->ecf', tiles, w_up, precision=HIGH))
    hidden_units = low(jax.nn.silu(gate_value) * up_value)
    expert_rows = low_back(jnp.einsum('ecf,efd->ecd', hidden_units, w_down, precision=HIGH)).reshape(EXPERTS * CAP, D)
    picked = jnp.take(expert_rows, places.reshape(-1), axis=0).reshape(places.shape[0], TOP, D)
    return lax.optimization_barrier(jnp.sum(picked * gates[:, :, None], axis=1))

def forward(activations, gain_attn, w_query, w_key, w_value, w_out, gain_moe, expert_gate, expert_up, expert_down, positions, key_pos, places, route_gates):
    normed_one = low(rms_norm(activations, gain_attn))
    queries = low_back(jnp.dot(normed_one, w_query, precision=HIGH)).reshape(TOKENS, HEADS, HD)
    keys = low_back(jnp.dot(normed_one, w_key, precision=HIGH)).reshape(TOKENS, KV_HEADS, HD)
    values = low(low_back(jnp.dot(normed_one, w_value, precision=HIGH))).reshape(TOKENS, KV_HEADS, HD)
    cosine, sine = rope_tables(positions, HD)
    q_rot = low(queries * cosine[:, None] + rotate_half(queries) * sine[:, None])
    k_rot = low(keys * cosine[:, None] + rotate_half(keys) * sine[:, None])
    block_rows = min(512, LENGTH)
    blocks = TOKENS // block_rows
    seq_ids = (jnp.arange(blocks, dtype=jnp.int32) // (LENGTH // block_rows)).astype(jnp.int32)
    keys_seq = k_rot.reshape(TOKENS // LENGTH, LENGTH, KV_HEADS, HD)
    values_seq = values.reshape(TOKENS // LENGTH, LENGTH, KV_HEADS, HD)
    attend_step = jax.checkpoint(attention_block)
    mixed = lax.map(lambda item: attend_step(item[0], item[1], item[2], keys_seq, values_seq, key_pos), (q_rot.reshape(blocks, block_rows, HEADS, HD), positions.reshape(blocks, block_rows), seq_ids))
    mixed = low(low_back(mixed.reshape(TOKENS, HEADS * HD)))
    attended = low_back(jnp.dot(mixed, w_out, precision=HIGH))
    hidden_state = activations + attended
    normed_two = low(rms_norm(hidden_state, gain_moe))
    groups = TOKENS // BLK
    expert_step = jax.checkpoint(expert_block)
    mixture = lax.map(lambda item: expert_step(item[0], item[1], item[2], expert_gate, expert_up, expert_down), (normed_two.reshape(groups, BLK, D), places, route_gates.reshape(groups, BLK, TOP)))
    return hidden_state + mixture.reshape(TOKENS, D)

def reference(activations, gain_attn, w_query, w_key, w_value, w_out, gain_moe, expert_gate, expert_up, expert_down, routes, route_gates, layout, out_grad):
    half_rows = BLK // 2
    spots = jnp.arange(LENGTH, dtype=jnp.int32)
    key_pos = (jnp.take(layout, spots // half_rows) * half_rows + spots % half_rows).astype(jnp.int32)
    positions = jnp.tile(key_pos, TOKENS // LENGTH)
    places = jax.vmap(lambda block: slot_places(block, CAP, EXPERTS))(routes.reshape(TOKENS // BLK, BLK, TOP))
    inputs = tuple((array_in.astype(jnp.float32) for array_in in (activations, gain_attn, w_query, w_key, w_value, w_out, gain_moe, expert_gate, expert_up, expert_down)))
    gates = route_gates.astype(jnp.float32)

    def closed(*values):
        return forward(*values, positions, key_pos, places, gates)
    output, pullback = jax.vjp(closed, *inputs)
    d_input, d_gain_one, d_query, d_key, d_value, d_out, d_gain_two, d_gate, d_up, d_down = pullback(out_grad.astype(jnp.float32))
    return (output.astype(jnp.bfloat16), d_input, d_gain_one, d_query, d_key, d_value, d_out, d_gain_two, d_gate, d_up, d_down)
```

```python
import functools

import jax
import jax.numpy as jnp
import numpy as np
from jax import lax
from jax.experimental import pallas as pl
from jax.experimental.pallas import tpu as pltpu
from jax.sharding import Mesh
from jax.sharding import PartitionSpec as P

D = 1536
HALF = 768
HD = 64
EXPERTS = 10
OWN = 5
FC = 128
EPS = 1e-05
SCALE = 0.125
CHUNK = 512
SEG = 128
ROWS = 3 * SEG
NEG = -1e30
B16 = jnp.bfloat16
F32 = jnp.float32
X = ("shard", "xh")
PLANE = ("shard", "xh", "z")
VMEM = pltpu.VMEM
SMEM = pltpu.SMEM


def nn(a, b):
    return lax.dot_general(a, b, (((1,), (0,)), ((), ())), preferred_element_type=F32)


def nt(a, b):
    return lax.dot_general(a, b, (((1,), (1,)), ((), ())), preferred_element_type=F32)


def tn(a, b):
    return lax.dot_general(a, b, (((0,), (0,)), ((), ())), preferred_element_type=F32)


def x_pairs(k):
    pairs = []
    for sh in range(2):
        for xh in range(2):
            at = (2 * xh + sh + k) % 4
            pairs.append((sh * 2 + xh, (at % 2) * 2 + at // 2))
    return pairs


def to_x(v, k):
    return lax.ppermute(v, X, x_pairs(k))


def other_core(v):
    return lax.ppermute(v, "core", [(0, 1), (1, 0)])


def context_pairs(dz, dx):
    return [
        (zz * 2 + xx, ((zz + dz) % 4) * 2 + (xx + dx) % 2) for zz in range(4) for xx in range(2)
    ]


def over_y(v):
    return lax.all_to_all(v, "tensor", 0, 0, tiled=True)


def half_of(s):
    return pl.ds(pl.multiple_of(s * HALF, HALF), HALF)


def seg_of(info, layout, slot, blk, j):
    dz, dx = slot // 2, slot % 2
    zz = lax.rem(info[2] - dz + 4, 4)
    xx = lax.rem(info[3] + dx, 2)
    cc = info[1] if blk == 0 else 1 - info[1]
    return layout[((zz * 2 + xx) * 2 + cc) * 2 + j]


def angle_rows(at, ca, sa, cb, sb):
    ca, sa = ca[pl.ds(at, 1), :], sa[pl.ds(at, 1), :]
    return ca * cb[...] - sa * sb[...], sa * cb[...] + ca * sb[...]


def low_lanes(shape):
    return lax.broadcasted_iota(jnp.int32, shape, 1) < HD


def first_half_of_head(shape):
    return (lax.broadcasted_iota(jnp.int32, shape, 1) & (HD - 1)) < HD // 2


def rope(u, cos, sin):
    turned = jnp.where(
        first_half_of_head(u.shape), -pltpu.roll(u, 96, 1), pltpu.roll(u, 32, 1)
    )
    return u * cos + turned * sin


def unrope(u, cos, sin):
    w = u * sin
    turned = jnp.where(
        first_half_of_head(u.shape), pltpu.roll(w, 96, 1), -pltpu.roll(w, 32, 1)
    )
    return u * cos + turned


def qkv_kernel(
    info, layout, xo, xt, gain_o, gain_t, wa, wb, ra, rb, ca, sa, cb, sb, a_out, q_out, kv_out
):
    s = info[0]
    for blk, ref in enumerate((xo, xt)):
        lo = ref[:, half_of(s)].astype(F32)
        hi = ref[:, half_of(1 - s)].astype(F32)
        mean = (
            jnp.sum(lo * lo, axis=1, keepdims=True) + jnp.sum(hi * hi, axis=1, keepdims=True)
        ) / D
        inv = lax.rsqrt(mean + EPS)
        alo = (lo * inv * gain_o[...].astype(F32)).astype(B16)
        ahi = (hi * inv * gain_t[...].astype(F32)).astype(B16)
        a_out[blk * 256 : blk * 256 + 256, :HALF] = alo
        a_out[blk * 256 : blk * 256 + 256, HALF:] = ahi
        t = (
            nn(alo[:, :384], wa[...])
            + nn(alo[:, 384:], wb[...])
            + nn(ahi[:, :384], ra[...])
            + nn(ahi[:, 384:], rb[...])
        )
        for j in range(2):
            cos, sin = angle_rows(seg_of(info, layout, 0, blk, j), ca, sa, cb, sb)
            tt = t[j * SEG : (j + 1) * SEG]
            low = low_lanes((SEG, SEG))
            t0 = rope(tt[:, :128], cos, sin)
            t1 = rope(tt[:, 128:256], cos, sin)
            t2 = tt[:, 256:]
            rows = slice(blk * 256 + j * SEG, blk * 256 + (j + 1) * SEG)
            zero = jnp.zeros_like(t0)

            def scaled(v):
                return (v.astype(B16).astype(F32) * SCALE).astype(B16)

            q_out[0, rows] = scaled(jnp.where(low, t0, zero))
            q_out[1, rows] = scaled(jnp.where(low, pltpu.roll(t0, HD, 1), zero))
            q_out[2, rows] = scaled(jnp.where(low, t1, zero))
            kv_out[rows] = jnp.where(low, pltpu.roll(t1, HD, 1), t2).astype(B16)


def fill_sorted(info, layout, slots, ks, kst):
    for slot in range(8):
        for blk in range(2):
            for j in range(2):
                at = pl.multiple_of(seg_of(info, layout, slot, blk, j) * SEG, SEG)
                part = slots[slot][blk * 256 + j * SEG : blk * 256 + (j + 1) * SEG, :]
                ks[pl.ds(at, SEG), :] = part
                kst[:, pl.ds(at, SEG)] = part.astype(F32).T.astype(B16)


def allowed_keys(j, pos):
    key = j * CHUNK + lax.broadcasted_iota(jnp.int32, (CHUNK, ROWS), 0)
    query = pos * SEG + (lax.broadcasted_iota(jnp.int32, (CHUNK, ROWS), 1) & (SEG - 1))
    return key <= query


def heads_of(q, i):
    return jnp.concatenate([q[h, i * SEG : (i + 1) * SEG, :] for h in range(3)], axis=0)


def attend_kernel(info, layout, q, *refs):
    slots, o_out, lse_out, ks, kst = refs[:8], refs[8], refs[9], refs[10], refs[11]
    fill_sorted(info, layout, slots, ks, kst)
    low = low_lanes((SEG, SEG))
    for i in range(4):
        pos = seg_of(info, layout, 0, i // 2, i % 2)
        qi = heads_of(q, i)
        full = lax.div(pos, CHUNK // SEG)

        def step(j, carry, edge=False):
            top, total, acc = carry
            at = pl.multiple_of(j * CHUNK, CHUNK)
            sc = nt(ks[pl.ds(at, CHUNK), :], qi)
            if edge:
                sc = jnp.where(allowed_keys(j, pos), sc, NEG)
            new = jnp.maximum(top, jnp.max(sc, axis=0, keepdims=True))
            e = jnp.exp(sc - new)
            back = jnp.exp(top - new)
            total = total * back + jnp.sum(e, axis=0, keepdims=True)
            acc = acc * back + nn(kst[:, pl.ds(at, CHUNK)], e.astype(B16))
            return new, total, acc

        start = (
            jnp.full((1, ROWS), NEG, F32),
            jnp.zeros((1, ROWS), F32),
            jnp.zeros((SEG, ROWS), F32),
        )
        top, total, acc = step(full, lax.fori_loop(0, full, step, start), edge=True)
        lse_out[i] = top + jnp.log(total)
        o = (acc / total).T
        o0, o1, o2 = o[:SEG], o[SEG : 2 * SEG], o[2 * SEG :]
        rows = slice(i * SEG, (i + 1) * SEG)
        o_out[rows, :SEG] = jnp.where(low, pltpu.roll(o0, HD, 1), o1).astype(B16)
        o_out[rows, SEG:] = jnp.where(low, pltpu.roll(o2, HD, 1), jnp.zeros_like(o2)).astype(B16)


def attend_back_kernel(info, layout, q, do_own, do_oth, o, lse, ca, sa, cb, sb, *refs):
    slots, dq_out, dkv_out, ks, kst, dkv = refs[:8], refs[8], refs[9], refs[10], refs[11], refs[12]
    fill_sorted(info, layout, slots, ks, kst)
    dkv[...] = jnp.zeros_like(dkv)
    low = low_lanes((SEG, SEG))

    def spread(t0, t1):
        zero = jnp.zeros((SEG, SEG), F32)
        return jnp.concatenate(
            [
                jnp.where(low, zero, pltpu.roll(t0, HD, 1)),
                jnp.where(low, zero, t0),
                jnp.where(low, zero, pltpu.roll(t1, HD, 1)),
            ],
            axis=0,
        )

    for i in range(4):
        pos = seg_of(info, layout, 0, i // 2, i % 2)
        qi = heads_of(q, i)
        do = do_own if i < 2 else do_oth
        here = slice((i % 2) * SEG, (i % 2 + 1) * SEG)
        rows = slice(i * SEG, (i + 1) * SEG)
        dof = spread(do[here, :SEG].astype(F32), do[here, SEG:].astype(F32))
        of = spread(o[rows, :SEG].astype(F32), o[rows, SEG:].astype(F32))
        delta = jnp.sum((dof * of).T, axis=0, keepdims=True)
        doi = dof.astype(B16)
        lse_i = lse[i]
        full = lax.div(pos, CHUNK // SEG)

        def step(j, acc, edge=False):
            at = pl.multiple_of(j * CHUNK, CHUNK)
            kv = ks[pl.ds(at, CHUNK), :]
            p = jnp.exp(nt(kv, qi) - lse_i)
            if edge:
                p = jnp.where(allowed_keys(j, pos), p, 0.0)
            ds = (p * (nt(kv, doi) - delta)).astype(B16)
            dkv[pl.ds(at, CHUNK), :] += nn(ds, qi) + nn(p.astype(B16), doi)
            return acc + nn(kst[:, pl.ds(at, CHUNK)], ds)

        acc = step(full, lax.fori_loop(0, full, step, jnp.zeros((SEG, ROWS), F32)), edge=True)
        dq = acc.T * SCALE
        cos, sin = angle_rows(pos, ca, sa, cb, sb)
        d0, d1, d2 = [unrope(dq[h * SEG : (h + 1) * SEG], cos, sin) for h in range(3)]
        dq_out[rows, :SEG] = jnp.where(low, d0, pltpu.roll(d1, HD, 1)).astype(B16)
        dq_out[rows, SEG:] = jnp.where(low, d2, jnp.zeros_like(d2)).astype(B16)
    for slot in range(8):
        for blk in range(2):
            for j in range(2):
                at = pl.multiple_of(seg_of(info, layout, slot, blk, j) * SEG, SEG)
                dkv_out[slot, blk * 256 + j * SEG : blk * 256 + (j + 1) * SEG, :] = dkv[
                    pl.ds(at, SEG), :
                ].astype(B16)


def token_kernel(info, x, o_tok, w_own, w_oth, gain_o, gain_t, h_out, b_out):
    s = info[0]
    here = pl.ds(pl.multiple_of(info[4] * 64, 64), 64)
    acc = jnp.zeros((64, D), F32)
    for y in range(4):
        acc += nn(o_tok[y, :, :192], w_own[y]) + nn(o_tok[y, :, 256:448], w_oth[y])
    lo = x[here, half_of(s)].astype(F32) + acc[:, :HALF]
    hi = x[here, half_of(1 - s)].astype(F32) + acc[:, HALF:]
    mean = (
        jnp.sum(lo * lo, axis=1, keepdims=True) + jnp.sum(hi * hi, axis=1, keepdims=True)
    ) / D
    inv = lax.rsqrt(mean + EPS)
    h_out[:, :HALF] = lo
    h_out[:, HALF:] = hi
    b_out[:, :HALF] = (lo * inv * gain_o[...].astype(F32)).astype(B16)
    b_out[:, HALF:] = (hi * inv * gain_t[...].astype(F32)).astype(B16)


def norm_back(grads, sources, gains):
    mean = sum(jnp.sum(v * v, axis=1, keepdims=True) for v in sources) / D
    inv = lax.rsqrt(mean + EPS)
    weighted = [d * g for d, g in zip(grads, gains)]
    dot = sum(jnp.sum(w * v, axis=1, keepdims=True) for w, v in zip(weighted, sources)) / D
    cube = inv * inv * inv * dot
    return (
        [inv * w - v * cube for w, v in zip(weighted, sources)],
        [jnp.sum(d * v * inv, axis=0, keepdims=True) for d, v in zip(grads, sources)],
    )


def token_back_kernel(
    info, h, db, g, w_own, w_oth, gain_o, gain_t, dh_out, dattn_out, do_out, gain_out
):
    s = info[0]
    here = pl.ds(pl.multiple_of(info[4] * 64, 64), 64)
    total = sum(db[y].astype(F32) for y in range(4))
    halves = (slice(0, HALF), slice(HALF, D))
    back, gsum = norm_back(
        [total[:, k] for k in halves],
        [h[:, k] for k in halves],
        [gain_o[...].astype(F32), gain_t[...].astype(F32)],
    )
    for k, part, sums, half in zip(halves, back, gsum, (s, 1 - s)):
        dh = g[here, half_of(half)].astype(F32) + part
        dh_out[:, k] = dh
        dattn_out[:, k] = dh.astype(B16)
        gain_out[:, k] = sums
    dattn = dattn_out[...]
    pad = jnp.zeros((64, 64), B16)
    for y in range(4):
        do_out[y, :, 0:192] = nt(dattn, w_own[y]).astype(B16)
        do_out[y, :, 192:256] = pad
        do_out[y, :, 256:448] = nt(dattn, w_oth[y]).astype(B16)
        do_out[y, :, 448:512] = pad


def input_back_kernel(info, dh, da, x, gain_o, gain_t, ig_out, gain_out):
    s = info[0]
    here = pl.ds(pl.multiple_of(info[4] * 64, 64), 64)
    total = sum(da[y].astype(F32) for y in range(4))
    halves = (slice(0, HALF), slice(HALF, D))
    back, gsum = norm_back(
        [total[:, k] for k in halves],
        [x[here, half_of(half)].astype(F32) for half in (s, 1 - s)],
        [gain_o[...].astype(F32), gain_t[...].astype(F32)],
    )
    for k, part, sums in zip(halves, back, gsum):
        ig_out[:, k] = (dh[:, k] + part).astype(B16)
        gain_out[:, k] = sums


def qkv_back_kernel(info, layout, dq, own, others, wa, wb, ra, rb, ca, sa, cb, sb, d_out, da_own, da_oth):
    for i in range(4):
        rows = slice(i * SEG, (i + 1) * SEG)
        total = own[rows].astype(F32)
        for r in range(7):
            total += others[r, rows].astype(F32)
        cos, sin = angle_rows(seg_of(info, layout, 0, i // 2, i % 2), ca, sa, cb, sb)
        low = low_lanes((SEG, SEG))
        dk = unrope(total, cos, sin)
        d_out[rows, :SEG] = dq[rows, :SEG]
        d_out[rows, SEG : 2 * SEG] = jnp.where(
            low, dq[rows, SEG:].astype(F32), pltpu.roll(dk, HD, 1)
        ).astype(B16)
        d_out[rows, 2 * SEG :] = jnp.where(low, jnp.zeros_like(total), total).astype(B16)
    for k, out in enumerate((da_own, da_oth)):
        d = d_out[k * 256 : (k + 1) * 256, :]
        for n, w in enumerate((wa, wb, ra, rb)):
            out[:, n * 384 : (n + 1) * 384] = nt(d, w[...]).astype(B16)


def lift_kernel(info, g_own, g_oth, d_own, d_ra, d_rb, out):
    s = info[0]
    hi = jnp.concatenate([d_ra[0], d_rb[0]], axis=0)
    for k, g in enumerate((g_own, g_oth)):
        out[0, k * 256 : (k + 1) * 256] = nt(g[:, half_of(s)], d_own[0]) + nt(
            g[:, half_of(1 - s)], hi
        )


def expert_kernel(
    b_own, b_oth, w, gd, g_own, g_oth, u_own, u_oth, db_own, db_oth, hw_out, dgu_out, acc
):
    e = pl.program_id(0)
    lo = jnp.concatenate([g_own[0], u_own[0]], axis=1)
    hi = jnp.concatenate([g_oth[0], u_oth[0]], axis=1)

    @pl.when(e == 0)
    def _():
        acc[...] = jnp.zeros_like(acc)

    for k, b in enumerate((b_own, b_oth)):
        rows = slice(k * 256, (k + 1) * 256)
        gu = nn(b[:, :HALF], lo) + nn(b[:, HALF:], hi)
        gate, up = gu[:, :FC], gu[:, FC:]
        sg = jax.nn.sigmoid(gate)
        silu = gate * sg
        weight = w[0, rows]
        hw_out[0, rows] = (silu * up * weight).astype(B16)
        dh = gd[0, rows] * weight
        dgate = (dh * up * sg * (1.0 + gate * (1.0 - sg))).astype(B16)
        dup = (dh * silu).astype(B16)
        d = jnp.concatenate([dgate, dup], axis=1)
        dgu_out[0, rows] = d
        acc[rows, :HALF] += nt(d, lo)
        acc[rows, HALF:] += nt(d, hi)

    @pl.when(e == OWN - 1)
    def _():
        db_own[...] = acc[:256].astype(B16)
        db_oth[...] = acc[256:].astype(B16)


def expert_grad_kernel(info, b_own, b_oth, g_own, g_oth, hw, dgu, out_a, out_b):
    s = info[0]
    for half in range(2):
        k = slice(half * HALF, (half + 1) * HALF)
        sh = (s + half) & 1
        dw = (tn(b_own[:, k], dgu[0, :256]) + tn(b_oth[:, k], dgu[0, 256:])).astype(B16)
        dd = (
            tn(hw[0, :256], g_own[:, half_of(sh)]) + tn(hw[0, 256:], g_oth[:, half_of(sh)])
        ).astype(B16)
        for d in range(8):
            xh, z = d // 4, d % 4
            for kind in range(3):
                if kind < 2:
                    piece = dw[d * 96 : (d + 1) * 96, kind * FC : (kind + 1) * FC]
                else:
                    piece = jnp.concatenate(
                        [dd[d * 16 : (d + 1) * 16, l * FC : (l + 1) * FC] for l in range(6)], axis=0
                    )
                out_a[sh * 2 + xh, z, kind, 0] = piece[:48]
                out_b[z, sh * 2 + xh, kind, 0] = piece[48:]


def expert_out_kernel(hw, d_own, d_ra, d_rb, out_own, out_oth, acc):
    e = pl.program_id(0)
    hi = jnp.concatenate([d_ra[0], d_rb[0]], axis=0)

    @pl.when(e == 0)
    def _():
        acc[...] = jnp.zeros_like(acc)

    acc[:, :HALF] += nn(hw[0], d_own[0])
    acc[:, HALF:] += nn(hw[0], hi)

    @pl.when(e == OWN - 1)
    def _():
        out_own[...] = acc[:256].astype(B16)
        out_oth[...] = acc[256:].astype(B16)


def smem():
    return pl.BlockSpec(memory_space=SMEM)


def whole():
    return pl.BlockSpec(memory_space=VMEM)


def each(*shape):
    return pl.BlockSpec((1, *shape), lambda e: (e,) + (0,) * len(shape))


def fixed(*shape):
    return pl.BlockSpec(shape, lambda e: (0,) * len(shape))


def shape_of(shape, dtype):
    return jax.ShapeDtypeStruct(shape, dtype)


def run(kernel, name, ins, in_specs, outs, out_specs, flops, scratch=(), grid=None, mib=48):
    moved = sum(int(np.prod(v.shape)) * v.dtype.itemsize for v in (*ins, *outs))
    extra = {} if grid is None else {"grid": grid}
    return pl.pallas_call(
        kernel,
        name=name,
        in_specs=in_specs,
        out_specs=out_specs,
        out_shape=outs,
        scratch_shapes=list(scratch),
        cost_estimate=pl.CostEstimate(flops=int(flops), bytes_accessed=moved, transcendentals=0),
        compiler_params=pltpu.CompilerParams(vmem_limit_bytes=mib * 2**20),
        **extra,
    )(*ins)


def angle_tables():
    freq = 10000.0 ** (-np.arange(0, HD, 2) / HD)
    freq = np.tile(freq, 4)[None, :]
    coarse = np.arange(32)[:, None] * SEG * freq
    fine = np.arange(SEG)[:, None] * freq
    return tuple(
        jnp.asarray(v.astype(np.float32))
        for v in (np.cos(coarse), np.sin(coarse), np.cos(fine), np.sin(fine))
    )


def per_device(
    x,
    gain_attn,
    w_query,
    w_key,
    w_value,
    w_out,
    gain_moe,
    expert_gate,
    expert_up,
    expert_down,
    routes,
    route_gates,
    layout,
    g,
):
    s = lax.axis_index("shard")
    c = lax.axis_index("core")
    info = jnp.stack(
        [s, c, lax.axis_index("z"), lax.axis_index("xh"), lax.axis_index("tensor")]
    ).astype(jnp.int32)
    first = c == 0
    tables = angle_tables()

    def mine(v, axis):
        width = v.shape[axis] // 2
        return jnp.where(
            first,
            lax.slice_in_dim(v, 0, width, axis=axis),
            lax.slice_in_dim(v, width, 2 * width, axis=axis),
        )

    def both_cores(own, oth, axis):
        return jnp.where(
            first, jnp.concatenate([own, oth], axis), jnp.concatenate([oth, own], axis)
        )

    def natural(v):
        return jnp.where(s == 0, v, jnp.concatenate([v[:, HALF:], v[:, :HALF]], axis=1))

    packed = jnp.concatenate(
        [mine(w_query, 1), mine(w_key, 1), jnp.zeros((HALF, HD), B16), mine(w_value, 1)], axis=1
    )
    wa, wb = packed[:384], packed[384:]
    ra, rb = to_x(wa, 1), to_x(wb, -1)
    gains = jnp.stack([gain_attn, gain_moe])
    gains_t = to_x(gains, 1)
    g1o, g1t, g2o, g2t = gains[0:1], gains_t[0:1], gains[1:2], gains_t[1:2]
    x_t = other_core(x)
    a, q, kv = run(
        qkv_kernel,
        "qkv",
        (info, layout, x, x_t, g1o, g1t, wa, wb, ra, rb, *tables),
        [smem(), smem()] + [whole()] * 12,
        (shape_of((512, D), B16), shape_of((3, 512, 128), B16), shape_of((512, 128), B16)),
        [whole()] * 3,
        2 * 512 * D * 384,
    )
    slots = [kv] + [
        lax.ppermute(kv, ("z", "xh"), context_pairs(o // 2, o % 2)) for o in range(1, 8)
    ]
    wo = mine(w_out, 0)
    wo_t = jnp.concatenate([to_x(wo[:96], 1), to_x(wo[96:], -1)], axis=0)
    wo_own = lax.all_gather(jnp.concatenate([wo, wo_t], axis=1), "tensor")
    wo_oth = other_core(wo_own)
    o, lse = run(
        attend_kernel,
        "attend",
        (info, layout, q, *slots),
        [smem(), smem()] + [whole()] * 9,
        (shape_of((512, 256), B16), shape_of((4, 1, ROWS), F32)),
        [whole()] * 2,
        4 * 512 * 3 * 4096 * 128,
        scratch=[VMEM((4096, 128), B16), VMEM((128, 4096), B16)],
    )
    g_t = other_core(g)
    gate_c, up_c, down_c, _ = lax.optimization_barrier(
        (
            lax.dynamic_slice_in_dim(expert_gate, c * OWN, OWN, 0),
            lax.dynamic_slice_in_dim(expert_up, c * OWN, OWN, 0),
            lax.dynamic_slice_in_dim(expert_down, c * OWN, OWN, 0),
            kv,
        )
    )
    gate_t, up_t = to_x(gate_c, 1), to_x(up_c, -1)
    down_ra, down_rb = to_x(down_c[:, :64], 1), to_x(down_c[:, 64:], -1)
    ids = jnp.arange(EXPERTS, dtype=jnp.int32)
    share = jnp.sum(
        jnp.where(routes[:, :, None] == ids[None, None, :], route_gates[:, :, None], 0.0), axis=1
    )
    share = jnp.concatenate([share, other_core(share)], axis=0)
    share = jnp.where(first, share[:, :OWN], share[:, OWN:]).T[:, :, None]
    lifted = run(
        lift_kernel,
        "lift",
        (info, g, g_t, down_c, down_ra, down_rb),
        [smem(), fixed(256, D), fixed(256, D), each(FC, HALF), each(64, HALF), each(64, HALF)],
        (shape_of((OWN, 512, FC), F32),),
        [each(512, FC)],
        2 * 512 * D * 640,
        grid=(OWN,),
    )[0]

    o_all = jnp.concatenate([o[:256], other_core(o[256:])], axis=1)
    o_tok = over_y(o_all.reshape(4, 64, 512))
    h, b64 = run(
        token_kernel,
        "token",
        (info, x, o_tok, wo_own, wo_oth, g2o, g2t),
        [smem()] + [whole()] * 6,
        (shape_of((64, D), F32), shape_of((64, D), B16)),
        [whole()] * 2,
        2 * 64 * D * D,
    )
    b_own = over_y(jnp.broadcast_to(b64[None], (4, 64, D))).reshape(256, D)
    b_oth = other_core(b_own)
    db_own, db_oth, hw, dgu = run(
        expert_kernel,
        "expert",
        (b_own, b_oth, share, lifted, gate_c, gate_t, up_c, up_t),
        [fixed(256, D), fixed(256, D), each(512, 1), each(512, FC)] + [each(HALF, FC)] * 4,
        (
            shape_of((256, D), B16),
            shape_of((256, D), B16),
            shape_of((OWN, 512, FC), B16),
            shape_of((OWN, 512, 2 * FC), B16),
        ),
        [fixed(256, D), fixed(256, D), each(512, FC), each(512, 2 * FC)],
        4 * 2 * 512 * D * 640,
        scratch=[VMEM((512, D), F32)],
        grid=(OWN,),
    )
    db = db_own + other_core(db_oth)
    db = over_y(db.reshape(4, 64, D))
    dh, dattn, do_tok, gsum_moe = run(
        token_back_kernel,
        "token_back",
        (info, h, db, g, wo_own, wo_oth, g2o, g2t),
        [smem()] + [whole()] * 7,
        (
            shape_of((64, D), F32),
            shape_of((64, D), B16),
            shape_of((4, 64, 512), B16),
            shape_of((1, D), F32),
        ),
        [whole()] * 4,
        2 * 64 * D * D,
    )
    ea, eb = run(
        expert_grad_kernel,
        "expert_grad",
        (info, b_own, b_oth, g, g_t, hw, dgu),
        [smem()] + [fixed(256, D)] * 4 + [each(512, FC), each(512, 2 * FC)],
        (shape_of((4, 4, 3, OWN, 48, FC), B16), shape_of((4, 4, 3, OWN, 48, FC), B16)),
        [pl.BlockSpec((4, 4, 3, 1, 48, FC), lambda e: (0, 0, 0, e, 0, 0))] * 2,
        3 * 2 * 512 * D * 640,
        grid=(OWN,),
    )
    moe_own, moe_oth = run(
        expert_out_kernel,
        "expert_out",
        (hw, down_c, down_ra, down_rb),
        [each(512, FC), each(FC, HALF), each(64, HALF), each(64, HALF)],
        (shape_of((256, D), B16), shape_of((256, D), B16)),
        [fixed(256, D)] * 2,
        2 * 512 * D * 640,
        scratch=[VMEM((512, D), F32)],
        grid=(OWN,),
    )

    def summed(v):
        return jnp.sum(v.astype(F32), axis=0)

    ea = summed(lax.all_to_all(ea, X, 0, 0, tiled=True)).astype(B16)
    eb = summed(lax.all_to_all(eb, "z", 0, 0, tiled=True)).astype(B16)
    ea = summed(lax.all_to_all(ea, "z", 0, 0, tiled=True)).astype(B16)
    eb = summed(lax.all_to_all(eb, X, 0, 0, tiled=True)).astype(B16)
    e_own = lax.all_gather(jnp.stack([ea, eb]), ("xh", "z"))
    e_oth = other_core(e_own)

    do = over_y(do_tok).reshape(256, 512)
    do_oth = other_core(do[:, 256:])
    dq, dkv = run(
        attend_back_kernel,
        "attend_back",
        (info, layout, q, do[:, :256], do_oth, o, lse, *tables, *slots),
        [smem(), smem()] + [whole()] * 17,
        (shape_of((512, 256), B16), shape_of((8, 512, 128), B16)),
        [whole()] * 2,
        10 * 512 * 3 * 4096 * 128,
        scratch=[VMEM((4096, 128), B16), VMEM((128, 4096), B16), VMEM((4096, 128), F32)],
    )
    returned = jnp.stack(
        [
            lax.ppermute(dkv[n], ("z", "xh"), context_pairs(-(n // 2), n % 2))
            for n in range(1, 8)
        ]
    )
    dqkv, da_own, da_oth = run(
        qkv_back_kernel,
        "qkv_back",
        (info, layout, dq, dkv[0], returned, wa, wb, ra, rb, *tables),
        [smem(), smem()] + [whole()] * 11,
        (shape_of((512, 384), B16), shape_of((256, D), B16), shape_of((256, D), B16)),
        [whole()] * 3,
        2 * 512 * D * 384,
    )
    da = over_y((da_own + other_core(da_oth)).reshape(4, 64, D))
    ig, gsum_attn = run(
        input_back_kernel,
        "input_back",
        (info, dh, da, x, g1o, g1t),
        [smem()] + [whole()] * 5,
        (shape_of((64, D), B16), shape_of((1, D), F32)),
        [whole()] * 2,
        64 * D * 20,
    )
    input_grad = over_y(jnp.broadcast_to(ig[None], (4, 64, D))).reshape(256, D)
    input_grad = natural(input_grad).astype(F32)

    moe = over_y((moe_own + other_core(moe_oth)).reshape(4, 64, D))
    out64 = (h + summed(moe)).astype(B16)
    output = natural(over_y(jnp.broadcast_to(out64[None], (4, 64, D))).reshape(256, D))

    d_qkv = tn(a, dqkv).astype(B16).reshape(2, HALF, 384)
    d_qkv = jnp.where(s == 0, d_qkv, d_qkv[::-1]).reshape(16, 96, 384)
    d_qkv = summed(lax.all_to_all(d_qkv, PLANE, 0, 0, tiled=True)).astype(B16)
    d_qkv = lax.all_gather(d_qkv, ("xh", "z")).reshape(HALF, 384)
    d_qkv_t = other_core(d_qkv)
    dattn = over_y(jnp.broadcast_to(dattn[None], (4, 64, D))).reshape(256, D)
    dattn = jnp.concatenate([dattn, other_core(dattn)], axis=0)
    d_out = tn(o, dattn)[:192].astype(B16)
    d_out = jnp.stack([d_out[:, :HALF], d_out[:, HALF:]])
    d_out = jnp.where(s == 0, d_out, d_out[::-1]).reshape(16, 24, HALF)
    d_out = summed(lax.all_to_all(d_out, PLANE, 0, 0, tiled=True)).astype(B16)
    d_out = lax.all_gather(d_out, ("xh", "z")).reshape(192, HALF)
    d_out = both_cores(d_out, other_core(d_out), 0).astype(F32)
    wq_grad = both_cores(d_qkv[:, :192], d_qkv_t[:, :192], 1).astype(F32)
    wk_grad = both_cores(d_qkv[:, 192:256], d_qkv_t[:, 192:256], 1).astype(F32)
    wv_grad = both_cores(d_qkv[:, 320:], d_qkv_t[:, 320:], 1).astype(F32)

    def weight(v, kind):
        part = v[:, :, kind]
        if kind < 2:
            return part.transpose(2, 0, 1, 3, 4).reshape(OWN, HALF, FC)
        part = part.reshape(8, 2, OWN, 3, 16, FC).transpose(2, 0, 4, 1, 3, 5)
        return part.reshape(OWN, FC, HALF)

    expert_grads = [
        both_cores(weight(e_own, kind), weight(e_oth, kind), 0).astype(F32) for kind in range(3)
    ]
    gsum = natural(jnp.concatenate([gsum_attn, gsum_moe], axis=0))
    gsum = lax.psum(gsum, ("shard", "z", "xh", "core", "tensor"))
    gsum = lax.dynamic_slice_in_dim(gsum, s * HALF, HALF, 1)
    return (
        output,
        input_grad,
        gsum[0],
        wq_grad,
        wk_grad,
        wv_grad,
        d_out,
        gsum[1],
        expert_grads[0],
        expert_grads[1],
        expert_grads[2],
    )


def solution(mesh):
    fine = Mesh(
        mesh.devices.reshape(2, 4, 2, 2, 4), ("shard", "z", "xh", "core", "tensor")
    )
    rows = P(("shard", "z", "xh", "core"), None)
    placed = (
        rows,
        P("shard"),
        P("shard", "tensor"),
        P("shard", "tensor"),
        P("shard", "tensor"),
        P("tensor", "shard"),
        P("shard"),
        P(None, "shard", "tensor"),
        P(None, "shard", "tensor"),
        P(None, "tensor", "shard"),
        rows,
        rows,
        P(),
        rows,
    )
    return jax.shard_map(
        per_device,
        mesh=fine,
        in_specs=placed,
        out_specs=(
            rows,
            rows,
            P("shard"),
            P("shard", "tensor"),
            P("shard", "tensor"),
            P("shard", "tensor"),
            P("tensor", "shard"),
            P("shard"),
            P(None, "shard", "tensor"),
            P(None, "shard", "tensor"),
            P(None, "tensor", "shard"),
        ),
        check_vma=False,
    )
```

```python
import functools

import jax
import jax.numpy as jnp
import numpy as np
from jax import lax
from jax.experimental import pallas as pl
from jax.experimental.pallas import tpu as pltpu
from jax.sharding import Mesh
from jax.sharding import PartitionSpec as P

D = 1536
HALF = 768
HD = 64
EXPERTS = 10
OWN = 5
FC = 128
EPS = 1e-05
SCALE = 0.125
CHUNK = 512
SEG = 128
ROWS = 3 * SEG
NEG = -1e30
B16 = jnp.bfloat16
F32 = jnp.float32
X = ("shard", "xh")
PLANE = ("shard", "xh", "z")
VMEM = pltpu.VMEM
SMEM = pltpu.SMEM


def nn(a, b):
    return lax.dot_general(a, b, (((1,), (0,)), ((), ())), preferred_element_type=F32)


def nt(a, b):
    return lax.dot_general(a, b, (((1,), (1,)), ((), ())), preferred_element_type=F32)


def tn(a, b):
    return lax.dot_general(a, b, (((0,), (0,)), ((), ())), preferred_element_type=F32)


def x_pairs(k):
    pairs = []
    for sh in range(2):
        for xh in range(2):
            at = (2 * xh + sh + k) % 4
            pairs.append((sh * 2 + xh, (at % 2) * 2 + at // 2))
    return pairs


def to_x(v, k):
    return lax.ppermute(v, X, x_pairs(k))


def other_core(v):
    return lax.ppermute(v, "core", [(0, 1), (1, 0)])


def to_y(v, k):
    return lax.ppermute(v, "tensor", [(i, (i + k) % 4) for i in range(4)])


def to_z(v, k):
    return lax.ppermute(v, "z", [(i, (i + k) % 4) for i in range(4)])


def over_y(v):
    return lax.all_to_all(v, "tensor", 0, 0, tiled=True)


def from_each_y(v):
    return [to_y(v, 4 - k) for k in range(1, 4)]


def after(v, *others):
    return lax.optimization_barrier((v, *others))[0]


def half_of(s):
    return pl.ds(pl.multiple_of(s * HALF, HALF), HALF)


def piece_of(info, k):
    return pl.ds(pl.multiple_of(((info[4] + k) & 3) * 64, 64), 64)


def seg_at(info, layout, slot, blk, j):
    cc = info[1] if blk == 0 else 1 - info[1]
    return layout[(slot * 2 + cc) * 2 + j]


def seg_of(info, layout, blk, j):
    return seg_at(info, layout, info[2] * 2 + info[3], blk, j)


def angle_rows(at, ca, sa, cb, sb):
    ca, sa = ca[pl.ds(at, 1), :], sa[pl.ds(at, 1), :]
    return ca * cb[...] - sa * sb[...], sa * cb[...] + ca * sb[...]


def low_lanes(shape):
    return lax.broadcasted_iota(jnp.int32, shape, 1) < HD


def first_half_of_head(shape):
    return (lax.broadcasted_iota(jnp.int32, shape, 1) & (HD - 1)) < HD // 2


def rope(u, cos, sin):
    turned = jnp.where(
        first_half_of_head(u.shape), -pltpu.roll(u, 96, 1), pltpu.roll(u, 32, 1)
    )
    return u * cos + turned * sin


def unrope(u, cos, sin):
    w = u * sin
    turned = jnp.where(
        first_half_of_head(u.shape), pltpu.roll(w, 96, 1), -pltpu.roll(w, 32, 1)
    )
    return u * cos + turned


def qkv_kernel(
    info, layout, xo, xt, gain_o, gain_t, wa, wb, ra, rb, ca, sa, cb, sb, a_out, q_out, kv_out
):
    s = info[0]
    for blk, ref in enumerate((xo, xt)):
        lo = ref[:, half_of(s)].astype(F32)
        hi = ref[:, half_of(1 - s)].astype(F32)
        mean = (
            jnp.sum(lo * lo, axis=1, keepdims=True) + jnp.sum(hi * hi, axis=1, keepdims=True)
        ) / D
        inv = lax.rsqrt(mean + EPS)
        alo = (lo * inv * gain_o[...].astype(F32)).astype(B16)
        ahi = (hi * inv * gain_t[...].astype(F32)).astype(B16)
        a_out[blk * 256 : blk * 256 + 256, :HALF] = alo
        a_out[blk * 256 : blk * 256 + 256, HALF:] = ahi
        t = (
            nn(alo[:, :384], wa[...])
            + nn(alo[:, 384:], wb[...])
            + nn(ahi[:, :384], ra[...])
            + nn(ahi[:, 384:], rb[...])
        )
        for j in range(2):
            cos, sin = angle_rows(seg_of(info, layout, blk, j), ca, sa, cb, sb)
            tt = t[j * SEG : (j + 1) * SEG]
            low = low_lanes((SEG, SEG))
            t0 = rope(tt[:, :128], cos, sin)
            t1 = rope(tt[:, 128:256], cos, sin)
            t2 = tt[:, 256:]
            rows = slice(blk * 256 + j * SEG, blk * 256 + (j + 1) * SEG)
            zero = jnp.zeros_like(t0)

            def scaled(v):
                return (v.astype(B16).astype(F32) * SCALE).astype(B16)

            q_out[0, rows] = scaled(jnp.where(low, t0, zero))
            q_out[1, rows] = scaled(jnp.where(low, pltpu.roll(t0, HD, 1), zero))
            q_out[2, rows] = scaled(jnp.where(low, t1, zero))
            kv = jnp.where(low, pltpu.roll(t1, HD, 1), t2).astype(B16)
            for slot in range(8):
                kv_out[slot, rows] = kv


def fill_sorted(info, layout, slots, ks, kst):
    for slot in range(8):
        for blk in range(2):
            for j in range(2):
                at = pl.multiple_of(seg_at(info, layout, slot, blk, j) * SEG, SEG)
                part = slots[slot, blk * 256 + j * SEG : blk * 256 + (j + 1) * SEG, :]
                ks[pl.ds(at, SEG), :] = part
                kst[:, pl.ds(at, SEG)] = part.astype(F32).T.astype(B16)


def allowed_keys(j, pos):
    key = j * CHUNK + lax.broadcasted_iota(jnp.int32, (CHUNK, ROWS), 0)
    query = pos * SEG + (lax.broadcasted_iota(jnp.int32, (CHUNK, ROWS), 1) & (SEG - 1))
    return key <= query


def heads_of(q, i):
    return jnp.concatenate([q[h, i * SEG : (i + 1) * SEG, :] for h in range(3)], axis=0)


def attend_kernel(info, layout, q, slots, o_out, o_send, lse_out, ks, kst):
    fill_sorted(info, layout, slots, ks, kst)
    low = low_lanes((SEG, SEG))
    for i in range(4):
        pos = seg_of(info, layout, i // 2, i % 2)
        qi = heads_of(q, i)
        full = lax.div(pos, CHUNK // SEG)

        def step(j, carry, edge=False):
            top, total, acc = carry
            at = pl.multiple_of(j * CHUNK, CHUNK)
            sc = nt(ks[pl.ds(at, CHUNK), :], qi)
            if edge:
                sc = jnp.where(allowed_keys(j, pos), sc, NEG)
            new = jnp.maximum(top, jnp.max(sc, axis=0, keepdims=True))
            e = jnp.exp(sc - new)
            back = jnp.exp(top - new)
            total = total * back + jnp.sum(e, axis=0, keepdims=True)
            acc = acc * back + nn(kst[:, pl.ds(at, CHUNK)], e.astype(B16))
            return new, total, acc

        start = (
            jnp.full((1, ROWS), NEG, F32),
            jnp.zeros((1, ROWS), F32),
            jnp.zeros((SEG, ROWS), F32),
        )
        top, total, acc = step(full, lax.fori_loop(0, full, step, start), edge=True)
        lse_out[i] = top + jnp.log(total)
        o = (acc / total).T
        o0, o1, o2 = o[:SEG], o[SEG : 2 * SEG], o[2 * SEG :]
        left = jnp.where(low, pltpu.roll(o0, HD, 1), o1).astype(B16)
        right = jnp.where(low, pltpu.roll(o2, HD, 1), jnp.zeros_like(o2)).astype(B16)
        for out, at in ((o_out, i * SEG),) + (((o_send, (i - 2) * SEG),) if i >= 2 else ()):
            out[at : at + SEG, :SEG] = left
            out[at : at + SEG, SEG:] = right


def attend_back_kernel(
    info, layout, q, do_own, do_oth, o, lse, ca, sa, cb, sb, slots, dq_out, dkv_out, ks, kst, dkv
):
    fill_sorted(info, layout, slots, ks, kst)
    dkv[...] = jnp.zeros_like(dkv)
    low = low_lanes((SEG, SEG))

    def spread(t0, t1):
        zero = jnp.zeros((SEG, SEG), F32)
        return jnp.concatenate(
            [
                jnp.where(low, zero, pltpu.roll(t0, HD, 1)),
                jnp.where(low, zero, t0),
                jnp.where(low, zero, pltpu.roll(t1, HD, 1)),
            ],
            axis=0,
        )

    for i in range(4):
        pos = seg_of(info, layout, i // 2, i % 2)
        qi = heads_of(q, i)
        rows = slice(i * SEG, (i + 1) * SEG)
        here = slice((i % 2) * SEG, (i % 2 + 1) * SEG)
        do, at = (do_own, 0) if i < 2 else (do_oth, 256)
        dof = spread(
            do[here, at : at + SEG].astype(F32), do[here, at + SEG : at + 2 * SEG].astype(F32)
        )
        of = spread(o[rows, :SEG].astype(F32), o[rows, SEG:].astype(F32))
        delta = jnp.sum((dof * of).T, axis=0, keepdims=True)
        doi = dof.astype(B16)
        lse_i = lse[i]
        full = lax.div(pos, CHUNK // SEG)

        def step(j, acc, edge=False):
            at = pl.multiple_of(j * CHUNK, CHUNK)
            kv = ks[pl.ds(at, CHUNK), :]
            p = jnp.exp(nt(kv, qi) - lse_i)
            if edge:
                p = jnp.where(allowed_keys(j, pos), p, 0.0)
            ds = (p * (nt(kv, doi) - delta)).astype(B16)
            dkv[pl.ds(at, CHUNK), :] += nn(ds, qi) + nn(p.astype(B16), doi)
            return acc + nn(kst[:, pl.ds(at, CHUNK)], ds)

        acc = step(full, lax.fori_loop(0, full, step, jnp.zeros((SEG, ROWS), F32)), edge=True)
        dq = acc.T * SCALE
        cos, sin = angle_rows(pos, ca, sa, cb, sb)
        d0, d1, d2 = [unrope(dq[h * SEG : (h + 1) * SEG], cos, sin) for h in range(3)]
        dq_out[rows, :SEG] = jnp.where(low, d0, pltpu.roll(d1, HD, 1)).astype(B16)
        dq_out[rows, SEG:] = jnp.where(low, d2, jnp.zeros_like(d2)).astype(B16)
    for slot in range(8):
        for blk in range(2):
            for j in range(2):
                at = pl.multiple_of(seg_at(info, layout, slot, blk, j) * SEG, SEG)
                dkv_out[slot, blk * 256 + j * SEG : blk * 256 + (j + 1) * SEG, :] = dkv[
                    pl.ds(at, SEG), :
                ].astype(B16)


def token_kernel(info, x, o, w_own, w_oth, gain_o, gain_t, h_out, b_out):
    s = info[0]
    here = piece_of(info, 0)
    alo = jnp.zeros((64, HALF), F32)
    ahi = jnp.zeros((64, HALF), F32)
    for y in range(4):
        for part, w in ((o[y, :, :192], w_own), (o[y, :, 256:448], w_oth)):
            alo += nn(part, w[y, 0])
            ahi += nn(part, w[y, 1])
    lo = x[here, half_of(s)].astype(F32) + alo
    hi = x[here, half_of(1 - s)].astype(F32) + ahi
    mean = (
        jnp.sum(lo * lo, axis=1, keepdims=True) + jnp.sum(hi * hi, axis=1, keepdims=True)
    ) / D
    inv = lax.rsqrt(mean + EPS)
    h_out[:, :HALF] = lo
    h_out[:, HALF:] = hi
    blo = (lo * inv * gain_o[...].astype(F32)).astype(B16)
    bhi = (hi * inv * gain_t[...].astype(F32)).astype(B16)
    b_out[:, :HALF] = blo
    b_out[:, HALF:] = bhi


def norm_back(grads, sources, gains):
    mean = sum(jnp.sum(v * v, axis=1, keepdims=True) for v in sources) / D
    inv = lax.rsqrt(mean + EPS)
    weighted = [d * g for d, g in zip(grads, gains)]
    dot = sum(jnp.sum(w * v, axis=1, keepdims=True) for w, v in zip(weighted, sources)) / D
    cube = inv * inv * inv * dot
    return (
        [inv * w - v * cube for w, v in zip(weighted, sources)],
        [jnp.sum(d * v * inv, axis=0, keepdims=True) for d, v in zip(grads, sources)],
    )


def fold_kernel(info, own, received, out0, out1, out2, out3):
    for n in range(own.shape[0] // 256):
        for k, out in enumerate((out0, out1, out2, out3)):
            rows = pl.ds(pl.multiple_of(n * 256 + ((info[4] + k) & 3) * 64, 64), 64)
            total = own[rows].astype(F32) + received[rows].astype(F32)
            out[n * 64 : (n + 1) * 64] = total.astype(out.dtype)


def token_back_kernel(
    info, h, d0, d1, d2, d3, g, w_own, w_oth, gain_o, gain_t, dh_out, dattn_out, do_out, gain_out,
    y_out,
):
    s = info[0]
    here = piece_of(info, 0)
    total = sum(d[:64].astype(F32) for d in (d0, d1, d2, d3))
    y_out[...] = (h[...] + sum(d[64:].astype(F32) for d in (d0, d1, d2, d3))).astype(B16)
    halves = (slice(0, HALF), slice(HALF, D))
    back, gsum = norm_back(
        [total[:, k] for k in halves],
        [h[:, k] for k in halves],
        [gain_o[...].astype(F32), gain_t[...].astype(F32)],
    )
    for k, part, sums, half in zip(halves, back, gsum, (s, 1 - s)):
        dh = g[here, half_of(half)].astype(F32) + part
        dh_out[:, k] = dh
        for y in range(4):
            dattn_out[y, :, k] = dh.astype(B16)
        gain_out[:, k] = sums
    dattn = dattn_out[0]
    pad = jnp.zeros((64, 64), B16)
    for y in range(4):
        for at, w in ((0, w_own), (256, w_oth)):
            do = nt(dattn[:, :HALF], w[y, 0]) + nt(dattn[:, HALF:], w[y, 1])
            do_out[y, :, at : at + 192] = do.astype(B16)
            do_out[y, :, at + 192 : at + 256] = pad


def input_back_kernel(info, dh, d0, d1, d2, d3, x, gain_o, gain_t, y64, out):
    s = info[0]
    here = piece_of(info, 0)
    total = sum(d[...].astype(F32) for d in (d0, d1, d2, d3))
    halves = (slice(0, HALF), slice(HALF, D))
    back, _ = norm_back(
        [total[:, k] for k in halves],
        [x[here, half_of(half)].astype(F32) for half in (s, 1 - s)],
        [gain_o[...].astype(F32), gain_t[...].astype(F32)],
    )
    for k, part in zip(halves, back):
        out[:64, k] = (dh[:, k] + part).astype(B16)
    out[64:] = y64[...]


def place_kernel(info, p0, p1, p2, p3, grad, y):
    s = info[0]
    for k, p in enumerate((p0, p1, p2, p3)):
        for n, out in enumerate((grad, y)):
            rows = slice(n * 64, (n + 1) * 64)
            out[piece_of(info, k), half_of(s)] = p[rows, :HALF].astype(out.dtype)
            out[piece_of(info, k), half_of(1 - s)] = p[rows, HALF:].astype(out.dtype)


def qkv_back_kernel(
    info, layout, dq, dkv, wa, wb, ra, rb, ca, sa, cb, sb, d_out, da_own, da_oth
):
    for i in range(4):
        rows = slice(i * SEG, (i + 1) * SEG)
        total = sum(dkv[r, rows].astype(F32) for r in range(8))
        cos, sin = angle_rows(seg_of(info, layout, i // 2, i % 2), ca, sa, cb, sb)
        low = low_lanes((SEG, SEG))
        dk = unrope(total, cos, sin)
        d_out[rows, :SEG] = dq[rows, :SEG]
        d_out[rows, SEG : 2 * SEG] = jnp.where(
            low, dq[rows, SEG:].astype(F32), pltpu.roll(dk, HD, 1)
        ).astype(B16)
        d_out[rows, 2 * SEG :] = jnp.where(low, jnp.zeros_like(total), total).astype(B16)
    for n, out in enumerate((da_own, da_oth)):
        d = d_out[n * 256 : (n + 1) * 256, :]
        for m, w in enumerate((wa, wb, ra, rb)):
            out[:, m * 384 : (m + 1) * 384] = nt(d, w[...]).astype(B16)


def attend_grad_kernel(
    info, a, dqkv, dattn_own, dattn_oth, o, gsum_moe, wa, wb, ra, rb, out
):
    s = info[0]
    d = dqkv[...]
    for m, w in enumerate((wa, wb, ra, rb)):
        k = slice(m * 384, (m + 1) * 384)
        dw = tn(a[:, k], d)
        along = dw * w[...].astype(F32)
        along = along[:, :SEG] + along[:, SEG : 2 * SEG] + along[:, 2 * SEG :]
        gain = jnp.sum(along.T, axis=0, keepdims=True)
        moe = gsum_moe[:, k]
        dwo = tn(dattn_own[:, k], o[:256]) + tn(dattn_oth[:, k], o[256:])
        low = low_lanes((384, SEG))
        last = jnp.where(low, dwo[:, SEG:], dw[:, 2 * SEG :])
        sh = (s + m // 2) & 1
        row = lax.broadcasted_iota(jnp.int32, (16, SEG), 0)
        for z in range(4):
            at = sh * 8 + (m % 2) * 4 + z
            part = slice(z * 96, (z + 1) * 96)
            out[at, :96, : 2 * SEG] = dw[part, : 2 * SEG].astype(B16)
            out[at, :96, 2 * SEG : 3 * SEG] = last[part].astype(B16)
            out[at, :96, 3 * SEG :] = dwo[part, :SEG].astype(B16)
            pad = jnp.zeros((1, 32), F32)
            g0 = jnp.concatenate([gain[:, part], pad], axis=1)
            g1 = jnp.concatenate([moe[:, part], pad], axis=1)
            both = jnp.where(row == 0, g0, jnp.where(row == 1, g1, 0.0))
            out[at, 96:, :SEG] = both.astype(B16)
            out[at, 96:, SEG:] = jnp.zeros((16, 3 * SEG), B16)


def lift_kernel(info, g_own, g_oth, d_own, d_ra, d_rb, out, g_out):
    s = info[0]
    hi = jnp.concatenate([d_ra[0], d_rb[0]], axis=0)

    @pl.when(pl.program_id(0) == 0)
    def _():
        for n, g in enumerate((g_own, g_oth)):
            rows = slice(n * 256, (n + 1) * 256)
            g_out[rows, :HALF] = g[:, half_of(s)]
            g_out[rows, HALF:] = g[:, half_of(1 - s)]

    out[0] = nt(g_out[:, :HALF], d_own[0]) + nt(g_out[:, HALF:], hi)


def expert_kernel(
    info, b0, b1, b2, b3, b4, b5, b6, b7, w, gd, g_own, g_oth, u_own, u_oth, d_own, d_ra, d_rb,
    out_own, out_oth, hw_out, dgu_out, b, acc, moe,
):
    e = pl.program_id(0)
    lo = jnp.concatenate([g_own[0], u_own[0]], axis=1)
    hi = jnp.concatenate([g_oth[0], u_oth[0]], axis=1)
    down = jnp.concatenate([d_ra[0], d_rb[0]], axis=0)

    @pl.when(e == 0)
    def _():
        acc[...] = jnp.zeros_like(acc)
        moe[...] = jnp.zeros_like(moe)
        for n, ref in enumerate((b0, b1, b2, b3, b4, b5, b6, b7)):
            at = (n // 4) * 256 + ((info[4] + n) & 3) * 64
            b[pl.ds(pl.multiple_of(at, 64), 64)] = ref[...]

    for k in range(2):
        rows = slice(k * 256, (k + 1) * 256)
        gu = nn(b[rows, :HALF], lo) + nn(b[rows, HALF:], hi)
        gate, up = gu[:, :FC], gu[:, FC:]
        sg = jax.nn.sigmoid(gate)
        silu = gate * sg
        here = lax.broadcasted_iota(jnp.int32, (256, OWN), 1) == e
        weight = jnp.sum(jnp.where(here, w[rows], 0.0), axis=1, keepdims=True)
        hw = (silu * up * weight).astype(B16)
        hw_out[0, rows] = hw
        moe[rows, :HALF] += nn(hw, d_own[0])
        moe[rows, HALF:] += nn(hw, down)
        dh = gd[0, rows] * weight
        dgate = (dh * up * sg * (1.0 + gate * (1.0 - sg))).astype(B16)
        dup = (dh * silu).astype(B16)
        d = jnp.concatenate([dgate, dup], axis=1)
        dgu_out[0, rows] = d
        acc[rows, :HALF] += nt(d, lo)
        acc[rows, HALF:] += nt(d, hi)

    @pl.when(e == OWN - 1)
    def _():
        for n, out in enumerate((out_own, out_oth)):
            out[:256] = acc[n * 256 : (n + 1) * 256].astype(B16)
            out[256:] = moe[n * 256 : (n + 1) * 256].astype(B16)


def expert_grad_kernel(info, b, g, hw, dgu, *refs):
    by_x, by_z, dws, dds = refs[:5], refs[5:10], refs[10], refs[11]
    at_x = 2 * info[3] + info[0]

    def put(refs, step, k, kind, value):
        if step == 2:
            refs[2 + k // 2][k % 2, kind, 0] = value
        else:
            refs[{0: 0, 1: 1, 3: 4}[step]][k, kind, 0] = value

    for half in range(2):
        k = slice(half * HALF, (half + 1) * HALF)
        dws[...] = tn(b[:, k], dgu[0]).astype(B16)
        dds[...] = tn(hw[0], g[:, k]).astype(B16)
        for step in (half, half + 2):
            xq = ((at_x + step) & 3) >> 1
            for dz in range(4):
                at = xq * 4 + ((info[2] + dz) & 3)
                for kind in range(3):
                    if kind < 2:
                        piece = dws[
                            pl.ds(pl.multiple_of(at * 96, 32), 96), kind * FC : (kind + 1) * FC
                        ]
                    else:
                        part = dds[pl.ds(pl.multiple_of(at * 16, 16), 16), :]
                        piece = jnp.concatenate(
                            [part[:, l * FC : (l + 1) * FC] for l in range(6)], axis=0
                        )
                    put(by_x, step, dz, kind, piece[:48])
                    put(by_z, dz, step, kind, piece[48:])


def pass_on_kernel(*refs):
    for n in (0, 4):
        up, down, got_up, got_down = refs[n : n + 4]
        out_up, out_down = refs[8 + n // 2], refs[9 + n // 2]
        out_up[:2] = (up[:2].astype(F32) + got_up[...].astype(F32)).astype(B16)
        out_up[2:] = up[2:]
        out_down[:2] = down[:2]
        out_down[2:] = (down[2:].astype(F32) + got_down[...].astype(F32)).astype(B16)


def gather_sum_kernel(*refs):
    for n in (0, 3):
        outs = refs[6 + n // 3 * 4 : 10 + n // 3 * 4]
        for k, out in enumerate(outs):
            out[...] = sum(p[k].astype(F32) for p in refs[n : n + 3]).astype(out.dtype)


def sum_kernel(*refs):
    for n in range(2):
        refs[8 + n][...] = sum(p[...].astype(F32) for p in refs[n * 4 : n * 4 + 4]).astype(B16)


def stack_kernel(n, info, *refs):
    at = info[2] if n == 4 else info[3]
    for k, ref in enumerate(refs[:-1]):
        refs[-1][(at + k) & (n - 1)] = ref[...]


def assemble_kernel(info, *refs):
    gate, up, down = refs[10:]

    def write(everywhere, *by_z):
        def place(v, n, xh, z, part):
            at = xh * 4 + z
            rows = pl.ds(pl.multiple_of(at * 96 + part * 48, 16), 48)
            gate[0, rows] = v[n, 0, 0].astype(F32)
            up[0, rows] = v[n, 1, 0].astype(F32)
            rows = pl.ds(pl.multiple_of(at * 16, 16), 16)
            for l in range(3):
                down[0, rows, (part * 3 + l) * FC : (part * 3 + l + 1) * FC] = v[
                    n, 2, 0, l * 16 : (l + 1) * 16
                ].astype(F32)

        for n in range(8):
            place(everywhere, n, n // 4, n % 4, 0)
        for k, v in enumerate(by_z):
            for xh in range(2):
                place(v, xh, xh, (info[2] + k) & 3, 1)

    @pl.when(pl.program_id(0) == 0)
    def _():
        write(*refs[:5])

    @pl.when(pl.program_id(0) == 1)
    def _():
        write(*refs[5:10])


def finish_kernel(info, own, oth, wq, wk, wv, wo_out, wo):
    first = info[1] == 0
    low = low_lanes((96, SEG))
    for at in range(8):
        rows = slice(at * 96, (at + 1) * 96)
        a, b = own[at, :96].astype(F32), oth[at, :96].astype(F32)
        a, b = jnp.where(first, a, b), jnp.where(first, b, a)
        a = [a[:, n * SEG : (n + 1) * SEG] for n in range(4)]
        b = [b[:, n * SEG : (n + 1) * SEG] for n in range(4)]
        turned = [pltpu.roll(v, HD, 1) for v in b]
        wq[rows, :SEG] = a[0]
        wq[rows, SEG : 2 * SEG] = jnp.where(low, a[1], turned[0])
        wq[rows, 2 * SEG :] = jnp.where(low, turned[0], turned[1])
        wk[rows] = jnp.where(low, pltpu.roll(a[1], HD, 1), b[1])
        wv[rows] = jnp.where(low, pltpu.roll(a[2], HD, 1), b[2])
        wo[rows, :SEG] = a[3]
        wo[rows, SEG : 2 * SEG] = jnp.where(low, a[2], turned[3])
        wo[rows, 2 * SEG :] = jnp.where(low, turned[3], turned[2])
    wo_out[...] = wo[...].T


def smem():
    return pl.BlockSpec(memory_space=SMEM)


def whole():
    return None


def each(*shape):
    return pl.BlockSpec((1, *shape), lambda e: (e,) + (0,) * len(shape))


def fixed(*shape):
    return pl.BlockSpec(shape, lambda e: (0,) * len(shape))


def shape_of(shape, dtype):
    return jax.ShapeDtypeStruct(shape, dtype)


def cost(us):
    return pl.CostEstimate(flops=int(us * 3.3e9), bytes_accessed=int(us * 1e7), transcendentals=0)


def run(kernel, name, us, ins, in_specs, outs, out_specs, scratch=(), grid=(1,), mib=60):
    def block(spec, v):
        return fixed(*v.shape) if spec is None else spec

    return pl.pallas_call(
        kernel,
        name=name,
        grid=grid,
        in_specs=[block(spec, v) for spec, v in zip(in_specs, ins, strict=True)],
        out_specs=[block(spec, v) for spec, v in zip(out_specs, outs, strict=True)],
        out_shape=outs,
        scratch_shapes=list(scratch),
        cost_estimate=cost(us),
        compiler_params=pltpu.CompilerParams(vmem_limit_bytes=mib * 2**20),
    )(*ins)


def angle_tables():
    freq = 10000.0 ** (-np.arange(0, HD, 2) / HD)
    freq = np.tile(freq, 4)[None, :]
    coarse = np.arange(32)[:, None] * SEG * freq
    fine = np.arange(SEG)[:, None] * freq
    return tuple(
        jnp.asarray(v.astype(np.float32))
        for v in (np.cos(coarse), np.sin(coarse), np.cos(fine), np.sin(fine))
    )


def per_device(
    x,
    gain_attn,
    w_query,
    w_key,
    w_value,
    w_out,
    gain_moe,
    expert_gate,
    expert_up,
    expert_down,
    routes,
    route_gates,
    layout,
    g,
):
    s = lax.axis_index("shard")
    c = lax.axis_index("core")
    info = jnp.stack(
        [s, c, lax.axis_index("z"), lax.axis_index("xh"), lax.axis_index("tensor")]
    ).astype(jnp.int32)
    first = c == 0
    tables = angle_tables()

    def mine(v, axis):
        width = v.shape[axis] // 2
        return jnp.where(
            first,
            lax.slice_in_dim(v, 0, width, axis=axis),
            lax.slice_in_dim(v, width, 2 * width, axis=axis),
        )

    def both_cores(own, oth, axis):
        return jnp.where(
            first, jnp.concatenate([own, oth], axis), jnp.concatenate([oth, own], axis)
        )

    packed = jnp.concatenate(
        [mine(w_query, 1), mine(w_key, 1), jnp.zeros((HALF, HD), B16), mine(w_value, 1)], axis=1
    )
    wa, wb = packed[:384], packed[384:]
    ra, rb = to_x(wa, 1), to_x(wb, -1)
    x_t = other_core(x)
    wo = mine(after(w_out, wa, wb), 0)
    wo_t = jnp.concatenate([to_x(wo[:96], 1), to_x(wo[96:], -1)], axis=0)
    gains = jnp.stack([gain_attn, gain_moe])
    gains_t = to_x(gains, 1)
    g1o, g1t, g2o, g2t = gains[0:1], gains_t[0:1], gains[1:2], gains_t[1:2]
    a, q, kv = run(
        qkv_kernel,
        "qkv",
        3,
        (info, layout, x, x_t, g1o, g1t, wa, wb, ra, rb, *tables),
        [smem(), smem()] + [whole()] * 12,
        (shape_of((512, D), B16), shape_of((3, 512, 128), B16), shape_of((8, 512, 128), B16)),
        [whole()] * 3,
    )
    slots = lax.all_to_all(kv, ("z", "xh"), 0, 0, tiled=True)
    wo_own = lax.all_gather(jnp.stack([wo, wo_t]), "tensor")
    down_c = lax.dynamic_slice_in_dim(after(expert_down, slots), c * OWN, OWN, 0)
    gate_c = lax.dynamic_slice_in_dim(after(expert_gate, slots), c * OWN, OWN, 0)
    up_c = lax.dynamic_slice_in_dim(after(expert_up, slots), c * OWN, OWN, 0)
    down_ra, down_rb = to_x(down_c[:, :64], 1), to_x(down_c[:, 64:], -1)
    gate_t, up_t = to_x(gate_c, 1), to_x(up_c, -1)
    g_t = other_core(after(g, kv))
    ids = jnp.arange(EXPERTS, dtype=jnp.int32)
    share = jnp.sum(
        jnp.where(routes[:, :, None] == ids[None, None, :], route_gates[:, :, None], 0.0), axis=1
    )
    share = after(share, kv)
    share = jnp.concatenate([share, other_core(share)], axis=0)
    share = jnp.where(first, share[:, :OWN], share[:, OWN:])
    o, o_send, lse = run(
        attend_kernel,
        "attend",
        14,
        (info, layout, after(q, share), slots),
        [smem(), smem()] + [whole()] * 2,
        (shape_of((512, 256), B16), shape_of((256, 256), B16), shape_of((4, 1, ROWS), F32)),
        [whole()] * 3,
        scratch=[VMEM((4096, 128), B16), VMEM((128, 4096), B16)],
    )
    lifted, g_roll = run(
        lift_kernel,
        "lift",
        5,
        (info, after(g, o), g_t, down_c, down_ra, down_rb),
        [smem(), fixed(256, D), fixed(256, D), each(FC, HALF), each(64, HALF), each(64, HALF)],
        (shape_of((OWN, 512, FC), F32), shape_of((512, D), B16)),
        [each(512, FC), fixed(512, D)],
        grid=(OWN,),
    )
    wo_oth = other_core(after(wo_own, o))
    o_all = jnp.concatenate([o[:256], other_core(o_send)], axis=1)
    o_tok = over_y(o_all.reshape(4, 64, 512))
    o_tok = after(o_tok, lifted)
    h, b64 = run(
        token_kernel,
        "token",
        3,
        (info, x, o_tok, wo_own, wo_oth, g2o, g2t),
        [smem()] + [whole()] * 6,
        (shape_of((64, D), F32), shape_of((64, D), B16)),
        [whole()] * 2,
    )
    b_own = [b64, *from_each_y(b64)]
    b_oth = [other_core(v) for v in b_own]
    out_own, out_oth, hw, dgu, b = run(
        expert_kernel,
        "expert",
        13,
        (info, *b_own, *b_oth, share, lifted, gate_c, gate_t, up_c, up_t, down_c, down_ra, down_rb),
        [smem()]
        + [whole()] * 9
        + [each(512, FC)]
        + [each(HALF, FC)] * 4
        + [each(FC, HALF), each(64, HALF), each(64, HALF)],
        (
            shape_of((512, D), B16),
            shape_of((512, D), B16),
            shape_of((OWN, 512, FC), B16),
            shape_of((OWN, 512, 2 * FC), B16),
            shape_of((512, D), B16),
        ),
        [whole(), whole(), each(512, FC), each(512, 2 * FC), whole()],
        scratch=[VMEM((512, D), F32), VMEM((512, D), F32)],
        grid=(OWN,),
    )

    def to_tokens(own, oth, name):
        return run(
            fold_kernel,
            name,
            2,
            (info, own, other_core(oth)),
            [smem()] + [whole()] * 2,
            (shape_of((own.shape[0] // 4, D), F32),)
            + (shape_of((own.shape[0] // 4, D), B16),) * 3,
            [whole()] * 4,
        )

    def over_pieces(parts):
        return [parts[0]] + [to_y(parts[k], k) for k in range(1, 4)]

    db = to_tokens(out_own, out_oth, "fold_b")
    halves = shape_of((2, 3, OWN, 48, FC), B16)
    quarter = shape_of((4, 3, OWN, 48, FC), B16)

    def by_expert(n):
        return pl.BlockSpec((n, 3, 1, 48, FC), lambda e: (0, 0, e, 0, 0))

    sent = run(
        expert_grad_kernel,
        "expert_grad",
        8.3,
        (info, after(b, db[1]), g_roll, hw, dgu),
        [smem(), fixed(512, D), fixed(512, D), each(512, FC), each(512, 2 * FC)],
        (quarter, quarter, halves, halves, quarter) * 2,
        [by_expert(4), by_expert(4), by_expert(2), by_expert(2), by_expert(4)] * 2,
        scratch=[VMEM((HALF, 2 * FC), B16), VMEM((FC, HALF), B16)],
        grid=(OWN,),
    )
    flat = (3 * OWN * 48, FC)
    sent = [v.reshape(-1, *flat) for v in sent]
    xs, zs = sent[:5], sent[5:]
    db = over_pieces(db)
    db[0] = after(db[0], *sent)
    dh, dattn, do_tok, gsum_moe, y64 = run(
        token_back_kernel,
        "token_back",
        4.4,
        (info, h, *db, g, wo_own, wo_oth, g2o, g2t),
        [smem()] + [whole()] * 10,
        (
            shape_of((64, D), F32),
            shape_of((4, 64, D), B16),
            shape_of((4, 64, 512), B16),
            shape_of((1, D), F32),
            shape_of((64, D), B16),
        ),
        [whole()] * 5,
    )
    xs[2], xs[3], zs[2], zs[3], _ = lax.optimization_barrier((xs[2], xs[3], zs[2], zs[3], dh))
    passing = (to_x(xs[2], 1), to_x(xs[3], -1), to_z(zs[2], 1), to_z(zs[3], -1))
    do = over_y(do_tok).reshape(256, 512)
    do_oth = other_core(do)
    four = shape_of((4, *flat), B16)
    x_up, x_down, z_up, z_down = run(
        pass_on_kernel,
        "pass_on",
        3,
        (xs[1], xs[4], *passing[:2], zs[1], zs[4], *passing[2:]),
        [whole()] * 8,
        (four,) * 4,
        [whole()] * 4,
    )
    got = (to_x(x_up, 1), to_x(x_down, -1), to_z(z_up, 1), to_z(z_down, -1))

    do = after(do, x_up)
    dattn = over_y(after(dattn, do)).reshape(256, D)
    dq, dkv = run(
        attend_back_kernel,
        "attend_back",
        16,
        (info, layout, q, do, do_oth, o, lse, *tables, slots),
        [smem(), smem()] + [whole()] * 10,
        (shape_of((512, 256), B16), shape_of((8, 512, 128), B16)),
        [whole()] * 2,
        scratch=[VMEM((4096, 128), B16), VMEM((128, 4096), B16), VMEM((4096, 128), F32)],
    )
    dkv = lax.all_to_all(after(dkv, *got, dattn), ("z", "xh"), 0, 0, tiled=True)
    dattn_oth = other_core(dattn)

    one, one32 = shape_of(flat, B16), shape_of(flat, F32)
    xz = run(
        gather_sum_kernel,
        "plane_sum",
        4,
        (after(xs[0], dq), *got[:2], zs[0], *got[2:]),
        [whole()] * 6,
        (one32, one, one, one) * 2,
        [whole()] * 8,
    )
    second = [xz[0]] + [to_z(xz[k], k) for k in range(1, 4)]
    second += [xz[4]] + [to_x(xz[4 + k], k) for k in range(1, 4)]
    dkv = after(dkv, dattn_oth)
    dqkv, da_own, da_oth = run(
        qkv_back_kernel,
        "qkv_back",
        5.6,
        (info, layout, dq, dkv, wa, wb, ra, rb, *tables),
        [smem(), smem()] + [whole()] * 10,
        (shape_of((512, 384), B16), shape_of((256, D), B16), shape_of((256, D), B16)),
        [whole()] * 3,
    )
    ea, eb = run(
        sum_kernel, "plane_sum2", 1, (after(second[0], dqkv), *second[1:]), [whole()] * 8, (one, one), [whole()] * 2
    )

    grads = run(
        attend_grad_kernel,
        "attend_grad",
        4.4,
        (info, a, after(dqkv, ea, eb), dattn, dattn_oth, o, gsum_moe, wa, wb, ra, rb),
        [smem()] + [whole()] * 10,
        (shape_of((16, 112, 512), B16),),
        [whole()],
    )[0]
    grads_in = grads
    grads = lax.all_to_all(grads, PLANE, 0, 0, tiled=True)
    def stacked(arrays, name):
        n = len(arrays)
        return run(
            functools.partial(stack_kernel, n),
            name,
            1,
            (info, *arrays),
            [smem()] + [whole()] * n,
            (shape_of((n, *flat), B16),),
            [whole()],
        )[0]

    ea = lax.all_gather(ea, ("xh", "z"))
    eb_pair = stacked([eb, to_x(eb, 2)], "along_x")
    e_own = [ea, eb_pair] + [to_z(eb_pair, 4 - k) for k in range(1, 4)]
    da = over_pieces(to_tokens(after(da_own, grads_in), da_oth, "fold_a"))
    e_own = [v.reshape(-1, 3, OWN, 48, FC) for v in e_own]
    e_oth = [other_core(v) for v in e_own]

    ig = run(
        input_back_kernel,
        "input_back",
        1,
        (info, dh, *da, x, g1o, g1t, y64),
        [smem()] + [whole()] * 9,
        (shape_of((128, D), B16),),
        [whole()],
    )[0]


    input_grad, output = run(
        place_kernel,
        "place",
        3,
        (info, ig, *from_each_y(ig)),
        [smem()] + [whole()] * 4,
        (shape_of((256, D), F32), shape_of((256, D), B16)),
        [whole()] * 2,
    )

    grads = jnp.sum(grads.astype(F32), axis=0).astype(B16)
    grads = lax.all_to_all(
        jnp.broadcast_to(grads[None], (8, 112, 512)), ("xh", "z"), 0, 0, tiled=True
    )
    grads = after(grads, *e_own[1:])
    grads_t = other_core(grads)
    gsum = grads[:, 96:98, :96].astype(F32).transpose(1, 0, 2).reshape(2, HALF)
    gsum = gsum + sum(from_each_y(gsum))
    gsum = gsum + other_core(gsum)

    expert_grads = pl.pallas_call(
        assemble_kernel,
        name="assemble",
        grid_spec=pltpu.PrefetchScalarGridSpec(
            num_scalar_prefetch=1,
            grid=(2, OWN),
            in_specs=[
                pl.BlockSpec(
                    (n, 3, 1, 48, FC),
                    (lambda q, e, info: (0, 0, jnp.where(q == 0, e, OWN - 1), 0, 0))
                    if own
                    else (lambda q, e, info: (0, 0, jnp.where(q == 0, 0, e), 0, 0)),
                )
                for own in (True, False)
                for n in (8, 2, 2, 2, 2)
            ],
            out_specs=[
                pl.BlockSpec(
                    (1, *shape), lambda n, e, info: (((info[1] + n) & 1) * OWN + e, 0, 0)
                )
                for shape in ((HALF, FC), (HALF, FC), (FC, HALF))
            ],
        ),
        out_shape=(
            shape_of((EXPERTS, HALF, FC), F32),
            shape_of((EXPERTS, HALF, FC), F32),
            shape_of((EXPERTS, FC, HALF), F32),
        ),
        cost_estimate=cost(9),
        compiler_params=pltpu.CompilerParams(vmem_limit_bytes=60 * 2**20),
    )(info, *e_own, *e_oth)
    wq_grad, wk_grad, wv_grad, wo_grad = run(
        finish_kernel,
        "finish",
        3,
        (info, grads, after(grads_t, expert_grads[0])),
        [smem()] + [whole()] * 2,
        tuple(shape_of(v, F32) for v in ((HALF, 384), (HALF, 128), (HALF, 128), (384, HALF))),
        [whole()] * 4,
        scratch=[VMEM((HALF, 384), F32)],
    )
    return (
        output,
        input_grad,
        gsum[0] / gain_attn.astype(F32),
        wq_grad,
        wk_grad,
        wv_grad,
        wo_grad,
        gsum[1],
        *expert_grads,
    )


def solution(mesh):
    fine = Mesh(
        mesh.devices.reshape(2, 4, 2, 2, 4), ("shard", "z", "xh", "core", "tensor")
    )
    rows = P(("shard", "z", "xh", "core"), None)
    placed = (
        rows,
        P("shard"),
        P("shard", "tensor"),
        P("shard", "tensor"),
        P("shard", "tensor"),
        P("tensor", "shard"),
        P("shard"),
        P(None, "shard", "tensor"),
        P(None, "shard", "tensor"),
        P(None, "tensor", "shard"),
        rows,
        rows,
        P(),
        rows,
    )
    return jax.shard_map(
        per_device,
        mesh=fine,
        in_specs=placed,
        out_specs=(
            rows,
            rows,
            P("shard"),
            P("shard", "tensor"),
            P("shard", "tensor"),
            P("shard", "tensor"),
            P("tensor", "shard"),
            P("shard"),
            P(None, "shard", "tensor"),
            P(None, "shard", "tensor"),
            P(None, "tensor", "shard"),
        ),
        check_vma=False,
    )
```

```python
import functools

import jax
import jax.numpy as jnp
import numpy as np
from jax import lax
from jax.experimental import pallas as pl
from jax.experimental.pallas import tpu as pltpu
from jax.sharding import Mesh
from jax.sharding import PartitionSpec as P

D = 1536
HALF = 768
HD = 64
EXPERTS = 10
OWN = 5
FC = 128
EPS = 1e-05
SCALE = 0.125
CHUNK = 1024
SEG = 128
ROWS = 3 * SEG
NEG = -1e30
B16 = jnp.bfloat16
F32 = jnp.float32
X = ("shard", "xh")
PLANE = ("shard", "xh", "z")
VMEM = pltpu.VMEM
SMEM = pltpu.SMEM


def nn(a, b):
    return lax.dot_general(a, b, (((1,), (0,)), ((), ())), preferred_element_type=F32)


def nt(a, b):
    return lax.dot_general(a, b, (((1,), (1,)), ((), ())), preferred_element_type=F32)


def tn(a, b):
    return lax.dot_general(a, b, (((0,), (0,)), ((), ())), preferred_element_type=F32)


def x_pairs(k):
    pairs = []
    for sh in range(2):
        for xh in range(2):
            at = (2 * xh + sh + k) % 4
            pairs.append((sh * 2 + xh, (at % 2) * 2 + at // 2))
    return pairs


def to_x(v, k):
    return lax.ppermute(v, X, x_pairs(k))


def other_core(v):
    return lax.ppermute(v, "core", [(0, 1), (1, 0)])


def to_y(v, k):
    return lax.ppermute(v, "tensor", [(i, (i + k) % 4) for i in range(4)])


def to_z(v, k):
    return lax.ppermute(v, "z", [(i, (i + k) % 4) for i in range(4)])


def over_y(v):
    return lax.all_to_all(v, "tensor", 0, 0, tiled=True)


def from_each_y(v):
    return [to_y(v, 4 - k) for k in range(1, 4)]


def after(v, *others):
    return lax.optimization_barrier((v, *others))[0]


def half_of(s):
    return pl.ds(pl.multiple_of(s * HALF, HALF), HALF)


def piece_of(info, k):
    return pl.ds(pl.multiple_of(((info[4] + k) & 3) * 64, 64), 64)


def seg_at(info, layout, slot, blk, j):
    cc = info[1] if blk == 0 else 1 - info[1]
    return layout[(slot * 2 + cc) * 2 + j]


def seg_of(info, layout, blk, j):
    return seg_at(info, layout, info[2] * 2 + info[3], blk, j)


def angle_rows(at, ca, sa, cb, sb):
    ca, sa = ca[pl.ds(at, 1), :], sa[pl.ds(at, 1), :]
    return ca * cb[...] - sa * sb[...], sa * cb[...] + ca * sb[...]


def low_lanes(shape):
    return lax.broadcasted_iota(jnp.int32, shape, 1) < HD


def first_half_of_head(shape):
    return (lax.broadcasted_iota(jnp.int32, shape, 1) & (HD - 1)) < HD // 2


def rope(u, cos, sin):
    turned = jnp.where(
        first_half_of_head(u.shape), -pltpu.roll(u, 96, 1), pltpu.roll(u, 32, 1)
    )
    return u * cos + turned * sin


def unrope(u, cos, sin):
    w = u * sin
    turned = jnp.where(
        first_half_of_head(u.shape), pltpu.roll(w, 96, 1), -pltpu.roll(w, 32, 1)
    )
    return u * cos + turned


def qkv_kernel(
    info, layout, xo, xt, gain_o, gain_t, wa, wb, ra, rb, ca, sa, cb, sb, a_out, q_out, kv_out
):
    s = info[0]
    for blk, ref in enumerate((xo, xt)):
        lo = ref[:, half_of(s)].astype(F32)
        hi = ref[:, half_of(1 - s)].astype(F32)
        mean = (
            jnp.sum(lo * lo, axis=1, keepdims=True) + jnp.sum(hi * hi, axis=1, keepdims=True)
        ) / D
        inv = lax.rsqrt(mean + EPS)
        alo = (lo * inv * gain_o[...].astype(F32)).astype(B16)
        ahi = (hi * inv * gain_t[...].astype(F32)).astype(B16)
        a_out[blk * 256 : blk * 256 + 256, :HALF] = alo
        a_out[blk * 256 : blk * 256 + 256, HALF:] = ahi
        t = (
            nn(alo[:, :384], wa[...])
            + nn(alo[:, 384:], wb[...])
            + nn(ahi[:, :384], ra[...])
            + nn(ahi[:, 384:], rb[...])
        )
        for j in range(2):
            cos, sin = angle_rows(seg_of(info, layout, blk, j), ca, sa, cb, sb)
            tt = t[j * SEG : (j + 1) * SEG]
            low = low_lanes((SEG, SEG))
            t0 = rope(tt[:, :128], cos, sin)
            t1 = rope(tt[:, 128:256], cos, sin)
            t2 = tt[:, 256:]
            rows = slice(blk * 256 + j * SEG, blk * 256 + (j + 1) * SEG)
            zero = jnp.zeros_like(t0)

            def scaled(v):
                return (v.astype(B16).astype(F32) * SCALE).astype(B16)

            q_out[0, rows] = scaled(jnp.where(low, t0, zero))
            q_out[1, rows] = scaled(jnp.where(low, pltpu.roll(t0, HD, 1), zero))
            q_out[2, rows] = scaled(jnp.where(low, t1, zero))
            kv = jnp.where(low, pltpu.roll(t1, HD, 1), t2).astype(B16)
            for slot in range(8):
                kv_out[slot, rows] = kv


def fill_sorted(info, layout, slots, ks, kst):
    for slot in range(8):
        for blk in range(2):
            for j in range(2):
                at = pl.multiple_of(seg_at(info, layout, slot, blk, j) * SEG, SEG)
                part = slots[slot, blk * 256 + j * SEG : blk * 256 + (j + 1) * SEG, :]
                ks[pl.ds(at, SEG), :] = part
                kst[:, pl.ds(at, SEG)] = part.astype(F32).T.astype(B16)


def allowed_keys(j, pos):
    key = j * CHUNK + lax.broadcasted_iota(jnp.int32, (CHUNK, ROWS), 0)
    query = pos * SEG + (lax.broadcasted_iota(jnp.int32, (CHUNK, ROWS), 1) & (SEG - 1))
    return key <= query


def heads_of(q, i):
    return jnp.concatenate([q[h, i * SEG : (i + 1) * SEG, :] for h in range(3)], axis=0)


def attend_kernel(info, layout, q, slots, o_out, o_send, lse_out, ks, kst):
    fill_sorted(info, layout, slots, ks, kst)
    low = low_lanes((SEG, SEG))
    for pair in range(2):
        at_pos = [seg_of(info, layout, pair, n) for n in range(2)]
        qs = [heads_of(q, pair * 2 + n) for n in range(2)]
        full = [lax.div(p, CHUNK // SEG) for p in at_pos]

        def one(j, carry, n, edge):
            top, total, acc = carry
            at = pl.multiple_of(j * CHUNK, CHUNK)
            sc = nt(ks[pl.ds(at, CHUNK), :], qs[n])
            if edge:
                sc = jnp.where(allowed_keys(j, at_pos[n]), sc, NEG)
            new = jnp.maximum(top, jnp.max(sc, axis=0, keepdims=True))
            e = jnp.exp(sc - new)
            back = jnp.exp(top - new)
            total = total * back + jnp.sum(e, axis=0, keepdims=True)
            acc = acc * back + nn(kst[:, pl.ds(at, CHUNK)], e.astype(B16))
            return new, total, acc

        start = (
            jnp.full((1, ROWS), NEG, F32),
            jnp.zeros((1, ROWS), F32),
            jnp.zeros((SEG, ROWS), F32),
        )
        both = jnp.minimum(full[0], full[1])

        def two(j, carry):
            return one(j, carry[0], 0, False), one(j, carry[1], 1, False)

        carry = lax.fori_loop(0, both, two, (start, start))
        rest = [
            lax.fori_loop(both, full[n], lambda j, c, n=n: one(j, c, n, False), carry[n])
            for n in range(2)
        ]
        ends = [one(full[n], rest[n], n, True) for n in range(2)]
        for n in range(2):
            i = pair * 2 + n
            top, total, acc = ends[n]
            lse_out[i] = top + jnp.log(total)
            o = (acc / total).T
            o0, o1, o2 = o[:SEG], o[SEG : 2 * SEG], o[2 * SEG :]
            left = jnp.where(low, pltpu.roll(o0, HD, 1), o1).astype(B16)
            right = jnp.where(low, pltpu.roll(o2, HD, 1), jnp.zeros_like(o2)).astype(B16)
            for out, at in ((o_out, i * SEG),) + (((o_send, (i - 2) * SEG),) if i >= 2 else ()):
                out[at : at + SEG, :SEG] = left
                out[at : at + SEG, SEG:] = right


def attend_back_kernel(
    info, layout, q, do_own, do_oth, o, lse, ca, sa, cb, sb, ks, kst, dq_out, dkv_out, dkv
):
    dkv[...] = jnp.zeros_like(dkv)
    low = low_lanes((SEG, SEG))

    def spread(t0, t1):
        zero = jnp.zeros((SEG, SEG), F32)
        return jnp.concatenate(
            [
                jnp.where(low, zero, pltpu.roll(t0, HD, 1)),
                jnp.where(low, zero, t0),
                jnp.where(low, zero, pltpu.roll(t1, HD, 1)),
            ],
            axis=0,
        )

    for pair in range(2):
        at_pos = [seg_of(info, layout, pair, n) for n in range(2)]
        qs, dos, deltas, lses = [], [], [], []
        do, at = (do_own, 0) if pair == 0 else (do_oth, 256)
        for n in range(2):
            rows = slice((pair * 2 + n) * SEG, (pair * 2 + n + 1) * SEG)
            here = slice(n * SEG, (n + 1) * SEG)
            dof = spread(
                do[here, at : at + SEG].astype(F32), do[here, at + SEG : at + 2 * SEG].astype(F32)
            )
            of = spread(o[rows, :SEG].astype(F32), o[rows, SEG:].astype(F32))
            qs.append(heads_of(q, pair * 2 + n))
            dos.append(dof.astype(B16))
            deltas.append(jnp.sum((dof * of).T, axis=0, keepdims=True))
            lses.append(lse[pair * 2 + n])
        full = [lax.div(p, CHUNK // SEG) for p in at_pos]

        def one(j, acc, n, edge):
            at = pl.multiple_of(j * CHUNK, CHUNK)
            kv = ks[pl.ds(at, CHUNK), :]
            p = jnp.exp(nt(kv, qs[n]) - lses[n])
            if edge:
                p = jnp.where(allowed_keys(j, at_pos[n]), p, 0.0)
            ds = (p * (nt(kv, dos[n]) - deltas[n])).astype(B16)
            return (
                acc + nn(kst[:, pl.ds(at, CHUNK)], ds),
                nn(ds, qs[n]) + nn(p.astype(B16), dos[n]),
            )

        def alone(j, acc, n, edge=False):
            acc, more = one(j, acc, n, edge)
            dkv[pl.ds(pl.multiple_of(j * CHUNK, CHUNK), CHUNK), :] += more
            return acc

        def two(j, accs):
            a0, m0 = one(j, accs[0], 0, False)
            a1, m1 = one(j, accs[1], 1, False)
            dkv[pl.ds(pl.multiple_of(j * CHUNK, CHUNK), CHUNK), :] += m0 + m1
            return a0, a1

        zero = jnp.zeros((SEG, ROWS), F32)
        both = jnp.minimum(full[0], full[1])
        accs = lax.fori_loop(0, both, two, (zero, zero))
        accs = [
            lax.fori_loop(both, full[n], lambda j, c, n=n: alone(j, c, n), accs[n])
            for n in range(2)
        ]
        accs = [alone(full[n], accs[n], n, True) for n in range(2)]
        for n in range(2):
            rows = slice((pair * 2 + n) * SEG, (pair * 2 + n + 1) * SEG)
            dq = accs[n].T * SCALE
            cos, sin = angle_rows(at_pos[n], ca, sa, cb, sb)
            d0, d1, d2 = [unrope(dq[h * SEG : (h + 1) * SEG], cos, sin) for h in range(3)]
            dq_out[rows, :SEG] = jnp.where(low, d0, pltpu.roll(d1, HD, 1)).astype(B16)
            dq_out[rows, SEG:] = jnp.where(low, d2, jnp.zeros_like(d2)).astype(B16)
    for slot in range(8):
        for blk in range(2):
            for j in range(2):
                at = pl.multiple_of(seg_at(info, layout, slot, blk, j) * SEG, SEG)
                dkv_out[slot, blk * 256 + j * SEG : blk * 256 + (j + 1) * SEG, :] = dkv[
                    pl.ds(at, SEG), :
                ].astype(B16)


def token_kernel(info, x, o, w_own, w_oth, gain_o, gain_t, h_out, b_out):
    s = info[0]
    here = piece_of(info, 0)
    alo = jnp.zeros((64, HALF), F32)
    ahi = jnp.zeros((64, HALF), F32)
    for y in range(4):
        for part, w in ((o[y, :, :192], w_own), (o[y, :, 256:448], w_oth)):
            alo += nn(part, w[y, 0])
            ahi += nn(part, w[y, 1])
    lo = x[here, half_of(s)].astype(F32) + alo
    hi = x[here, half_of(1 - s)].astype(F32) + ahi
    mean = (
        jnp.sum(lo * lo, axis=1, keepdims=True) + jnp.sum(hi * hi, axis=1, keepdims=True)
    ) / D
    inv = lax.rsqrt(mean + EPS)
    h_out[:, :HALF] = lo
    h_out[:, HALF:] = hi
    blo = (lo * inv * gain_o[...].astype(F32)).astype(B16)
    bhi = (hi * inv * gain_t[...].astype(F32)).astype(B16)
    b_out[:, :HALF] = blo
    b_out[:, HALF:] = bhi


def norm_back(grads, sources, gains):
    mean = sum(jnp.sum(v * v, axis=1, keepdims=True) for v in sources) / D
    inv = lax.rsqrt(mean + EPS)
    weighted = [d * g for d, g in zip(grads, gains)]
    dot = sum(jnp.sum(w * v, axis=1, keepdims=True) for w, v in zip(weighted, sources)) / D
    cube = inv * inv * inv * dot
    return (
        [inv * w - v * cube for w, v in zip(weighted, sources)],
        [jnp.sum(d * v * inv, axis=0, keepdims=True) for d, v in zip(grads, sources)],
    )


def fold_kernel(info, own, received, out0, out1, out2, out3, *rest):
    for k, out in enumerate((out0, out1, out2, out3)):
        rows = piece_of(info, k)
        out[...] = (own[rows].astype(F32) + received[rows].astype(F32)).astype(out.dtype)
    if rest:
        total = own[256:].astype(F32) + received[256:].astype(F32)
        rest[0][...] = total.astype(B16).reshape(4, 64, D)


def token_back_kernel(
    info, h, d0, d1, d2, d3, moe, g, w_own, w_oth, gain_o, gain_t, dh_out, both_out, do_out, gain_out
):
    s = info[0]
    here = piece_of(info, 0)
    total = sum(d[...].astype(F32) for d in (d0, d1, d2, d3))
    halves = (slice(0, HALF), slice(HALF, D))
    back, gsum = norm_back(
        [total[:, k] for k in halves],
        [h[:, k] for k in halves],
        [gain_o[...].astype(F32), gain_t[...].astype(F32)],
    )
    for k, part, sums, half in zip(halves, back, gsum, (s, 1 - s)):
        dh = g[here, half_of(half)].astype(F32) + part
        dh_out[:, k] = dh
        for y in range(4):
            both_out[y, :64, k] = dh.astype(B16)
            both_out[y, 64:, k] = moe[y, :, k]
        gain_out[:, k] = sums
    dattn = both_out[0, :64]
    pad = jnp.zeros((64, 64), B16)
    for y in range(4):
        for at, w in ((0, w_own), (256, w_oth)):
            do = nt(dattn[:, :HALF], w[y, 0]) + nt(dattn[:, HALF:], w[y, 1])
            do_out[y, :, at : at + 192] = do.astype(B16)
            do_out[y, :, at + 192 : at + 256] = pad


def input_back_kernel(info, dh, d0, d1, d2, d3, x, gain_o, gain_t, h, both, out):
    s = info[0]
    here = piece_of(info, 0)
    total = sum(d[...].astype(F32) for d in (d0, d1, d2, d3))
    halves = (slice(0, HALF), slice(HALF, D))
    back, _ = norm_back(
        [total[:, k] for k in halves],
        [x[here, half_of(half)].astype(F32) for half in (s, 1 - s)],
        [gain_o[...].astype(F32), gain_t[...].astype(F32)],
    )
    for k, part in zip(halves, back):
        out[:64, k] = (dh[:, k] + part).astype(B16)
    out[64:] = (h[...] + sum(both[y, 64:].astype(F32) for y in range(4))).astype(B16)


def place_kernel(info, p0, p1, p2, p3, grad, y):
    s = info[0]
    for k, p in enumerate((p0, p1, p2, p3)):
        for n, out in enumerate((grad, y)):
            rows = slice(n * 64, (n + 1) * 64)
            out[piece_of(info, k), half_of(s)] = p[rows, :HALF].astype(out.dtype)
            out[piece_of(info, k), half_of(1 - s)] = p[rows, HALF:].astype(out.dtype)


def qkv_back_kernel(
    info, layout, dq, dkv, wa, wb, ra, rb, ca, sa, cb, sb, d_out, da_own, da_oth
):
    for i in range(4):
        rows = slice(i * SEG, (i + 1) * SEG)
        total = sum(dkv[r, rows].astype(F32) for r in range(8))
        cos, sin = angle_rows(seg_of(info, layout, i // 2, i % 2), ca, sa, cb, sb)
        low = low_lanes((SEG, SEG))
        dk = unrope(total, cos, sin)
        d_out[rows, :SEG] = dq[rows, :SEG]
        d_out[rows, SEG : 2 * SEG] = jnp.where(
            low, dq[rows, SEG:].astype(F32), pltpu.roll(dk, HD, 1)
        ).astype(B16)
        d_out[rows, 2 * SEG :] = jnp.where(low, jnp.zeros_like(total), total).astype(B16)
    for n, out in enumerate((da_own, da_oth)):
        d = d_out[n * 256 : (n + 1) * 256, :]
        for m, w in enumerate((wa, wb, ra, rb)):
            out[:, m * 384 : (m + 1) * 384] = nt(d, w[...]).astype(B16)


def early_grad_kernel(info, a, dq, own, oth, o, wa, wb, ra, rb, out, along_out):
    s = info[0]
    low = low_lanes((384, SEG))
    for m, w in enumerate((wa, wb, ra, rb)):
        k = slice(m * 384, (m + 1) * 384)
        dw = tn(a[:, k], dq[...])
        dwo = jnp.zeros((384, 256), F32)
        for n, both in enumerate((own, oth)):
            for y in range(4):
                at = n * 256 + y * 64
                dwo += tn(both[y, :64, k], o[at : at + 64])
        along = dw[:, :SEG] * w[:, :SEG].astype(F32)
        along += jnp.where(low, dw[:, SEG:] * w[:, SEG : 2 * SEG].astype(F32), 0.0)
        along_out[:, k] = jnp.sum(along.T, axis=0, keepdims=True)
        last = jnp.where(low, dw[:, SEG:], pltpu.roll(dwo[:, SEG:], HD, 1))
        sh = (s + m // 2) & 1
        for z in range(4):
            at = sh * 8 + (m % 2) * 4 + z
            part = slice(z * 96, (z + 1) * 96)
            out[at, :, :SEG] = dw[part, :SEG].astype(B16)
            out[at, :, SEG : 2 * SEG] = last[part].astype(B16)
            out[at, :, 2 * SEG :] = dwo[part, :SEG].astype(B16)


def late_grad_kernel(info, a, dqkv, gain_q, gain_moe, wa, wb, ra, rb, out):
    s = info[0]
    low = low_lanes((512, SEG))
    low_w = low_lanes((384, SEG))

    def joined(low, v):
        return jnp.where(low, pltpu.roll(v[:, SEG : 2 * SEG].astype(F32), HD, 1), v[:, 2 * SEG :].astype(F32))

    d = joined(low, dqkv[...]).astype(B16)
    row = lax.broadcasted_iota(jnp.int32, (16, SEG), 0)
    for m, w in enumerate((wa, wb, ra, rb)):
        k = slice(m * 384, (m + 1) * 384)
        dw = tn(a[:, k], d)
        gain = jnp.sum((dw * joined(low_w, w[...])).T, axis=0, keepdims=True) + gain_q[:, k]
        moe = gain_moe[:, k]
        sh = (s + m // 2) & 1
        for z in range(4):
            at = sh * 8 + (m % 2) * 4 + z
            part = slice(z * 96, (z + 1) * 96)
            out[at, :96] = dw[part].astype(B16)
            pad = jnp.zeros((1, 32), F32)
            g0 = jnp.concatenate([gain[:, part], pad], axis=1)
            g1 = jnp.concatenate([moe[:, part], pad], axis=1)
            out[at, 96:] = jnp.where(row == 0, g0, jnp.where(row == 1, g1, 0.0)).astype(B16)


def lift_kernel(info, g_own, g_oth, d_own, d_ra, d_rb, out, g_out):
    s = info[0]
    hi = jnp.concatenate([d_ra[0], d_rb[0]], axis=0)

    @pl.when(pl.program_id(0) == 0)
    def _():
        for n, g in enumerate((g_own, g_oth)):
            rows = slice(n * 256, (n + 1) * 256)
            g_out[rows, :HALF] = g[:, half_of(s)]
            g_out[rows, HALF:] = g[:, half_of(1 - s)]

    out[0] = nt(g_out[:, :HALF], d_own[0]) + nt(g_out[:, HALF:], hi)


def expert_kernel(
    info, b0, b1, b2, b3, b4, b5, b6, b7, w, gd, g_own, g_oth, u_own, u_oth, d_own, d_ra, d_rb,
    out_own, out_oth, hw_out, dgu_out, b, wlo, whi, dlo, dhi, dall, hall,
):
    e = pl.program_id(0)
    lo = jnp.concatenate([g_own[0], u_own[0]], axis=1)
    hi = jnp.concatenate([g_oth[0], u_oth[0]], axis=1)
    pair = pl.ds(pl.multiple_of(e * 2 * FC, 2 * FC), 2 * FC)
    one = pl.ds(pl.multiple_of(e * FC, FC), FC)
    wlo[:, pair] = lo
    whi[:, pair] = hi
    dlo[one] = d_own[0]
    dhi[one] = jnp.concatenate([d_ra[0], d_rb[0]], axis=0)

    @pl.when(e == 0)
    def _():
        for n, ref in enumerate((b0, b1, b2, b3, b4, b5, b6, b7)):
            at = (n // 4) * 256 + ((info[4] + n) & 3) * 64
            b[pl.ds(pl.multiple_of(at, 64), 64)] = ref[...]

    for k in range(2):
        rows = slice(k * 256, (k + 1) * 256)
        gu = nn(b[rows, :HALF], lo) + nn(b[rows, HALF:], hi)
        gate, up = gu[:, :FC], gu[:, FC:]
        sg = jax.nn.sigmoid(gate)
        silu = gate * sg
        here = lax.broadcasted_iota(jnp.int32, (256, OWN), 1) == e
        weight = jnp.sum(jnp.where(here, w[rows], 0.0), axis=1, keepdims=True)
        hw = (silu * up * weight).astype(B16)
        hw_out[0, rows] = hw
        hall[rows, one] = hw
        dh = gd[0, rows] * weight
        dgate = (dh * up * sg * (1.0 + gate * (1.0 - sg))).astype(B16)
        dup = (dh * silu).astype(B16)
        d = jnp.concatenate([dgate, dup], axis=1)
        dgu_out[0, rows] = d
        dall[rows, pair] = d

    @pl.when(e == OWN - 1)
    def _():
        for n, out in enumerate((out_own, out_oth)):
            rows = slice(n * 256, (n + 1) * 256)
            for k in range(6):
                c2 = slice(k * 256, (k + 1) * 256)
                if k < 3:
                    out[:256, c2] = nt(dall[rows], wlo[c2]).astype(B16)
                    out[256:, c2] = nn(hall[rows], dlo[:, c2]).astype(B16)
                else:
                    c1 = slice((k - 3) * 256, (k - 2) * 256)
                    out[:256, c2] = nt(dall[rows], whi[c1]).astype(B16)
                    out[256:, c2] = nn(hall[rows], dhi[:, c1]).astype(B16)


def expert_grad_kernel(info, b, g, hw, dgu, *refs):
    by_x, by_z, dws, dds = refs[:5], refs[5:10], refs[10], refs[11]
    at_x = 2 * info[3] + info[0]

    def put(refs, step, k, kind, value):
        if step == 2:
            refs[2 + k // 2][k % 2, kind, 0] = value
        else:
            refs[{0: 0, 1: 1, 3: 4}[step]][k, kind, 0] = value

    for half in range(2):
        k = slice(half * HALF, (half + 1) * HALF)
        dws[...] = tn(b[:, k], dgu[0]).astype(B16)
        dds[...] = tn(hw[0], g[:, k]).astype(B16)
        for step in (half, half + 2):
            xq = ((at_x + step) & 3) >> 1
            for dz in range(4):
                at = xq * 4 + ((info[2] + dz) & 3)
                for kind in range(3):
                    if kind < 2:
                        piece = dws[
                            pl.ds(pl.multiple_of(at * 96, 32), 96), kind * FC : (kind + 1) * FC
                        ]
                    else:
                        part = dds[pl.ds(pl.multiple_of(at * 16, 16), 16), :]
                        piece = jnp.concatenate(
                            [part[:, l * FC : (l + 1) * FC] for l in range(6)], axis=0
                        )
                    put(by_x, step, dz, kind, piece[:48])
                    put(by_z, dz, step, kind, piece[48:])


def pass_on_kernel(*refs):
    for n in (0, 4):
        up, down, got_up, got_down = refs[n : n + 4]
        out_up, out_down = refs[8 + n // 2], refs[9 + n // 2]
        out_up[:2] = (up[:2].astype(F32) + got_up[...].astype(F32)).astype(B16)
        out_up[2:] = up[2:]
        out_down[:2] = down[:2]
        out_down[2:] = (down[2:].astype(F32) + got_down[...].astype(F32)).astype(B16)


def gather_sum_kernel(*refs):
    for n in (0, 3):
        outs = refs[6 + n // 3 * 4 : 10 + n // 3 * 4]
        for k, out in enumerate(outs):
            out[...] = sum(p[k].astype(F32) for p in refs[n : n + 3]).astype(out.dtype)


def sum_kernel(*refs):
    for n in range(2):
        refs[8 + n][...] = sum(p[...].astype(F32) for p in refs[n * 4 : n * 4 + 4]).astype(B16)


def stack_kernel(n, info, *refs):
    at = info[2] if n == 4 else info[3]
    for k, ref in enumerate(refs[:-1]):
        refs[-1][(at + k) & (n - 1)] = ref[...]


def assemble_kernel(info, *refs):
    gate, up, down = refs[10:]

    def write(everywhere, *by_z):
        def place(v, n, xh, z, part):
            at = xh * 4 + z
            rows = pl.ds(pl.multiple_of(at * 96 + part * 48, 16), 48)
            gate[0, rows] = v[n, 0, 0].astype(F32)
            up[0, rows] = v[n, 1, 0].astype(F32)
            rows = pl.ds(pl.multiple_of(at * 16, 16), 16)
            for l in range(3):
                down[0, rows, (part * 3 + l) * FC : (part * 3 + l + 1) * FC] = v[
                    n, 2, 0, l * 16 : (l + 1) * 16
                ].astype(F32)

        for n in range(8):
            place(everywhere, n, n // 4, n % 4, 0)
        for k, v in enumerate(by_z):
            for xh in range(2):
                place(v, xh, xh, (info[2] + k) & 3, 1)

    @pl.when(pl.program_id(0) == 0)
    def _():
        write(*refs[:5])

    @pl.when(pl.program_id(0) == 1)
    def _():
        write(*refs[5:10])


def sum_grads_kernel(early, late, out):
    first = sum(early[n].astype(F32) for n in range(16)).astype(B16)
    second = sum(late[n].astype(F32) for n in range(16)).astype(B16)
    for n in range(8):
        out[n, :96, : 3 * SEG] = first
        out[n, 96:, : 3 * SEG] = jnp.zeros((16, 3 * SEG), B16)
        out[n, :, 3 * SEG :] = second


def finish_kernel(info, own, oth, wq, wk, wv, wo_out, wo):
    first = info[1] == 0
    low = low_lanes((96, SEG))
    for at in range(8):
        rows = slice(at * 96, (at + 1) * 96)
        a, b = own[at, :96].astype(F32), oth[at, :96].astype(F32)
        a, b = jnp.where(first, a, b), jnp.where(first, b, a)
        a = [a[:, n * SEG : (n + 1) * SEG] for n in range(4)]
        b = [b[:, n * SEG : (n + 1) * SEG] for n in range(4)]
        at_turn = [pltpu.roll(v, HD, 1) for v in a]
        turned = [pltpu.roll(v, HD, 1) for v in b]
        wq[rows, :SEG] = a[0]
        wq[rows, SEG : 2 * SEG] = jnp.where(low, a[1], turned[0])
        wq[rows, 2 * SEG :] = jnp.where(low, turned[0], turned[1])
        wk[rows] = jnp.where(low, a[3], turned[3])
        wv[rows] = jnp.where(low, at_turn[3], b[3])
        wo[rows, :SEG] = a[2]
        wo[rows, SEG : 2 * SEG] = jnp.where(low, at_turn[1], turned[2])
        wo[rows, 2 * SEG :] = jnp.where(low, turned[2], b[1])
    wo_out[...] = wo[...].T


def smem():
    return pl.BlockSpec(memory_space=SMEM)


def whole():
    return None


def each(*shape):
    return pl.BlockSpec((1, *shape), lambda e: (e,) + (0,) * len(shape))


def fixed(*shape):
    return pl.BlockSpec(shape, lambda e: (0,) * len(shape))


def shape_of(shape, dtype):
    return jax.ShapeDtypeStruct(shape, dtype)


def cost(us):
    return pl.CostEstimate(flops=int(us * 3.3e9), bytes_accessed=int(us * 1e7), transcendentals=0)


def run(kernel, name, us, ins, in_specs, outs, out_specs, scratch=(), grid=(1,), mib=60):
    def block(spec, v):
        return fixed(*v.shape) if spec is None else spec

    return pl.pallas_call(
        kernel,
        name=name,
        grid=grid,
        in_specs=[block(spec, v) for spec, v in zip(in_specs, ins, strict=True)],
        out_specs=[block(spec, v) for spec, v in zip(out_specs, outs, strict=True)],
        out_shape=outs,
        scratch_shapes=list(scratch),
        cost_estimate=cost(us),
        compiler_params=pltpu.CompilerParams(vmem_limit_bytes=mib * 2**20),
    )(*ins)


def angle_tables():
    freq = 10000.0 ** (-np.arange(0, HD, 2) / HD)
    freq = np.tile(freq, 4)[None, :]
    coarse = np.arange(32)[:, None] * SEG * freq
    fine = np.arange(SEG)[:, None] * freq
    return tuple(
        jnp.asarray(v.astype(np.float32))
        for v in (np.cos(coarse), np.sin(coarse), np.cos(fine), np.sin(fine))
    )


def per_device(
    x,
    gain_attn,
    w_query,
    w_key,
    w_value,
    w_out,
    gain_moe,
    expert_gate,
    expert_up,
    expert_down,
    routes,
    route_gates,
    layout,
    g,
):
    s = lax.axis_index("shard")
    c = lax.axis_index("core")
    info = jnp.stack(
        [s, c, lax.axis_index("z"), lax.axis_index("xh"), lax.axis_index("tensor")]
    ).astype(jnp.int32)
    first = c == 0
    tables = angle_tables()

    def mine(v, axis):
        width = v.shape[axis] // 2
        return jnp.where(
            first,
            lax.slice_in_dim(v, 0, width, axis=axis),
            lax.slice_in_dim(v, width, 2 * width, axis=axis),
        )

    def both_cores(own, oth, axis):
        return jnp.where(
            first, jnp.concatenate([own, oth], axis), jnp.concatenate([oth, own], axis)
        )

    packed = jnp.concatenate(
        [mine(w_query, 1), mine(w_key, 1), jnp.zeros((HALF, HD), B16), mine(w_value, 1)], axis=1
    )
    wa, wb = packed[:384], packed[384:]
    ra, rb = to_x(wa, 1), to_x(wb, -1)
    x_t = other_core(x)
    wo = mine(after(w_out, wa, wb), 0)
    wo_up, wo_down = to_x(wo[:96], 1), to_x(wo[96:], -1)
    gains = jnp.stack([gain_attn, gain_moe])
    gains_t = to_x(gains, 1)
    g1o, g1t, g2o, g2t = gains[0:1], gains_t[0:1], gains[1:2], gains_t[1:2]
    a, q, kv = run(
        qkv_kernel,
        "qkv",
        0.02,
        (info, layout, x, x_t, g1o, g1t, wa, wb, ra, rb, *tables),
        [smem(), smem()] + [whole()] * 12,
        (shape_of((512, D), B16), shape_of((3, 512, 128), B16), shape_of((8, 512, 128), B16)),
        [whole()] * 3,
    )
    slots = lax.all_to_all(kv, ("z", "xh"), 0, 0, tiled=True)
    wo, wo_up, wo_down, _ = lax.optimization_barrier((wo, wo_up, wo_down, kv))
    wo_both = jnp.stack([wo, jnp.concatenate([wo_up, wo_down], axis=0)])
    wo_own = lax.all_gather(wo_both, "tensor")
    down_c = lax.dynamic_slice_in_dim(after(expert_down, kv), c * OWN, OWN, 0)
    gate_c = lax.dynamic_slice_in_dim(after(expert_gate, kv), c * OWN, OWN, 0)
    up_c = lax.dynamic_slice_in_dim(after(expert_up, kv), c * OWN, OWN, 0)
    down_a, down_b = down_c[:, :64], down_c[:, 64:]
    down_ra, down_rb = to_x(down_a, 1), to_x(down_b, -1)
    gate_t, up_t = to_x(gate_c, 1), to_x(up_c, -1)
    g_t = other_core(after(g, kv))
    ids = jnp.arange(EXPERTS, dtype=jnp.int32)
    share = jnp.sum(
        jnp.where(routes[:, :, None] == ids[None, None, :], route_gates[:, :, None], 0.0), axis=1
    )
    share = after(share, kv)
    share = jnp.concatenate([share, other_core(share)], axis=0)
    share = jnp.where(first, share[:, :OWN], share[:, OWN:])
    o, o_send, lse, ks, kst = run(
        attend_kernel,
        "attend",
        14,
        (info, layout, after(q, share, g_t, gate_c, up_c, down_c, down_a, down_b), slots),
        [smem(), smem()] + [whole()] * 2,
        (
            shape_of((512, 256), B16),
            shape_of((256, 256), B16),
            shape_of((4, 1, ROWS), F32),
            shape_of((4096, 128), B16),
            shape_of((128, 4096), B16),
        ),
        [whole()] * 5,
    )
    o_send = after(o_send, gate_t, up_t)
    o_got = other_core(o_send)
    wo_oth = other_core(after(wo_own, o_got))
    o_all = jnp.concatenate([o[:256], o_got], axis=1)
    o_tok = over_y(o_all.reshape(4, 64, 512))
    h, b64 = run(
        token_kernel,
        "token",
        0.02,
        (info, x, o_tok, wo_own, wo_oth, g2o, g2t),
        [smem()] + [whole()] * 6,
        (shape_of((64, D), F32), shape_of((64, D), B16)),
        [whole()] * 2,
    )
    lifted, g_roll = run(
        lift_kernel,
        "lift",
        6,
        (info, after(g, b64), g_t, down_c, down_ra, down_rb),
        [smem(), fixed(256, D), fixed(256, D), each(FC, HALF), each(64, HALF), each(64, HALF)],
        (shape_of((OWN, 512, FC), F32), shape_of((512, D), B16)),
        [each(512, FC), fixed(512, D)],
        grid=(OWN,),
    )
    b_own = [b64, *from_each_y(b64)]
    b_own = b_own[:1] + [after(v, lifted) for v in b_own[1:]]
    b_oth = [other_core(v) for v in b_own]
    out_own, out_oth, hw, dgu, b = run(
        expert_kernel,
        "expert",
        0.02,
        (info, *b_own, *b_oth, share, lifted, gate_c, gate_t, up_c, up_t, down_c, down_ra, down_rb),
        [smem()]
        + [whole()] * 9
        + [each(512, FC)]
        + [each(HALF, FC)] * 4
        + [each(FC, HALF), each(64, HALF), each(64, HALF)],
        (
            shape_of((512, D), B16),
            shape_of((512, D), B16),
            shape_of((OWN, 512, FC), B16),
            shape_of((OWN, 512, 2 * FC), B16),
            shape_of((512, D), B16),
        ),
        [whole(), whole(), each(512, FC), each(512, 2 * FC), whole()],
        scratch=[
            VMEM((HALF, 2 * FC * OWN), B16),
            VMEM((HALF, 2 * FC * OWN), B16),
            VMEM((FC * OWN, HALF), B16),
            VMEM((FC * OWN, HALF), B16),
            VMEM((512, 2 * FC * OWN), B16),
            VMEM((512, FC * OWN), B16),
        ],
        grid=(OWN,),
    )

    def to_tokens(own, oth, name):
        outs = (shape_of((64, D), F32),) + (shape_of((64, D), B16),) * 3
        if own.shape[0] > 256:
            outs += (shape_of((4, 64, D), B16),)
        return run(
            fold_kernel,
            name,
            2,
            (info, own, other_core(oth)),
            [smem()] + [whole()] * 2,
            outs,
            [whole()] * len(outs),
        )

    def over_pieces(parts):
        return [parts[0]] + [to_y(parts[k], k) for k in range(1, 4)]

    *db, moe = to_tokens(out_own, out_oth, "fold_b")
    halves = shape_of((2, 3, OWN, 48, FC), B16)
    quarter = shape_of((4, 3, OWN, 48, FC), B16)

    def by_expert(n):
        return pl.BlockSpec((n, 3, 1, 48, FC), lambda e: (0, 0, e, 0, 0))

    sent = run(
        expert_grad_kernel,
        "expert_grad",
        9,
        (info, after(b, db[1]), g_roll, hw, dgu),
        [smem(), fixed(512, D), fixed(512, D), each(512, FC), each(512, 2 * FC)],
        (quarter, quarter, halves, halves, quarter) * 2,
        [by_expert(4), by_expert(4), by_expert(2), by_expert(2), by_expert(4)] * 2,
        scratch=[VMEM((HALF, 2 * FC), B16), VMEM((FC, HALF), B16)],
        grid=(OWN,),
    )
    flat = (3 * OWN * 48, FC)
    sent = [v.reshape(-1, *flat) for v in sent]
    xs, zs = sent[:5], sent[5:]
    db = over_pieces(db)
    db[0] = after(db[0], *sent)
    dh, both, do_tok, gsum_moe = run(
        token_back_kernel,
        "token_back",
        0.02,
        (info, h, *db, moe, g, wo_own, wo_oth, g2o, g2t),
        [smem()] + [whole()] * 11,
        (
            shape_of((64, D), F32),
            shape_of((4, 128, D), B16),
            shape_of((4, 64, 512), B16),
            shape_of((1, D), F32),
        ),
        [whole()] * 4,
    )
    xs[2], xs[3], zs[2], zs[3], _ = lax.optimization_barrier((xs[2], xs[3], zs[2], zs[3], dh))
    passing = (to_x(xs[2], 1), to_x(xs[3], -1), to_z(zs[2], 1), to_z(zs[3], -1))
    do = over_y(do_tok).reshape(256, 512)
    do_oth = other_core(do)
    four = shape_of((4, *flat), B16)
    x_up, x_down, z_up, z_down = run(
        pass_on_kernel,
        "pass_on",
        0.02,
        (xs[1], xs[4], *passing[:2], zs[1], zs[4], *passing[2:]),
        [whole()] * 8,
        (four,) * 4,
        [whole()] * 4,
    )
    got = (to_x(x_up, 1), to_x(x_down, -1), to_z(z_up, 1), to_z(z_down, -1))

    do = after(do, x_up)
    both = over_y(after(both, do))
    dq, dkv = run(
        attend_back_kernel,
        "attend_back",
        16,
        (info, layout, q, do, do_oth, o, lse, *tables, ks, kst),
        [smem(), smem()] + [whole()] * 11,
        (shape_of((512, 256), B16), shape_of((8, 512, 128), B16)),
        [whole()] * 2,
        scratch=[VMEM((4096, 128), F32)],
    )
    dkv = lax.all_to_all(after(dkv, *got, both), ("z", "xh"), 0, 0, tiled=True)

    one, one32 = shape_of(flat, B16), shape_of(flat, F32)
    xz = run(
        gather_sum_kernel,
        "plane_sum",
        0.02,
        (after(xs[0], dq), *got[:2], zs[0], *got[2:]),
        [whole()] * 6,
        (one32, one, one, one) * 2,
        [whole()] * 8,
    )
    both_oth = other_core(after(both, xz[1]))
    early, gain_q = run(
        early_grad_kernel,
        "early_grad",
        1,
        (info, a, after(dq, xz[1]), both, both_oth, o, wa, wb, ra, rb),
        [smem()] + [whole()] * 9,
        (shape_of((16, 96, 384), B16), shape_of((1, D), F32)),
        [whole()] * 2,
    )
    xz = list(xz)
    xz[2], xz[6], _ = lax.optimization_barrier((xz[2], xz[6], gain_q))
    second = [xz[0]] + [to_z(xz[k], k) for k in range(1, 4)]
    second += [xz[4]] + [to_x(xz[4 + k], k) for k in range(1, 4)]
    early = lax.all_to_all(after(early, dkv), PLANE, 0, 0, tiled=True)
    dkv = after(dkv, gain_q)
    dqkv, da_own, da_oth = run(
        qkv_back_kernel,
        "qkv_back",
        6,
        (info, layout, dq, dkv, wa, wb, ra, rb, *tables),
        [smem(), smem()] + [whole()] * 10,
        (shape_of((512, 384), B16), shape_of((256, D), B16), shape_of((256, D), B16)),
        [whole()] * 3,
    )
    ea, eb = run(
        sum_kernel, "plane_sum2", 1, (after(second[0], dqkv), *second[1:]), [whole()] * 8, (one, one), [whole()] * 2
    )

    def stacked(arrays, name):
        n = len(arrays)
        return run(
            functools.partial(stack_kernel, n),
            name,
            1,
            (info, *arrays),
            [smem()] + [whole()] * n,
            (shape_of((n, *flat), B16),),
            [whole()],
        )[0]

    eb_pair = stacked([eb, to_x(eb, 2)], "along_x")
    da = over_pieces(to_tokens(da_own, da_oth, "fold_a"))
    late = run(
        late_grad_kernel,
        "late_grad",
        0.02,
        (info, a, after(dqkv, ea, eb, early, eb_pair, da[1], da[2], da[3]), gain_q, gsum_moe, wa, wb, ra, rb),
        [smem()] + [whole()] * 8,
        (shape_of((16, 112, 128), B16),),
        [whole()],
    )[0]
    grads_in = late
    late = lax.all_to_all(late, PLANE, 0, 0, tiled=True)
    ea = lax.all_gather(ea, ("xh", "z"))
    e_own = [ea, eb_pair] + [to_z(eb_pair, 4 - k) for k in range(1, 4)]
    da[0] = after(da[0], eb_pair)

    ig = run(
        input_back_kernel,
        "input_back",
        0.02,
        (info, dh, *da, x, g1o, g1t, h, both),
        [smem()] + [whole()] * 10,
        (shape_of((128, D), B16),),
        [whole()],
    )[0]


    late = after(late, ig, *e_own[2:])
    grads = run(
        sum_grads_kernel,
        "sum_grads",
        0.02,
        (early, late),
        [whole()] * 2,
        (shape_of((8, 112, 512), B16),),
        [whole()],
    )[0]
    ig_parts = from_each_y(ig)
    e_own[0] = after(e_own[0], grads, ig_parts[0])
    e_own = [v.reshape(-1, 3, OWN, 48, FC) for v in e_own]
    e_oth = [other_core(v) for v in e_own]
    expert_grads = pl.pallas_call(
        assemble_kernel,
        name="assemble",
        grid_spec=pltpu.PrefetchScalarGridSpec(
            num_scalar_prefetch=1,
            grid=(2, OWN),
            in_specs=[
                pl.BlockSpec(
                    (n, 3, 1, 48, FC),
                    (lambda q, e, info: (0, 0, jnp.where(q == 0, e, OWN - 1), 0, 0))
                    if own
                    else (lambda q, e, info: (0, 0, jnp.where(q == 0, 0, e), 0, 0)),
                )
                for own in (True, False)
                for n in (8, 2, 2, 2, 2)
            ],
            out_specs=[
                pl.BlockSpec(
                    (1, *shape), lambda n, e, info: (((info[1] + n) & 1) * OWN + e, 0, 0)
                )
                for shape in ((HALF, FC), (HALF, FC), (FC, HALF))
            ],
        ),
        out_shape=(
            shape_of((EXPERTS, HALF, FC), F32),
            shape_of((EXPERTS, HALF, FC), F32),
            shape_of((EXPERTS, FC, HALF), F32),
        ),
        cost_estimate=cost(0.02),
        compiler_params=pltpu.CompilerParams(vmem_limit_bytes=60 * 2**20),
    )(info, *e_own, *e_oth)
    input_grad, output = run(
        place_kernel,
        "place",
        0.02,
        (info, after(ig, expert_grads[0]), *ig_parts),
        [smem()] + [whole()] * 4,
        (shape_of((256, D), F32), shape_of((256, D), B16)),
        [whole()] * 2,
    )

    grads = lax.all_to_all(
        grads, ("xh", "z"), 0, 0, tiled=True
    )
    grads = after(grads, input_grad)
    grads_t = other_core(grads)
    gsum = grads[:, 96:98, 384:480].astype(F32).transpose(1, 0, 2).reshape(2, HALF)
    gsum = gsum + sum(from_each_y(gsum))
    gsum = gsum + other_core(gsum)

    wq_grad, wk_grad, wv_grad, wo_grad = run(
        finish_kernel,
        "finish",
        0.02,
        (info, grads, after(grads_t, expert_grads[0])),
        [smem()] + [whole()] * 2,
        tuple(shape_of(v, F32) for v in ((HALF, 384), (HALF, 128), (HALF, 128), (384, HALF))),
        [whole()] * 4,
        scratch=[VMEM((HALF, 384), F32)],
    )
    return (
        output,
        input_grad,
        gsum[0] / gain_attn.astype(F32),
        wq_grad,
        wk_grad,
        wv_grad,
        wo_grad,
        gsum[1],
        *expert_grads,
    )


def solution(mesh):
    fine = Mesh(
        mesh.devices.reshape(2, 4, 2, 2, 4), ("shard", "z", "xh", "core", "tensor")
    )
    rows = P(("shard", "z", "xh", "core"), None)
    placed = (
        rows,
        P("shard"),
        P("shard", "tensor"),
        P("shard", "tensor"),
        P("shard", "tensor"),
        P("tensor", "shard"),
        P("shard"),
        P(None, "shard", "tensor"),
        P(None, "shard", "tensor"),
        P(None, "tensor", "shard"),
        rows,
        rows,
        P(),
        rows,
    )
    return jax.shard_map(
        per_device,
        mesh=fine,
        in_specs=placed,
        out_specs=(
            rows,
            rows,
            P("shard"),
            P("shard", "tensor"),
            P("shard", "tensor"),
            P("shard", "tensor"),
            P("tensor", "shard"),
            P("shard"),
            P(None, "shard", "tensor"),
            P(None, "shard", "tensor"),
            P(None, "tensor", "shard"),
        ),
        check_vma=False,
    )
```

```python
import functools

import jax
import jax.numpy as jnp
import numpy as np
from jax import lax
from jax.experimental import pallas as pl
from jax.experimental.pallas import tpu as pltpu
from jax.sharding import Mesh
from jax.sharding import PartitionSpec as P

D = 1536
HALF = 768
HD = 64
EXPERTS = 10
OWN = 5
FC = 128
EPS = 1e-05
SCALE = 0.125
CHUNK = 1024
SEG = 128
ROWS = 3 * SEG
NEG = -1e30
B16 = jnp.bfloat16
F32 = jnp.float32
X = ("shard", "xh")
PLANE = ("shard", "xh", "z")
VMEM = pltpu.VMEM
SMEM = pltpu.SMEM


def nn(a, b):
    return lax.dot_general(a, b, (((1,), (0,)), ((), ())), preferred_element_type=F32)


def nt(a, b):
    return lax.dot_general(a, b, (((1,), (1,)), ((), ())), preferred_element_type=F32)


def tn(a, b):
    return lax.dot_general(a, b, (((0,), (0,)), ((), ())), preferred_element_type=F32)


def x_pairs(k):
    pairs = []
    for sh in range(2):
        for xh in range(2):
            at = (2 * xh + sh + k) % 4
            pairs.append((sh * 2 + xh, (at % 2) * 2 + at // 2))
    return pairs


def to_x(v, k):
    return lax.ppermute(v, X, x_pairs(k))


def other_core(v):
    return lax.ppermute(v, "core", [(0, 1), (1, 0)])


def to_y(v, k):
    return lax.ppermute(v, "tensor", [(i, (i + k) % 4) for i in range(4)])


def to_z(v, k):
    return lax.ppermute(v, "z", [(i, (i + k) % 4) for i in range(4)])


def over_y(v):
    return lax.all_to_all(v, "tensor", 0, 0, tiled=True)


def from_each_y(v):
    return [to_y(v, 4 - k) for k in range(1, 4)]


def after(v, *others):
    return lax.optimization_barrier((v, *others))[0]


def half_of(s):
    return pl.ds(pl.multiple_of(s * HALF, HALF), HALF)


def piece_of(info, k):
    return pl.ds(pl.multiple_of(((info[4] + k) & 3) * 64, 64), 64)


def seg_at(info, layout, slot, blk, j):
    cc = info[1] if blk == 0 else 1 - info[1]
    return layout[(slot * 2 + cc) * 2 + j]


def seg_of(info, layout, blk, j):
    return seg_at(info, layout, info[2] * 2 + info[3], blk, j)


def angle_rows(at, ca, sa, cb, sb):
    ca, sa = ca[pl.ds(at, 1), :], sa[pl.ds(at, 1), :]
    return ca * cb[...] - sa * sb[...], sa * cb[...] + ca * sb[...]


def low_lanes(shape):
    return lax.broadcasted_iota(jnp.int32, shape, 1) < HD


def first_half_of_head(shape):
    return (lax.broadcasted_iota(jnp.int32, shape, 1) & (HD - 1)) < HD // 2


def rope(u, cos, sin):
    turned = jnp.where(
        first_half_of_head(u.shape), -pltpu.roll(u, 96, 1), pltpu.roll(u, 32, 1)
    )
    return u * cos + turned * sin


def unrope(u, cos, sin):
    w = u * sin
    turned = jnp.where(
        first_half_of_head(u.shape), pltpu.roll(w, 96, 1), -pltpu.roll(w, 32, 1)
    )
    return u * cos + turned


def qkv_kernel(
    info, layout, xo, xt, gain_o, gain_t, wa, wb, ra, rb, ca, sa, cb, sb, a_out, q_out, kv_out
):
    s = info[0]
    for blk, ref in enumerate((xo, xt)):
        lo = ref[:, half_of(s)].astype(F32)
        hi = ref[:, half_of(1 - s)].astype(F32)
        mean = (
            jnp.sum(lo * lo, axis=1, keepdims=True) + jnp.sum(hi * hi, axis=1, keepdims=True)
        ) / D
        inv = lax.rsqrt(mean + EPS)
        alo = (lo * inv * gain_o[...].astype(F32)).astype(B16)
        ahi = (hi * inv * gain_t[...].astype(F32)).astype(B16)
        a_out[blk * 256 : blk * 256 + 256, :HALF] = alo
        a_out[blk * 256 : blk * 256 + 256, HALF:] = ahi
        t = (
            nn(alo[:, :384], wa[...])
            + nn(alo[:, 384:], wb[...])
            + nn(ahi[:, :384], ra[...])
            + nn(ahi[:, 384:], rb[...])
        )
        for j in range(2):
            cos, sin = angle_rows(seg_of(info, layout, blk, j), ca, sa, cb, sb)
            tt = t[j * SEG : (j + 1) * SEG]
            low = low_lanes((SEG, SEG))
            t0 = rope(tt[:, :128], cos, sin)
            t1 = rope(tt[:, 128:256], cos, sin)
            t2 = tt[:, 256:]
            rows = slice(blk * 256 + j * SEG, blk * 256 + (j + 1) * SEG)
            zero = jnp.zeros_like(t0)

            def scaled(v):
                return (v.astype(B16).astype(F32) * SCALE).astype(B16)

            q_out[0, rows] = scaled(jnp.where(low, t0, zero))
            q_out[1, rows] = scaled(jnp.where(low, pltpu.roll(t0, HD, 1), zero))
            q_out[2, rows] = scaled(jnp.where(low, t1, zero))
            kv = jnp.where(low, pltpu.roll(t1, HD, 1), t2).astype(B16)
            for slot in range(8):
                kv_out[slot, rows] = kv


def fill_sorted(info, layout, slots, ks, kst):
    for slot in range(8):
        for blk in range(2):
            for j in range(2):
                at = pl.multiple_of(seg_at(info, layout, slot, blk, j) * SEG, SEG)
                part = slots[slot, blk * 256 + j * SEG : blk * 256 + (j + 1) * SEG, :]
                ks[pl.ds(at, SEG), :] = part
                kst[:, pl.ds(at, SEG)] = part.astype(F32).T.astype(B16)


def allowed_keys(j, pos):
    key = j * CHUNK + lax.broadcasted_iota(jnp.int32, (CHUNK, ROWS), 0)
    query = pos * SEG + (lax.broadcasted_iota(jnp.int32, (CHUNK, ROWS), 1) & (SEG - 1))
    return key <= query


def heads_of(q, i):
    return jnp.concatenate([q[h, i * SEG : (i + 1) * SEG, :] for h in range(3)], axis=0)


def attend_kernel(info, layout, q, slots, o_out, o_send, lse_out, ks, kst):
    fill_sorted(info, layout, slots, ks, kst)
    low = low_lanes((SEG, SEG))
    for pair in range(2):
        at_pos = [seg_of(info, layout, pair, n) for n in range(2)]
        qs = [heads_of(q, pair * 2 + n) for n in range(2)]
        full = [lax.div(p, CHUNK // SEG) for p in at_pos]

        def one(j, carry, n, edge):
            top, total, acc = carry
            at = pl.multiple_of(j * CHUNK, CHUNK)
            sc = nt(ks[pl.ds(at, CHUNK), :], qs[n])
            if edge:
                sc = jnp.where(allowed_keys(j, at_pos[n]), sc, NEG)
            new = jnp.maximum(top, jnp.max(sc, axis=0, keepdims=True))
            e = jnp.exp(sc - new)
            back = jnp.exp(top - new)
            total = total * back + jnp.sum(e, axis=0, keepdims=True)
            acc = acc * back + nn(kst[:, pl.ds(at, CHUNK)], e.astype(B16))
            return new, total, acc

        start = (
            jnp.full((1, ROWS), NEG, F32),
            jnp.zeros((1, ROWS), F32),
            jnp.zeros((SEG, ROWS), F32),
        )
        both = jnp.minimum(full[0], full[1])

        def two(j, carry):
            return one(j, carry[0], 0, False), one(j, carry[1], 1, False)

        carry = lax.fori_loop(0, both, two, (start, start))
        rest = [
            lax.fori_loop(both, full[n], lambda j, c, n=n: one(j, c, n, False), carry[n])
            for n in range(2)
        ]
        ends = [one(full[n], rest[n], n, True) for n in range(2)]
        for n in range(2):
            i = pair * 2 + n
            top, total, acc = ends[n]
            lse_out[i] = top + jnp.log(total)
            o = (acc / total).T
            o0, o1, o2 = o[:SEG], o[SEG : 2 * SEG], o[2 * SEG :]
            left = jnp.where(low, pltpu.roll(o0, HD, 1), o1).astype(B16)
            right = jnp.where(low, pltpu.roll(o2, HD, 1), jnp.zeros_like(o2)).astype(B16)
            for out, at in ((o_out, i * SEG),) + (((o_send, (i - 2) * SEG),) if i >= 2 else ()):
                out[at : at + SEG, :SEG] = left
                out[at : at + SEG, SEG:] = right


def attend_back_kernel(
    info, layout, q, do_own, do_oth, o, lse, ca, sa, cb, sb, ks, kst, dq_out, dkv_out, dkv
):
    dkv[...] = jnp.zeros_like(dkv)
    low = low_lanes((SEG, SEG))

    def spread(t0, t1):
        zero = jnp.zeros((SEG, SEG), F32)
        return jnp.concatenate(
            [
                jnp.where(low, zero, pltpu.roll(t0, HD, 1)),
                jnp.where(low, zero, t0),
                jnp.where(low, zero, pltpu.roll(t1, HD, 1)),
            ],
            axis=0,
        )

    for pair in range(2):
        at_pos = [seg_of(info, layout, pair, n) for n in range(2)]
        qs, dos, deltas, lses = [], [], [], []
        do, at = (do_own, 0) if pair == 0 else (do_oth, 256)
        for n in range(2):
            rows = slice((pair * 2 + n) * SEG, (pair * 2 + n + 1) * SEG)
            here = slice(n * SEG, (n + 1) * SEG)
            dof = spread(
                do[here, at : at + SEG].astype(F32), do[here, at + SEG : at + 2 * SEG].astype(F32)
            )
            of = spread(o[rows, :SEG].astype(F32), o[rows, SEG:].astype(F32))
            qs.append(heads_of(q, pair * 2 + n))
            dos.append(dof.astype(B16))
            deltas.append(jnp.sum((dof * of).T, axis=0, keepdims=True))
            lses.append(lse[pair * 2 + n])
        full = [lax.div(p, CHUNK // SEG) for p in at_pos]

        def one(j, acc, n, edge):
            at = pl.multiple_of(j * CHUNK, CHUNK)
            kv = ks[pl.ds(at, CHUNK), :]
            p = jnp.exp(nt(kv, qs[n]) - lses[n])
            if edge:
                p = jnp.where(allowed_keys(j, at_pos[n]), p, 0.0)
            ds = (p * (nt(kv, dos[n]) - deltas[n])).astype(B16)
            return (
                acc + nn(kst[:, pl.ds(at, CHUNK)], ds),
                nn(ds, qs[n]) + nn(p.astype(B16), dos[n]),
            )

        def alone(j, acc, n, edge=False):
            acc, more = one(j, acc, n, edge)
            dkv[pl.ds(pl.multiple_of(j * CHUNK, CHUNK), CHUNK), :] += more
            return acc

        def two(j, accs):
            a0, m0 = one(j, accs[0], 0, False)
            a1, m1 = one(j, accs[1], 1, False)
            dkv[pl.ds(pl.multiple_of(j * CHUNK, CHUNK), CHUNK), :] += m0 + m1
            return a0, a1

        zero = jnp.zeros((SEG, ROWS), F32)
        both = jnp.minimum(full[0], full[1])
        accs = lax.fori_loop(0, both, two, (zero, zero))
        accs = [
            lax.fori_loop(both, full[n], lambda j, c, n=n: alone(j, c, n), accs[n])
            for n in range(2)
        ]
        accs = [alone(full[n], accs[n], n, True) for n in range(2)]
        for n in range(2):
            rows = slice((pair * 2 + n) * SEG, (pair * 2 + n + 1) * SEG)
            dq = accs[n].T * SCALE
            cos, sin = angle_rows(at_pos[n], ca, sa, cb, sb)
            d0, d1, d2 = [unrope(dq[h * SEG : (h + 1) * SEG], cos, sin) for h in range(3)]
            dq_out[rows, :SEG] = jnp.where(low, d0, pltpu.roll(d1, HD, 1)).astype(B16)
            dq_out[rows, SEG:] = jnp.where(low, d2, jnp.zeros_like(d2)).astype(B16)
    for slot in range(8):
        for blk in range(2):
            for j in range(2):
                at = pl.multiple_of(seg_at(info, layout, slot, blk, j) * SEG, SEG)
                dkv_out[slot, blk * 256 + j * SEG : blk * 256 + (j + 1) * SEG, :] = dkv[
                    pl.ds(at, SEG), :
                ].astype(B16)


def token_kernel(info, x, o, w_own, w_oth, gain_o, gain_t, h_out, b_out):
    s = info[0]
    here = piece_of(info, 0)
    alo = jnp.zeros((64, HALF), F32)
    ahi = jnp.zeros((64, HALF), F32)
    for y in range(4):
        for part, w in ((o[y, :, :192], w_own), (o[y, :, 256:448], w_oth)):
            alo += nn(part, w[y, 0])
            ahi += nn(part, w[y, 1])
    lo = x[here, half_of(s)].astype(F32) + alo
    hi = x[here, half_of(1 - s)].astype(F32) + ahi
    mean = (
        jnp.sum(lo * lo, axis=1, keepdims=True) + jnp.sum(hi * hi, axis=1, keepdims=True)
    ) / D
    inv = lax.rsqrt(mean + EPS)
    h_out[:, :HALF] = lo
    h_out[:, HALF:] = hi
    blo = (lo * inv * gain_o[...].astype(F32)).astype(B16)
    bhi = (hi * inv * gain_t[...].astype(F32)).astype(B16)
    b_out[:, :HALF] = blo
    b_out[:, HALF:] = bhi


def norm_back(grads, sources, gains):
    mean = sum(jnp.sum(v * v, axis=1, keepdims=True) for v in sources) / D
    inv = lax.rsqrt(mean + EPS)
    weighted = [d * g for d, g in zip(grads, gains)]
    dot = sum(jnp.sum(w * v, axis=1, keepdims=True) for w, v in zip(weighted, sources)) / D
    cube = inv * inv * inv * dot
    return (
        [inv * w - v * cube for w, v in zip(weighted, sources)],
        [jnp.sum(d * v * inv, axis=0, keepdims=True) for d, v in zip(grads, sources)],
    )


def fold_kernel(info, own, received, out0, out1, out2, out3, *rest):
    for k, out in enumerate((out0, out1, out2, out3)):
        rows = piece_of(info, k)
        out[...] = (own[rows].astype(F32) + received[rows].astype(F32)).astype(out.dtype)
    if rest:
        total = own[256:].astype(F32) + received[256:].astype(F32)
        rest[0][...] = total.astype(B16).reshape(4, 64, D)


def token_back_kernel(
    info, h, d0, d1, d2, d3, moe, g, w_own, w_oth, gain_o, gain_t, dh_out, both_out, do_out, gain_out
):
    s = info[0]
    here = piece_of(info, 0)
    total = sum(d[...].astype(F32) for d in (d0, d1, d2, d3))
    halves = (slice(0, HALF), slice(HALF, D))
    back, gsum = norm_back(
        [total[:, k] for k in halves],
        [h[:, k] for k in halves],
        [gain_o[...].astype(F32), gain_t[...].astype(F32)],
    )
    for k, part, sums, half in zip(halves, back, gsum, (s, 1 - s)):
        dh = g[here, half_of(half)].astype(F32) + part
        dh_out[:, k] = dh
        for y in range(4):
            both_out[y, :64, k] = dh.astype(B16)
            both_out[y, 64:, k] = moe[y, :, k]
        gain_out[:, k] = sums
    dattn = both_out[0, :64]
    pad = jnp.zeros((64, 64), B16)
    for y in range(4):
        for at, w in ((0, w_own), (256, w_oth)):
            do = nt(dattn[:, :HALF], w[y, 0]) + nt(dattn[:, HALF:], w[y, 1])
            do_out[y, :, at : at + 192] = do.astype(B16)
            do_out[y, :, at + 192 : at + 256] = pad


def input_back_kernel(info, dh, d0, d1, d2, d3, x, gain_o, gain_t, h, both, out):
    s = info[0]
    here = piece_of(info, 0)
    total = sum(d[...].astype(F32) for d in (d0, d1, d2, d3))
    halves = (slice(0, HALF), slice(HALF, D))
    back, _ = norm_back(
        [total[:, k] for k in halves],
        [x[here, half_of(half)].astype(F32) for half in (s, 1 - s)],
        [gain_o[...].astype(F32), gain_t[...].astype(F32)],
    )
    for k, part in zip(halves, back):
        out[:64, k] = (dh[:, k] + part).astype(B16)
    out[64:] = (h[...] + sum(both[y, 64:].astype(F32) for y in range(4))).astype(B16)


def place_kernel(info, p0, p1, p2, p3, grad, y):
    s = info[0]
    for k, p in enumerate((p0, p1, p2, p3)):
        for n, out in enumerate((grad, y)):
            rows = slice(n * 64, (n + 1) * 64)
            out[piece_of(info, k), half_of(s)] = p[rows, :HALF].astype(out.dtype)
            out[piece_of(info, k), half_of(1 - s)] = p[rows, HALF:].astype(out.dtype)


def qkv_back_kernel(
    info, layout, dq, dkv, wa, wb, ra, rb, ca, sa, cb, sb, d_out, da_own, da_oth
):
    for i in range(4):
        rows = slice(i * SEG, (i + 1) * SEG)
        total = sum(dkv[r, rows].astype(F32) for r in range(8))
        cos, sin = angle_rows(seg_of(info, layout, i // 2, i % 2), ca, sa, cb, sb)
        low = low_lanes((SEG, SEG))
        dk = unrope(total, cos, sin)
        d_out[rows, :SEG] = dq[rows, :SEG]
        d_out[rows, SEG : 2 * SEG] = jnp.where(
            low, dq[rows, SEG:].astype(F32), pltpu.roll(dk, HD, 1)
        ).astype(B16)
        d_out[rows, 2 * SEG :] = jnp.where(low, jnp.zeros_like(total), total).astype(B16)
    for n, out in enumerate((da_own, da_oth)):
        d = d_out[n * 256 : (n + 1) * 256, :]
        for m, w in enumerate((wa, wb, ra, rb)):
            out[:, m * 384 : (m + 1) * 384] = nt(d, w[...]).astype(B16)


def early_grad_kernel(info, a, dq, own, oth, o, wa, wb, ra, rb, out, along_out):
    s = info[0]
    low = low_lanes((384, SEG))
    for m, w in enumerate((wa, wb, ra, rb)):
        k = slice(m * 384, (m + 1) * 384)
        dw = tn(a[:, k], dq[...])
        dwo = jnp.zeros((384, 256), F32)
        for n, both in enumerate((own, oth)):
            for y in range(4):
                at = n * 256 + y * 64
                dwo += tn(both[y, :64, k], o[at : at + 64])
        along = dw[:, :SEG] * w[:, :SEG].astype(F32)
        along += jnp.where(low, dw[:, SEG:] * w[:, SEG : 2 * SEG].astype(F32), 0.0)
        along_out[:, k] = jnp.sum(along.T, axis=0, keepdims=True)
        last = jnp.where(low, dw[:, SEG:], pltpu.roll(dwo[:, SEG:], HD, 1))
        sh = (s + m // 2) & 1
        for z in range(4):
            at = sh * 8 + (m % 2) * 4 + z
            part = slice(z * 96, (z + 1) * 96)
            out[at, :, :SEG] = dw[part, :SEG].astype(B16)
            out[at, :, SEG : 2 * SEG] = last[part].astype(B16)
            out[at, :, 2 * SEG :] = dwo[part, :SEG].astype(B16)


def late_grad_kernel(info, a, dqkv, gain_q, gain_moe, wa, wb, ra, rb, out):
    s = info[0]
    low = low_lanes((512, SEG))
    low_w = low_lanes((384, SEG))

    def joined(low, v):
        return jnp.where(low, pltpu.roll(v[:, SEG : 2 * SEG].astype(F32), HD, 1), v[:, 2 * SEG :].astype(F32))

    d = joined(low, dqkv[...]).astype(B16)
    row = lax.broadcasted_iota(jnp.int32, (16, SEG), 0)
    for m, w in enumerate((wa, wb, ra, rb)):
        k = slice(m * 384, (m + 1) * 384)
        dw = tn(a[:, k], d)
        gain = jnp.sum((dw * joined(low_w, w[...])).T, axis=0, keepdims=True) + gain_q[:, k]
        moe = gain_moe[:, k]
        sh = (s + m // 2) & 1
        for z in range(4):
            at = sh * 8 + (m % 2) * 4 + z
            part = slice(z * 96, (z + 1) * 96)
            out[at, :96] = dw[part].astype(B16)
            pad = jnp.zeros((1, 32), F32)
            g0 = jnp.concatenate([gain[:, part], pad], axis=1)
            g1 = jnp.concatenate([moe[:, part], pad], axis=1)
            out[at, 96:] = jnp.where(row == 0, g0, jnp.where(row == 1, g1, 0.0)).astype(B16)


def lift_kernel(info, g_own, g_oth, d_own, d_ra, d_rb, out, g_out):
    s = info[0]
    hi = jnp.concatenate([d_ra[0], d_rb[0]], axis=0)

    @pl.when(pl.program_id(0) == 0)
    def _():
        for n, g in enumerate((g_own, g_oth)):
            rows = slice(n * 256, (n + 1) * 256)
            g_out[rows, :HALF] = g[:, half_of(s)]
            g_out[rows, HALF:] = g[:, half_of(1 - s)]

    out[0] = nt(g_out[:, :HALF], d_own[0]) + nt(g_out[:, HALF:], hi)


def expert_kernel(
    info, b0, b1, b2, b3, b4, b5, b6, b7, w, gd, g_own, g_oth, u_own, u_oth, d_own, d_ra, d_rb,
    out_own, out_oth, hw_out, dgu_out, b, wlo, whi, dlo, dhi, dall, hall,
):
    e = pl.program_id(0)
    lo = jnp.concatenate([g_own[0], u_own[0]], axis=1)
    hi = jnp.concatenate([g_oth[0], u_oth[0]], axis=1)
    pair = pl.ds(pl.multiple_of(e * 2 * FC, 2 * FC), 2 * FC)
    one = pl.ds(pl.multiple_of(e * FC, FC), FC)
    wlo[:, pair] = lo
    whi[:, pair] = hi
    dlo[one] = d_own[0]
    dhi[one] = jnp.concatenate([d_ra[0], d_rb[0]], axis=0)

    @pl.when(e == 0)
    def _():
        for n, ref in enumerate((b0, b1, b2, b3, b4, b5, b6, b7)):
            at = (n // 4) * 256 + ((info[4] + n) & 3) * 64
            b[pl.ds(pl.multiple_of(at, 64), 64)] = ref[...]

    for k in range(2):
        rows = slice(k * 256, (k + 1) * 256)
        gu = nn(b[rows, :HALF], lo) + nn(b[rows, HALF:], hi)
        gate, up = gu[:, :FC], gu[:, FC:]
        sg = jax.nn.sigmoid(gate)
        silu = gate * sg
        here = lax.broadcasted_iota(jnp.int32, (256, OWN), 1) == e
        weight = jnp.sum(jnp.where(here, w[rows], 0.0), axis=1, keepdims=True)
        hw = (silu * up * weight).astype(B16)
        hw_out[0, rows] = hw
        hall[rows, one] = hw
        dh = gd[0, rows] * weight
        dgate = (dh * up * sg * (1.0 + gate * (1.0 - sg))).astype(B16)
        dup = (dh * silu).astype(B16)
        d = jnp.concatenate([dgate, dup], axis=1)
        dgu_out[0, rows] = d
        dall[rows, pair] = d

    @pl.when(e == OWN - 1)
    def _():
        for n, out in enumerate((out_own, out_oth)):
            rows = slice(n * 256, (n + 1) * 256)
            for k in range(6):
                c2 = slice(k * 256, (k + 1) * 256)
                if k < 3:
                    out[:256, c2] = nt(dall[rows], wlo[c2]).astype(B16)
                    out[256:, c2] = nn(hall[rows], dlo[:, c2]).astype(B16)
                else:
                    c1 = slice((k - 3) * 256, (k - 2) * 256)
                    out[:256, c2] = nt(dall[rows], whi[c1]).astype(B16)
                    out[256:, c2] = nn(hall[rows], dhi[:, c1]).astype(B16)


def expert_grad_kernel(info, b, g, hw, dgu, *refs):
    by_x, by_z, dws, dds = refs[:5], refs[5:10], refs[10], refs[11]
    at_x = 2 * info[3] + info[0]

    def put(refs, step, k, kind, value):
        if step == 2:
            refs[2 + k // 2][k % 2, kind, 0] = value
        else:
            refs[{0: 0, 1: 1, 3: 4}[step]][k, kind, 0] = value

    for half in range(2):
        k = slice(half * HALF, (half + 1) * HALF)
        dws[...] = tn(b[:, k], dgu[0]).astype(B16)
        dds[...] = tn(hw[0], g[:, k]).astype(B16)
        for step in (half, half + 2):
            xq = ((at_x + step) & 3) >> 1
            for dz in range(4):
                at = xq * 4 + ((info[2] + dz) & 3)
                for kind in range(3):
                    if kind < 2:
                        piece = dws[
                            pl.ds(pl.multiple_of(at * 96, 32), 96), kind * FC : (kind + 1) * FC
                        ]
                    else:
                        part = dds[pl.ds(pl.multiple_of(at * 16, 16), 16), :]
                        piece = jnp.concatenate(
                            [part[:, l * FC : (l + 1) * FC] for l in range(6)], axis=0
                        )
                    put(by_x, step, dz, kind, piece[:48])
                    put(by_z, dz, step, kind, piece[48:])


def pass_on_kernel(*refs):
    for n in (0, 4):
        up, down, got_up, got_down = refs[n : n + 4]
        out_up, out_down = refs[8 + n // 2], refs[9 + n // 2]
        out_up[:2] = (up[:2].astype(F32) + got_up[...].astype(F32)).astype(B16)
        out_up[2:] = up[2:]
        out_down[:2] = down[:2]
        out_down[2:] = (down[2:].astype(F32) + got_down[...].astype(F32)).astype(B16)


def gather_sum_kernel(*refs):
    for n in (0, 3):
        outs = refs[6 + n // 3 * 4 : 10 + n // 3 * 4]
        for k, out in enumerate(outs):
            out[...] = sum(p[k].astype(F32) for p in refs[n : n + 3]).astype(out.dtype)


def sum_kernel(*refs):
    for n in range(2):
        refs[8 + n][...] = sum(p[...].astype(F32) for p in refs[n * 4 : n * 4 + 4]).astype(B16)


def stack_kernel(n, info, *refs):
    at = info[2] if n == 4 else info[3]
    for k, ref in enumerate(refs[:-1]):
        refs[-1][(at + k) & (n - 1)] = ref[...]


def assemble_kernel(info, *refs):
    gate, up, down = refs[10:]

    def write(everywhere, *by_z):
        def place(v, n, xh, z, part):
            at = xh * 4 + z
            rows = pl.ds(pl.multiple_of(at * 96 + part * 48, 16), 48)
            gate[0, rows] = v[n, 0, 0].astype(F32)
            up[0, rows] = v[n, 1, 0].astype(F32)
            rows = pl.ds(pl.multiple_of(at * 16, 16), 16)
            for l in range(3):
                down[0, rows, (part * 3 + l) * FC : (part * 3 + l + 1) * FC] = v[
                    n, 2, 0, l * 16 : (l + 1) * 16
                ].astype(F32)

        for n in range(8):
            place(everywhere, n, n // 4, n % 4, 0)
        for k, v in enumerate(by_z):
            for xh in range(2):
                place(v, xh, xh, (info[2] + k) & 3, 1)

    @pl.when(pl.program_id(0) == 0)
    def _():
        write(*refs[:5])

    @pl.when(pl.program_id(0) == 1)
    def _():
        write(*refs[5:10])


def sum_grads_kernel(early, late, out):
    first = sum(early[n].astype(F32) for n in range(16)).astype(B16)
    second = sum(late[n].astype(F32) for n in range(16)).astype(B16)
    for n in range(8):
        out[n, :96, : 3 * SEG] = first
        out[n, 96:, : 3 * SEG] = jnp.zeros((16, 3 * SEG), B16)
        out[n, :, 3 * SEG :] = second


def finish_kernel(info, own, oth, wq, wk, wv, wo_out, wo):
    first = info[1] == 0
    low = low_lanes((96, SEG))
    for at in range(8):
        rows = slice(at * 96, (at + 1) * 96)
        a, b = own[at, :96].astype(F32), oth[at, :96].astype(F32)
        a, b = jnp.where(first, a, b), jnp.where(first, b, a)
        a = [a[:, n * SEG : (n + 1) * SEG] for n in range(4)]
        b = [b[:, n * SEG : (n + 1) * SEG] for n in range(4)]
        at_turn = [pltpu.roll(v, HD, 1) for v in a]
        turned = [pltpu.roll(v, HD, 1) for v in b]
        wq[rows, :SEG] = a[0]
        wq[rows, SEG : 2 * SEG] = jnp.where(low, a[1], turned[0])
        wq[rows, 2 * SEG :] = jnp.where(low, turned[0], turned[1])
        wk[rows] = jnp.where(low, a[3], turned[3])
        wv[rows] = jnp.where(low, at_turn[3], b[3])
        wo[rows, :SEG] = a[2]
        wo[rows, SEG : 2 * SEG] = jnp.where(low, at_turn[1], turned[2])
        wo[rows, 2 * SEG :] = jnp.where(low, turned[2], b[1])
    wo_out[...] = wo[...].T


def smem():
    return pl.BlockSpec(memory_space=SMEM)


def whole():
    return None


def each(*shape):
    return pl.BlockSpec((1, *shape), lambda e: (e,) + (0,) * len(shape))


def fixed(*shape):
    return pl.BlockSpec(shape, lambda e: (0,) * len(shape))


def shape_of(shape, dtype):
    return jax.ShapeDtypeStruct(shape, dtype)


def cost(us):
    return pl.CostEstimate(flops=int(us * 3.3e9), bytes_accessed=int(us * 1e7), transcendentals=0)


def run(kernel, name, us, ins, in_specs, outs, out_specs, scratch=(), grid=(1,), mib=60):
    def block(spec, v):
        return fixed(*v.shape) if spec is None else spec

    return pl.pallas_call(
        kernel,
        name=name,
        grid=grid,
        in_specs=[block(spec, v) for spec, v in zip(in_specs, ins, strict=True)],
        out_specs=[block(spec, v) for spec, v in zip(out_specs, outs, strict=True)],
        out_shape=outs,
        scratch_shapes=list(scratch),
        cost_estimate=cost(us),
        compiler_params=pltpu.CompilerParams(vmem_limit_bytes=mib * 2**20),
    )(*ins)


def angle_tables():
    freq = 10000.0 ** (-np.arange(0, HD, 2) / HD)
    freq = np.tile(freq, 4)[None, :]
    coarse = np.arange(32)[:, None] * SEG * freq
    fine = np.arange(SEG)[:, None] * freq
    return tuple(
        jnp.asarray(v.astype(np.float32))
        for v in (np.cos(coarse), np.sin(coarse), np.cos(fine), np.sin(fine))
    )


def per_device(
    x,
    gain_attn,
    w_query,
    w_key,
    w_value,
    w_out,
    gain_moe,
    expert_gate,
    expert_up,
    expert_down,
    routes,
    route_gates,
    layout,
    g,
):
    s = lax.axis_index("shard")
    c = lax.axis_index("core")
    info = jnp.stack(
        [s, c, lax.axis_index("z"), lax.axis_index("xh"), lax.axis_index("tensor")]
    ).astype(jnp.int32)
    first = c == 0
    tables = angle_tables()

    def mine(v, axis):
        width = v.shape[axis] // 2
        return jnp.where(
            first,
            lax.slice_in_dim(v, 0, width, axis=axis),
            lax.slice_in_dim(v, width, 2 * width, axis=axis),
        )

    def both_cores(own, oth, axis):
        return jnp.where(
            first, jnp.concatenate([own, oth], axis), jnp.concatenate([oth, own], axis)
        )

    packed = jnp.concatenate(
        [mine(w_query, 1), mine(w_key, 1), jnp.zeros((HALF, HD), B16), mine(w_value, 1)], axis=1
    )
    wa, wb = packed[:384], packed[384:]
    ra, rb = to_x(wa, 1), to_x(wb, -1)
    x_t = other_core(x)
    wo = mine(after(w_out, wa, wb), 0)
    wo_up, wo_down = to_x(wo[:96], 1), to_x(wo[96:], -1)
    gains = jnp.stack([gain_attn, gain_moe])
    gains_t = to_x(gains, 1)
    g1o, g1t, g2o, g2t = gains[0:1], gains_t[0:1], gains[1:2], gains_t[1:2]
    a, q, kv = run(
        qkv_kernel,
        "qkv",
        0.02,
        (info, layout, x, x_t, g1o, g1t, wa, wb, ra, rb, *tables),
        [smem(), smem()] + [whole()] * 12,
        (shape_of((512, D), B16), shape_of((3, 512, 128), B16), shape_of((8, 512, 128), B16)),
        [whole()] * 3,
    )
    slots = lax.all_to_all(kv, ("z", "xh"), 0, 0, tiled=True)
    wo, wo_up, wo_down, _ = lax.optimization_barrier((wo, wo_up, wo_down, kv))
    wo_both = jnp.stack([wo, jnp.concatenate([wo_up, wo_down], axis=0)])
    wo_own = lax.all_gather(wo_both, "tensor")
    down_c = lax.dynamic_slice_in_dim(after(expert_down, kv), c * OWN, OWN, 0)
    gate_c = lax.dynamic_slice_in_dim(after(expert_gate, kv), c * OWN, OWN, 0)
    up_c = lax.dynamic_slice_in_dim(after(expert_up, kv), c * OWN, OWN, 0)
    down_a, down_b = down_c[:, :64], down_c[:, 64:]
    down_ra, down_rb = to_x(down_a, 1), to_x(down_b, -1)
    gate_t, up_t = to_x(gate_c, 1), to_x(up_c, -1)
    g_t = other_core(after(g, kv))
    ids = jnp.arange(EXPERTS, dtype=jnp.int32)
    share = jnp.sum(
        jnp.where(routes[:, :, None] == ids[None, None, :], route_gates[:, :, None], 0.0), axis=1
    )
    share = after(share, kv)
    share = jnp.concatenate([share, other_core(share)], axis=0)
    share = jnp.where(first, share[:, :OWN], share[:, OWN:])
    o, o_send, lse, ks, kst = run(
        attend_kernel,
        "attend",
        14,
        (info, layout, after(q, share, g_t, gate_c, up_c, down_c, down_a, down_b), slots),
        [smem(), smem()] + [whole()] * 2,
        (
            shape_of((512, 256), B16),
            shape_of((256, 256), B16),
            shape_of((4, 1, ROWS), F32),
            shape_of((4096, 128), B16),
            shape_of((128, 4096), B16),
        ),
        [whole()] * 5,
    )
    o_send = after(o_send, gate_t, up_t)
    o_got = other_core(o_send)
    wo_oth = other_core(after(wo_own, o_got))
    o_all = jnp.concatenate([o[:256], o_got], axis=1)
    o_tok = over_y(o_all.reshape(4, 64, 512))
    h, b64 = run(
        token_kernel,
        "token",
        0.02,
        (info, x, o_tok, wo_own, wo_oth, g2o, g2t),
        [smem()] + [whole()] * 6,
        (shape_of((64, D), F32), shape_of((64, D), B16)),
        [whole()] * 2,
    )
    lifted, g_roll = run(
        lift_kernel,
        "lift",
        6,
        (info, after(g, b64), g_t, down_c, down_ra, down_rb),
        [smem(), fixed(256, D), fixed(256, D), each(FC, HALF), each(64, HALF), each(64, HALF)],
        (shape_of((OWN, 512, FC), F32), shape_of((512, D), B16)),
        [each(512, FC), fixed(512, D)],
        grid=(OWN,),
    )
    b_own = [b64, *from_each_y(b64)]
    b_own = b_own[:1] + [after(v, lifted) for v in b_own[1:]]
    b_oth = [other_core(v) for v in b_own]
    out_own, out_oth, hw, dgu, b = run(
        expert_kernel,
        "expert",
        0.02,
        (info, *b_own, *b_oth, share, lifted, gate_c, gate_t, up_c, up_t, down_c, down_ra, down_rb),
        [smem()]
        + [whole()] * 9
        + [each(512, FC)]
        + [each(HALF, FC)] * 4
        + [each(FC, HALF), each(64, HALF), each(64, HALF)],
        (
            shape_of((512, D), B16),
            shape_of((512, D), B16),
            shape_of((OWN, 512, FC), B16),
            shape_of((OWN, 512, 2 * FC), B16),
            shape_of((512, D), B16),
        ),
        [whole(), whole(), each(512, FC), each(512, 2 * FC), whole()],
        scratch=[
            VMEM((HALF, 2 * FC * OWN), B16),
            VMEM((HALF, 2 * FC * OWN), B16),
            VMEM((FC * OWN, HALF), B16),
            VMEM((FC * OWN, HALF), B16),
            VMEM((512, 2 * FC * OWN), B16),
            VMEM((512, FC * OWN), B16),
        ],
        grid=(OWN,),
    )

    def to_tokens(own, oth, name):
        outs = (shape_of((64, D), F32),) + (shape_of((64, D), B16),) * 3
        if own.shape[0] > 256:
            outs += (shape_of((4, 64, D), B16),)
        return run(
            fold_kernel,
            name,
            2,
            (info, own, other_core(oth)),
            [smem()] + [whole()] * 2,
            outs,
            [whole()] * len(outs),
        )

    def over_pieces(parts):
        return [parts[0]] + [to_y(parts[k], k) for k in range(1, 4)]

    *db, moe = to_tokens(out_own, out_oth, "fold_b")
    halves = shape_of((2, 3, OWN, 48, FC), B16)
    quarter = shape_of((4, 3, OWN, 48, FC), B16)

    def by_expert(n):
        return pl.BlockSpec((n, 3, 1, 48, FC), lambda e: (0, 0, e, 0, 0))

    sent = run(
        expert_grad_kernel,
        "expert_grad",
        9,
        (info, after(b, db[1]), g_roll, hw, dgu),
        [smem(), fixed(512, D), fixed(512, D), each(512, FC), each(512, 2 * FC)],
        (quarter, quarter, halves, halves, quarter) * 2,
        [by_expert(4), by_expert(4), by_expert(2), by_expert(2), by_expert(4)] * 2,
        scratch=[VMEM((HALF, 2 * FC), B16), VMEM((FC, HALF), B16)],
        grid=(OWN,),
    )
    flat = (3 * OWN * 48, FC)
    sent = [v.reshape(-1, *flat) for v in sent]
    xs, zs = sent[:5], sent[5:]
    db = over_pieces(db)
    db[0] = after(db[0], *sent)
    dh, both, do_tok, gsum_moe = run(
        token_back_kernel,
        "token_back",
        0.02,
        (info, h, *db, moe, g, wo_own, wo_oth, g2o, g2t),
        [smem()] + [whole()] * 11,
        (
            shape_of((64, D), F32),
            shape_of((4, 128, D), B16),
            shape_of((4, 64, 512), B16),
            shape_of((1, D), F32),
        ),
        [whole()] * 4,
    )
    xs[2], xs[3], zs[2], zs[3], _ = lax.optimization_barrier((xs[2], xs[3], zs[2], zs[3], dh))
    passing = (to_x(xs[2], 1), to_x(xs[3], -1), to_z(zs[2], 1), to_z(zs[3], -1))
    do = over_y(do_tok).reshape(256, 512)
    do_oth = other_core(do)
    four = shape_of((4, *flat), B16)
    x_up, x_down, z_up, z_down = run(
        pass_on_kernel,
        "pass_on",
        0.02,
        (xs[1], xs[4], *passing[:2], zs[1], zs[4], *passing[2:]),
        [whole()] * 8,
        (four,) * 4,
        [whole()] * 4,
    )
    got = (to_x(x_up, 1), to_x(x_down, -1), to_z(z_up, 1), to_z(z_down, -1))

    do = after(do, x_up)
    both = over_y(after(both, do))
    dq, dkv = run(
        attend_back_kernel,
        "attend_back",
        16,
        (info, layout, q, do, do_oth, o, lse, *tables, ks, kst),
        [smem(), smem()] + [whole()] * 11,
        (shape_of((512, 256), B16), shape_of((8, 512, 128), B16)),
        [whole()] * 2,
        scratch=[VMEM((4096, 128), F32)],
    )
    dkv = lax.all_to_all(after(dkv, *got, both), ("z", "xh"), 0, 0, tiled=True)

    one, one32 = shape_of(flat, B16), shape_of(flat, F32)
    xz = run(
        gather_sum_kernel,
        "plane_sum",
        0.02,
        (after(xs[0], dq), *got[:2], zs[0], *got[2:]),
        [whole()] * 6,
        (one32, one, one, one) * 2,
        [whole()] * 8,
    )
    both_oth = other_core(after(both, xz[1]))
    early, gain_q = run(
        early_grad_kernel,
        "early_grad",
        1,
        (info, a, after(dq, xz[1]), both, both_oth, o, wa, wb, ra, rb),
        [smem()] + [whole()] * 9,
        (shape_of((16, 96, 384), B16), shape_of((1, D), F32)),
        [whole()] * 2,
    )
    xz = list(xz)
    xz[2], xz[6], _ = lax.optimization_barrier((xz[2], xz[6], gain_q))
    second = [xz[0]] + [to_z(xz[k], k) for k in range(1, 4)]
    second += [xz[4]] + [to_x(xz[4 + k], k) for k in range(1, 4)]
    early = lax.all_to_all(after(early, dkv), PLANE, 0, 0, tiled=True)
    dkv = after(dkv, gain_q)
    dqkv, da_own, da_oth = run(
        qkv_back_kernel,
        "qkv_back",
        6,
        (info, layout, dq, dkv, wa, wb, ra, rb, *tables),
        [smem(), smem()] + [whole()] * 10,
        (shape_of((512, 384), B16), shape_of((256, D), B16), shape_of((256, D), B16)),
        [whole()] * 3,
    )
    ea, eb = run(
        sum_kernel, "plane_sum2", 1, (after(second[0], dqkv), *second[1:]), [whole()] * 8, (one, one), [whole()] * 2
    )

    def stacked(arrays, name):
        n = len(arrays)
        return run(
            functools.partial(stack_kernel, n),
            name,
            1,
            (info, *arrays),
            [smem()] + [whole()] * n,
            (shape_of((n, *flat), B16),),
            [whole()],
        )[0]

    eb_pair = stacked([eb, to_x(eb, 2)], "along_x")
    da = over_pieces(to_tokens(da_own, da_oth, "fold_a"))
    late = run(
        late_grad_kernel,
        "late_grad",
        0.02,
        (info, a, after(dqkv, ea, eb, early, eb_pair, da[1], da[2], da[3]), gain_q, gsum_moe, wa, wb, ra, rb),
        [smem()] + [whole()] * 8,
        (shape_of((16, 112, 128), B16),),
        [whole()],
    )[0]
    grads_in = late
    late = lax.all_to_all(late, PLANE, 0, 0, tiled=True)
    ea = lax.all_gather(ea, ("xh", "z"))
    e_own = [ea, eb_pair] + [to_z(eb_pair, 4 - k) for k in range(1, 4)]
    da[0] = after(da[0], eb_pair)

    ig = run(
        input_back_kernel,
        "input_back",
        0.02,
        (info, dh, *da, x, g1o, g1t, h, both),
        [smem()] + [whole()] * 10,
        (shape_of((128, D), B16),),
        [whole()],
    )[0]


    late = after(late, ig, *e_own[2:])
    grads = run(
        sum_grads_kernel,
        "sum_grads",
        0.02,
        (early, late),
        [whole()] * 2,
        (shape_of((8, 112, 512), B16),),
        [whole()],
    )[0]
    ig_parts = from_each_y(ig)
    e_own[0] = after(e_own[0], grads, ig_parts[0])
    e_own = [v.reshape(-1, 3, OWN, 48, FC) for v in e_own]
    e_oth = [other_core(v) for v in e_own]
    expert_grads = pl.pallas_call(
        assemble_kernel,
        name="assemble",
        grid_spec=pltpu.PrefetchScalarGridSpec(
            num_scalar_prefetch=1,
            grid=(2, OWN),
            in_specs=[
                pl.BlockSpec(
                    (n, 3, 1, 48, FC),
                    (lambda q, e, info: (0, 0, jnp.where(q == 0, e, OWN - 1), 0, 0))
                    if own
                    else (lambda q, e, info: (0, 0, jnp.where(q == 0, 0, e), 0, 0)),
                )
                for own in (True, False)
                for n in (8, 2, 2, 2, 2)
            ],
            out_specs=[
                pl.BlockSpec(
                    (1, *shape), lambda n, e, info: (((info[1] + n) & 1) * OWN + e, 0, 0)
                )
                for shape in ((HALF, FC), (HALF, FC), (FC, HALF))
            ],
        ),
        out_shape=(
            shape_of((EXPERTS, HALF, FC), F32),
            shape_of((EXPERTS, HALF, FC), F32),
            shape_of((EXPERTS, FC, HALF), F32),
        ),
        cost_estimate=cost(0.02),
        compiler_params=pltpu.CompilerParams(vmem_limit_bytes=60 * 2**20),
    )(info, *e_own, *e_oth)
    input_grad, output = run(
        place_kernel,
        "place",
        0.02,
        (info, after(ig, expert_grads[0]), *ig_parts),
        [smem()] + [whole()] * 4,
        (shape_of((256, D), F32), shape_of((256, D), B16)),
        [whole()] * 2,
    )

    grads = lax.all_to_all(
        grads, ("xh", "z"), 0, 0, tiled=True
    )
    grads = after(grads, input_grad)
    grads_t = other_core(grads)
    gsum = grads[:, 96:, 3 * SEG :].astype(F32) + grads_t[:, 96:, 3 * SEG :].astype(F32)
    parts = [gsum, *from_each_y(gsum)]
    wq_grad, wk_grad, wv_grad, wo_grad = run(
        finish_kernel,
        "finish",
        0.02,
        (info, grads, after(grads_t, expert_grads[0])),
        [smem()] + [whole()] * 2,
        tuple(shape_of(v, F32) for v in ((HALF, 384), (HALF, 128), (HALF, 128), (384, HALF))),
        [whole()] * 4,
        scratch=[VMEM((HALF, 384), F32)],
    )
    gsum = sum(parts)[:, :2, :96].transpose(1, 0, 2).reshape(2, HALF)
    return (
        output,
        input_grad,
        gsum[0] / gain_attn.astype(F32),
        wq_grad,
        wk_grad,
        wv_grad,
        wo_grad,
        gsum[1],
        *expert_grads,
    )


def solution(mesh):
    fine = Mesh(
        mesh.devices.reshape(2, 4, 2, 2, 4), ("shard", "z", "xh", "core", "tensor")
    )
    rows = P(("shard", "z", "xh", "core"), None)
    placed = (
        rows,
        P("shard"),
        P("shard", "tensor"),
        P("shard", "tensor"),
        P("shard", "tensor"),
        P("tensor", "shard"),
        P("shard"),
        P(None, "shard", "tensor"),
        P(None, "shard", "tensor"),
        P(None, "tensor", "shard"),
        rows,
        rows,
        P(),
        rows,
    )
    return jax.shard_map(
        per_device,
        mesh=fine,
        in_specs=placed,
        out_specs=(
            rows,
            rows,
            P("shard"),
            P("shard", "tensor"),
            P("shard", "tensor"),
            P("shard", "tensor"),
            P("tensor", "shard"),
            P("shard"),
            P(None, "shard", "tensor"),
            P(None, "shard", "tensor"),
            P(None, "tensor", "shard"),
        ),
        check_vma=False,
    )
```

```python
import functools

import jax
import jax.numpy as jnp
import numpy as np
from jax import lax
from jax.experimental import pallas as pl
from jax.experimental.pallas import tpu as pltpu
from jax.sharding import Mesh
from jax.sharding import PartitionSpec as P

D = 1536
HALF = 768
HD = 64
EXPERTS = 10
OWN = 5
FC = 128
EPS = 1e-05
SCALE = 0.125
CHUNK = 1024
SEG = 128
ROWS = 3 * SEG
NEG = -1e30
B16 = jnp.bfloat16
F32 = jnp.float32
X = ("shard", "xh")
PLANE = ("shard", "xh", "z")
VMEM = pltpu.VMEM
SMEM = pltpu.SMEM


def nn(a, b):
    return lax.dot_general(a, b, (((1,), (0,)), ((), ())), preferred_element_type=F32)


def nt(a, b):
    return lax.dot_general(a, b, (((1,), (1,)), ((), ())), preferred_element_type=F32)


def tn(a, b):
    return lax.dot_general(a, b, (((0,), (0,)), ((), ())), preferred_element_type=F32)


def x_pairs(k):
    pairs = []
    for sh in range(2):
        for xh in range(2):
            at = (2 * xh + sh + k) % 4
            pairs.append((sh * 2 + xh, (at % 2) * 2 + at // 2))
    return pairs


def to_x(v, k):
    return lax.ppermute(v, X, x_pairs(k))


def other_core(v):
    return lax.ppermute(v, "core", [(0, 1), (1, 0)])


def to_y(v, k):
    return lax.ppermute(v, "tensor", [(i, (i + k) % 4) for i in range(4)])


def to_z(v, k):
    return lax.ppermute(v, "z", [(i, (i + k) % 4) for i in range(4)])


def over_y(v):
    return lax.all_to_all(v, "tensor", 0, 0, tiled=True)


def from_each_y(v):
    return [to_y(v, 4 - k) for k in range(1, 4)]


def after(v, *others):
    return lax.optimization_barrier((v, *others))[0]


def half_of(s):
    return pl.ds(pl.multiple_of(s * HALF, HALF), HALF)


def piece_of(info, k):
    return pl.ds(pl.multiple_of(((info[4] + k) & 3) * 64, 64), 64)


def seg_at(info, layout, slot, blk, j):
    cc = info[1] if blk == 0 else 1 - info[1]
    return layout[(slot * 2 + cc) * 2 + j]


def seg_of(info, layout, blk, j):
    return seg_at(info, layout, info[2] * 2 + info[3], blk, j)


def angle_rows(at, ca, sa, cb, sb):
    ca, sa = ca[pl.ds(at, 1), :], sa[pl.ds(at, 1), :]
    return ca * cb[...] - sa * sb[...], sa * cb[...] + ca * sb[...]


def low_lanes(shape):
    return lax.broadcasted_iota(jnp.int32, shape, 1) < HD


def first_half_of_head(shape):
    return (lax.broadcasted_iota(jnp.int32, shape, 1) & (HD - 1)) < HD // 2


def rope(u, cos, sin):
    turned = jnp.where(
        first_half_of_head(u.shape), -pltpu.roll(u, 96, 1), pltpu.roll(u, 32, 1)
    )
    return u * cos + turned * sin


def unrope(u, cos, sin):
    w = u * sin
    turned = jnp.where(
        first_half_of_head(u.shape), pltpu.roll(w, 96, 1), -pltpu.roll(w, 32, 1)
    )
    return u * cos + turned


def qkv_kernel(
    info, layout, xo, xt, gain_o, gain_t, wa, wb, ra, rb, ca, sa, cb, sb, a_out, q_out, kv_out
):
    s = info[0]
    for blk, ref in enumerate((xo, xt)):
        lo = ref[:, half_of(s)].astype(F32)
        hi = ref[:, half_of(1 - s)].astype(F32)
        mean = (
            jnp.sum(lo * lo, axis=1, keepdims=True) + jnp.sum(hi * hi, axis=1, keepdims=True)
        ) / D
        inv = lax.rsqrt(mean + EPS)
        alo = (lo * inv * gain_o[...].astype(F32)).astype(B16)
        ahi = (hi * inv * gain_t[...].astype(F32)).astype(B16)
        a_out[blk * 256 : blk * 256 + 256, :HALF] = alo
        a_out[blk * 256 : blk * 256 + 256, HALF:] = ahi
        t = (
            nn(alo[:, :384], wa[...])
            + nn(alo[:, 384:], wb[...])
            + nn(ahi[:, :384], ra[...])
            + nn(ahi[:, 384:], rb[...])
        )
        for j in range(2):
            cos, sin = angle_rows(seg_of(info, layout, blk, j), ca, sa, cb, sb)
            tt = t[j * SEG : (j + 1) * SEG]
            low = low_lanes((SEG, SEG))
            t0 = rope(tt[:, :128], cos, sin)
            t1 = rope(tt[:, 128:256], cos, sin)
            t2 = tt[:, 256:]
            rows = slice(blk * 256 + j * SEG, blk * 256 + (j + 1) * SEG)
            zero = jnp.zeros_like(t0)

            def scaled(v):
                return (v.astype(B16).astype(F32) * SCALE).astype(B16)

            q_out[0, rows] = scaled(jnp.where(low, t0, zero))
            q_out[1, rows] = scaled(jnp.where(low, pltpu.roll(t0, HD, 1), zero))
            q_out[2, rows] = scaled(jnp.where(low, t1, zero))
            kv = jnp.where(low, pltpu.roll(t1, HD, 1), t2).astype(B16)
            for slot in range(8):
                kv_out[slot, rows] = kv


def fill_sorted(info, layout, slots, ks, kst):
    for slot in range(8):
        for blk in range(2):
            for j in range(2):
                at = pl.multiple_of(seg_at(info, layout, slot, blk, j) * SEG, SEG)
                part = slots[slot, blk * 256 + j * SEG : blk * 256 + (j + 1) * SEG, :]
                ks[pl.ds(at, SEG), :] = part
                kst[:, pl.ds(at, SEG)] = part.astype(F32).T.astype(B16)


def allowed_keys(j, pos):
    key = j * CHUNK + lax.broadcasted_iota(jnp.int32, (CHUNK, ROWS), 0)
    query = pos * SEG + (lax.broadcasted_iota(jnp.int32, (CHUNK, ROWS), 1) & (SEG - 1))
    return key <= query


def heads_of(q, i):
    return jnp.concatenate([q[h, i * SEG : (i + 1) * SEG, :] for h in range(3)], axis=0)


def attend_kernel(info, layout, q, slots, o_out, o_send, lse_out, ks, kst):
    fill_sorted(info, layout, slots, ks, kst)
    low = low_lanes((SEG, SEG))
    for pair in range(2):
        at_pos = [seg_of(info, layout, pair, n) for n in range(2)]
        qs = [heads_of(q, pair * 2 + n) for n in range(2)]
        full = [lax.div(p, CHUNK // SEG) for p in at_pos]

        def one(j, carry, n, edge):
            top, total, acc = carry
            at = pl.multiple_of(j * CHUNK, CHUNK)
            sc = nt(ks[pl.ds(at, CHUNK), :], qs[n])
            if edge:
                sc = jnp.where(allowed_keys(j, at_pos[n]), sc, NEG)
            new = jnp.maximum(top, jnp.max(sc, axis=0, keepdims=True))
            e = jnp.exp(sc - new)
            back = jnp.exp(top - new)
            total = total * back + jnp.sum(e, axis=0, keepdims=True)
            acc = acc * back + nn(kst[:, pl.ds(at, CHUNK)], e.astype(B16))
            return new, total, acc

        start = (
            jnp.full((1, ROWS), NEG, F32),
            jnp.zeros((1, ROWS), F32),
            jnp.zeros((SEG, ROWS), F32),
        )
        both = jnp.minimum(full[0], full[1])

        def two(j, carry):
            return one(j, carry[0], 0, False), one(j, carry[1], 1, False)

        carry = lax.fori_loop(0, both, two, (start, start))
        rest = [
            lax.fori_loop(both, full[n], lambda j, c, n=n: one(j, c, n, False), carry[n])
            for n in range(2)
        ]
        ends = [one(full[n], rest[n], n, True) for n in range(2)]
        for n in range(2):
            i = pair * 2 + n
            top, total, acc = ends[n]
            lse_out[i] = top + jnp.log(total)
            o = (acc / total).T
            o0, o1, o2 = o[:SEG], o[SEG : 2 * SEG], o[2 * SEG :]
            left = jnp.where(low, pltpu.roll(o0, HD, 1), o1).astype(B16)
            right = jnp.where(low, pltpu.roll(o2, HD, 1), jnp.zeros_like(o2)).astype(B16)
            for out, at in ((o_out, i * SEG),) + (((o_send, (i - 2) * SEG),) if i >= 2 else ()):
                out[at : at + SEG, :SEG] = left
                out[at : at + SEG, SEG:] = right


def attend_back_kernel(
    info, layout, q, do_own, do_oth, o, lse, ca, sa, cb, sb, ks, kst, dq_out, dkv_out, dkv
):
    dkv[...] = jnp.zeros_like(dkv)
    low = low_lanes((SEG, SEG))

    def spread(t0, t1):
        zero = jnp.zeros((SEG, SEG), F32)
        return jnp.concatenate(
            [
                jnp.where(low, zero, pltpu.roll(t0, HD, 1)),
                jnp.where(low, zero, t0),
                jnp.where(low, zero, pltpu.roll(t1, HD, 1)),
            ],
            axis=0,
        )

    for pair in range(2):
        at_pos = [seg_of(info, layout, pair, n) for n in range(2)]
        qs, dos, deltas, lses = [], [], [], []
        do, at = (do_own, 0) if pair == 0 else (do_oth, 256)
        for n in range(2):
            rows = slice((pair * 2 + n) * SEG, (pair * 2 + n + 1) * SEG)
            here = slice(n * SEG, (n + 1) * SEG)
            dof = spread(
                do[here, at : at + SEG].astype(F32), do[here, at + SEG : at + 2 * SEG].astype(F32)
            )
            of = spread(o[rows, :SEG].astype(F32), o[rows, SEG:].astype(F32))
            qs.append(heads_of(q, pair * 2 + n))
            dos.append(dof.astype(B16))
            deltas.append(jnp.sum((dof * of).T, axis=0, keepdims=True))
            lses.append(lse[pair * 2 + n])
        full = [lax.div(p, CHUNK // SEG) for p in at_pos]

        def one(j, acc, n, edge):
            at = pl.multiple_of(j * CHUNK, CHUNK)
            kv = ks[pl.ds(at, CHUNK), :]
            p = jnp.exp(nt(kv, qs[n]) - lses[n])
            if edge:
                p = jnp.where(allowed_keys(j, at_pos[n]), p, 0.0)
            ds = (p * (nt(kv, dos[n]) - deltas[n])).astype(B16)
            return (
                acc + nn(kst[:, pl.ds(at, CHUNK)], ds),
                nn(ds, qs[n]) + nn(p.astype(B16), dos[n]),
            )

        def alone(j, acc, n, edge=False):
            acc, more = one(j, acc, n, edge)
            dkv[pl.ds(pl.multiple_of(j * CHUNK, CHUNK), CHUNK), :] += more
            return acc

        def two(j, accs):
            a0, m0 = one(j, accs[0], 0, False)
            a1, m1 = one(j, accs[1], 1, False)
            dkv[pl.ds(pl.multiple_of(j * CHUNK, CHUNK), CHUNK), :] += m0 + m1
            return a0, a1

        zero = jnp.zeros((SEG, ROWS), F32)
        both = jnp.minimum(full[0], full[1])
        accs = lax.fori_loop(0, both, two, (zero, zero))
        accs = [
            lax.fori_loop(both, full[n], lambda j, c, n=n: alone(j, c, n), accs[n])
            for n in range(2)
        ]
        accs = [alone(full[n], accs[n], n, True) for n in range(2)]
        for n in range(2):
            rows = slice((pair * 2 + n) * SEG, (pair * 2 + n + 1) * SEG)
            dq = accs[n].T * SCALE
            cos, sin = angle_rows(at_pos[n], ca, sa, cb, sb)
            d0, d1, d2 = [unrope(dq[h * SEG : (h + 1) * SEG], cos, sin) for h in range(3)]
            dq_out[rows, :SEG] = jnp.where(low, d0, pltpu.roll(d1, HD, 1)).astype(B16)
            dq_out[rows, SEG:] = jnp.where(low, d2, jnp.zeros_like(d2)).astype(B16)
    for slot in range(8):
        for blk in range(2):
            for j in range(2):
                at = pl.multiple_of(seg_at(info, layout, slot, blk, j) * SEG, SEG)
                dkv_out[slot, blk * 256 + j * SEG : blk * 256 + (j + 1) * SEG, :] = dkv[
                    pl.ds(at, SEG), :
                ].astype(B16)


def token_kernel(info, x, o, w_own, w_oth, gain_o, gain_t, h_out, b_out):
    s = info[0]
    here = piece_of(info, 0)
    alo = jnp.zeros((64, HALF), F32)
    ahi = jnp.zeros((64, HALF), F32)
    for y in range(4):
        for part, w in ((o[y, :, :192], w_own), (o[y, :, 256:448], w_oth)):
            alo += nn(part, w[y, 0])
            ahi += nn(part, w[y, 1])
    lo = x[here, half_of(s)].astype(F32) + alo
    hi = x[here, half_of(1 - s)].astype(F32) + ahi
    mean = (
        jnp.sum(lo * lo, axis=1, keepdims=True) + jnp.sum(hi * hi, axis=1, keepdims=True)
    ) / D
    inv = lax.rsqrt(mean + EPS)
    h_out[:, :HALF] = lo
    h_out[:, HALF:] = hi
    blo = (lo * inv * gain_o[...].astype(F32)).astype(B16)
    bhi = (hi * inv * gain_t[...].astype(F32)).astype(B16)
    b_out[:, :HALF] = blo
    b_out[:, HALF:] = bhi


def norm_back(grads, sources, gains):
    mean = sum(jnp.sum(v * v, axis=1, keepdims=True) for v in sources) / D
    inv = lax.rsqrt(mean + EPS)
    weighted = [d * g for d, g in zip(grads, gains)]
    dot = sum(jnp.sum(w * v, axis=1, keepdims=True) for w, v in zip(weighted, sources)) / D
    cube = inv * inv * inv * dot
    return (
        [inv * w - v * cube for w, v in zip(weighted, sources)],
        [jnp.sum(d * v * inv, axis=0, keepdims=True) for d, v in zip(grads, sources)],
    )


def fold_kernel(info, own, received, out0, out1, out2, out3, *rest):
    for k, out in enumerate((out0, out1, out2, out3)):
        rows = piece_of(info, k)
        out[...] = (own[rows].astype(F32) + received[rows].astype(F32)).astype(out.dtype)
    if rest:
        total = own[256:].astype(F32) + received[256:].astype(F32)
        rest[0][...] = total.astype(B16).reshape(4, 64, D)


def token_back_kernel(
    info, h, d0, d1, d2, d3, moe, g, w_own, w_oth, gain_o, gain_t, dh_out, both_out, do_out, gain_out
):
    s = info[0]
    here = piece_of(info, 0)
    total = sum(d[...].astype(F32) for d in (d0, d1, d2, d3))
    halves = (slice(0, HALF), slice(HALF, D))
    back, gsum = norm_back(
        [total[:, k] for k in halves],
        [h[:, k] for k in halves],
        [gain_o[...].astype(F32), gain_t[...].astype(F32)],
    )
    for k, part, sums, half in zip(halves, back, gsum, (s, 1 - s)):
        dh = g[here, half_of(half)].astype(F32) + part
        dh_out[:, k] = dh
        for y in range(4):
            both_out[y, :64, k] = dh.astype(B16)
            both_out[y, 64:, k] = moe[y, :, k]
        gain_out[:, k] = sums
    dattn = both_out[0, :64]
    pad = jnp.zeros((64, 64), B16)
    for y in range(4):
        for at, w in ((0, w_own), (256, w_oth)):
            do = nt(dattn[:, :HALF], w[y, 0]) + nt(dattn[:, HALF:], w[y, 1])
            do_out[y, :, at : at + 192] = do.astype(B16)
            do_out[y, :, at + 192 : at + 256] = pad


def input_back_kernel(info, dh, d0, d1, d2, d3, x, gain_o, gain_t, h, both, out):
    s = info[0]
    here = piece_of(info, 0)
    total = sum(d[...].astype(F32) for d in (d0, d1, d2, d3))
    halves = (slice(0, HALF), slice(HALF, D))
    back, _ = norm_back(
        [total[:, k] for k in halves],
        [x[here, half_of(half)].astype(F32) for half in (s, 1 - s)],
        [gain_o[...].astype(F32), gain_t[...].astype(F32)],
    )
    for k, part in zip(halves, back):
        out[:64, k] = (dh[:, k] + part).astype(B16)
    out[64:] = (h[...] + sum(both[y, 64:].astype(F32) for y in range(4))).astype(B16)


def place_kernel(info, p0, p1, p2, p3, grad, y):
    s = info[0]
    for k, p in enumerate((p0, p1, p2, p3)):
        for n, out in enumerate((grad, y)):
            rows = slice(n * 64, (n + 1) * 64)
            out[piece_of(info, k), half_of(s)] = p[rows, :HALF].astype(out.dtype)
            out[piece_of(info, k), half_of(1 - s)] = p[rows, HALF:].astype(out.dtype)


def qkv_back_kernel(
    info, layout, dq, dkv, wa, wb, ra, rb, ca, sa, cb, sb, d_out, da_own, da_oth
):
    for i in range(4):
        rows = slice(i * SEG, (i + 1) * SEG)
        total = sum(dkv[r, rows].astype(F32) for r in range(8))
        cos, sin = angle_rows(seg_of(info, layout, i // 2, i % 2), ca, sa, cb, sb)
        low = low_lanes((SEG, SEG))
        dk = unrope(total, cos, sin)
        d_out[rows, :SEG] = dq[rows, :SEG]
        d_out[rows, SEG : 2 * SEG] = jnp.where(
            low, dq[rows, SEG:].astype(F32), pltpu.roll(dk, HD, 1)
        ).astype(B16)
        d_out[rows, 2 * SEG :] = jnp.where(low, jnp.zeros_like(total), total).astype(B16)
    for n, out in enumerate((da_own, da_oth)):
        d = d_out[n * 256 : (n + 1) * 256, :]
        for m, w in enumerate((wa, wb, ra, rb)):
            out[:, m * 384 : (m + 1) * 384] = nt(d, w[...]).astype(B16)


def early_grad_kernel(info, a, dq, own, oth, o, wa, wb, ra, rb, out, along_out):
    s = info[0]
    low = low_lanes((384, SEG))
    for m, w in enumerate((wa, wb, ra, rb)):
        k = slice(m * 384, (m + 1) * 384)
        dw = tn(a[:, k], dq[...])
        dwo = jnp.zeros((384, 256), F32)
        for n, both in enumerate((own, oth)):
            for y in range(4):
                at = n * 256 + y * 64
                dwo += tn(both[y, :64, k], o[at : at + 64])
        along = dw[:, :SEG] * w[:, :SEG].astype(F32)
        along += jnp.where(low, dw[:, SEG:] * w[:, SEG : 2 * SEG].astype(F32), 0.0)
        along_out[:, k] = jnp.sum(along.T, axis=0, keepdims=True)
        last = jnp.where(low, dw[:, SEG:], pltpu.roll(dwo[:, SEG:], HD, 1))
        sh = (s + m // 2) & 1
        for z in range(4):
            at = sh * 8 + (m % 2) * 4 + z
            part = slice(z * 96, (z + 1) * 96)
            out[at, :, :SEG] = dw[part, :SEG].astype(B16)
            out[at, :, SEG : 2 * SEG] = last[part].astype(B16)
            out[at, :, 2 * SEG :] = dwo[part, :SEG].astype(B16)


def late_grad_kernel(info, a, dqkv, gain_q, gain_moe, wa, wb, ra, rb, out):
    s = info[0]
    low = low_lanes((512, SEG))
    low_w = low_lanes((384, SEG))

    def joined(low, v):
        return jnp.where(low, pltpu.roll(v[:, SEG : 2 * SEG].astype(F32), HD, 1), v[:, 2 * SEG :].astype(F32))

    d = joined(low, dqkv[...]).astype(B16)
    row = lax.broadcasted_iota(jnp.int32, (16, SEG), 0)
    for m, w in enumerate((wa, wb, ra, rb)):
        k = slice(m * 384, (m + 1) * 384)
        dw = tn(a[:, k], d)
        gain = jnp.sum((dw * joined(low_w, w[...])).T, axis=0, keepdims=True) + gain_q[:, k]
        moe = gain_moe[:, k]
        sh = (s + m // 2) & 1
        for z in range(4):
            at = sh * 8 + (m % 2) * 4 + z
            part = slice(z * 96, (z + 1) * 96)
            out[at, :96] = dw[part].astype(B16)
            pad = jnp.zeros((1, 32), F32)
            g0 = jnp.concatenate([gain[:, part], pad], axis=1)
            g1 = jnp.concatenate([moe[:, part], pad], axis=1)
            out[at, 96:] = jnp.where(row == 0, g0, jnp.where(row == 1, g1, 0.0)).astype(B16)


def lift_kernel(info, g_own, g_oth, d_own, d_ra, d_rb, out, g_out):
    s = info[0]
    hi = jnp.concatenate([d_ra[0], d_rb[0]], axis=0)

    @pl.when(pl.program_id(0) == 0)
    def _():
        for n, g in enumerate((g_own, g_oth)):
            rows = slice(n * 256, (n + 1) * 256)
            g_out[rows, :HALF] = g[:, half_of(s)]
            g_out[rows, HALF:] = g[:, half_of(1 - s)]

    out[0] = nt(g_out[:, :HALF], d_own[0]) + nt(g_out[:, HALF:], hi)


def expert_kernel(
    info, b0, b1, b2, b3, b4, b5, b6, b7, w, gd, g_own, g_oth, u_own, u_oth, d_own, d_ra, d_rb,
    out_own, out_oth, hw_out, dgu_out, b, wlo, whi, dlo, dhi, dall, hall,
):
    e = pl.program_id(0)
    lo = jnp.concatenate([g_own[0], u_own[0]], axis=1)
    hi = jnp.concatenate([g_oth[0], u_oth[0]], axis=1)
    pair = pl.ds(pl.multiple_of(e * 2 * FC, 2 * FC), 2 * FC)
    one = pl.ds(pl.multiple_of(e * FC, FC), FC)
    wlo[:, pair] = lo
    whi[:, pair] = hi
    dlo[one] = d_own[0]
    dhi[one] = jnp.concatenate([d_ra[0], d_rb[0]], axis=0)

    @pl.when(e == 0)
    def _():
        for n, ref in enumerate((b0, b1, b2, b3, b4, b5, b6, b7)):
            at = (n // 4) * 256 + ((info[4] + n) & 3) * 64
            b[pl.ds(pl.multiple_of(at, 64), 64)] = ref[...]

    for k in range(2):
        rows = slice(k * 256, (k + 1) * 256)
        gu = nn(b[rows, :HALF], lo) + nn(b[rows, HALF:], hi)
        gate, up = gu[:, :FC], gu[:, FC:]
        sg = jax.nn.sigmoid(gate)
        silu = gate * sg
        here = lax.broadcasted_iota(jnp.int32, (256, OWN), 1) == e
        weight = jnp.sum(jnp.where(here, w[rows], 0.0), axis=1, keepdims=True)
        hw = (silu * up * weight).astype(B16)
        hw_out[0, rows] = hw
        hall[rows, one] = hw
        dh = gd[0, rows] * weight
        dgate = (dh * up * sg * (1.0 + gate * (1.0 - sg))).astype(B16)
        dup = (dh * silu).astype(B16)
        d = jnp.concatenate([dgate, dup], axis=1)
        dgu_out[0, rows] = d
        dall[rows, pair] = d

    @pl.when(e == OWN - 1)
    def _():
        for n, out in enumerate((out_own, out_oth)):
            rows = slice(n * 256, (n + 1) * 256)
            for k in range(6):
                c2 = slice(k * 256, (k + 1) * 256)
                if k < 3:
                    out[:256, c2] = nt(dall[rows], wlo[c2]).astype(B16)
                    out[256:, c2] = nn(hall[rows], dlo[:, c2]).astype(B16)
                else:
                    c1 = slice((k - 3) * 256, (k - 2) * 256)
                    out[:256, c2] = nt(dall[rows], whi[c1]).astype(B16)
                    out[256:, c2] = nn(hall[rows], dhi[:, c1]).astype(B16)


def expert_grad_kernel(info, b, g, hw, dgu, *refs):
    by_x, by_z, dws, dds = refs[:5], refs[5:10], refs[10], refs[11]
    at_x = 2 * info[3] + info[0]

    def put(refs, step, k, kind, value):
        if step == 2:
            refs[2 + k // 2][k % 2, kind, 0] = value
        else:
            refs[{0: 0, 1: 1, 3: 4}[step]][k, kind, 0] = value

    for half in range(2):
        k = slice(half * HALF, (half + 1) * HALF)
        dws[...] = tn(b[:, k], dgu[0]).astype(B16)
        dds[...] = tn(hw[0], g[:, k]).astype(B16)
        for step in (half, half + 2):
            xq = ((at_x + step) & 3) >> 1
            for dz in range(4):
                at = xq * 4 + ((info[2] + dz) & 3)
                for kind in range(3):
                    if kind < 2:
                        piece = dws[
                            pl.ds(pl.multiple_of(at * 96, 32), 96), kind * FC : (kind + 1) * FC
                        ]
                    else:
                        part = dds[pl.ds(pl.multiple_of(at * 16, 16), 16), :]
                        piece = jnp.concatenate(
                            [part[:, l * FC : (l + 1) * FC] for l in range(6)], axis=0
                        )
                    put(by_x, step, dz, kind, piece[:48])
                    put(by_z, dz, step, kind, piece[48:])


def pass_on_kernel(*refs):
    for n, (mine, got) in enumerate(((0, 2), (1, 3), (4, 6), (5, 7))):
        refs[8 + n][...] = (refs[mine][...].astype(F32) + refs[got][...].astype(F32)).astype(B16)


def gather_sum_kernel(*refs):
    for n in (0, 3):
        outs = refs[6 + n // 3 * 4 : 10 + n // 3 * 4]
        for k, out in enumerate(outs):
            out[...] = sum(p[k].astype(F32) for p in refs[n : n + 3]).astype(out.dtype)


def sum_kernel(*refs):
    for n in range(2):
        refs[8 + n][...] = sum(p[...].astype(F32) for p in refs[n * 4 : n * 4 + 4]).astype(B16)


def stack_kernel(n, info, *refs):
    at = info[2] if n == 4 else info[3]
    for k, ref in enumerate(refs[:-1]):
        refs[-1][(at + k) & (n - 1)] = ref[...]


def assemble_kernel(info, *refs):
    gate, up, down = refs[10:]

    def write(e, everywhere, *by_z):
        def place(v, n, xh, z, part):
            at = xh * 4 + z
            rows = pl.ds(pl.multiple_of(at * 96 + part * 48, 16), 48)
            gate[e, rows] = v[n, 0, e].astype(F32)
            up[e, rows] = v[n, 1, e].astype(F32)
            rows = pl.ds(pl.multiple_of(at * 16, 16), 16)
            for l in range(3):
                down[e, rows, (part * 3 + l) * FC : (part * 3 + l + 1) * FC] = v[
                    n, 2, e, l * 16 : (l + 1) * 16
                ].astype(F32)

        for n in range(8):
            place(everywhere, n, n // 4, n % 4, 0)
        for k, v in enumerate(by_z):
            for xh in range(2):
                place(v, xh, xh, (info[2] + k) & 3, 1)

    @pl.when(pl.program_id(0) == 0)
    def _():
        pl.loop(0, OWN)(lambda e: write(e, *refs[:5]))

    @pl.when(pl.program_id(0) == 1)
    def _():
        pl.loop(0, OWN)(lambda e: write(e, *refs[5:10]))


def sum_grads_kernel(early, late, out):
    first = sum(early[n].astype(F32) for n in range(16)).astype(B16)
    second = sum(late[n].astype(F32) for n in range(16)).astype(B16)
    for n in range(8):
        out[n, :96, : 3 * SEG] = first
        out[n, 96:, : 3 * SEG] = jnp.zeros((16, 3 * SEG), B16)
        out[n, :, 3 * SEG :] = second


def finish_kernel(info, own, oth, wq, wk, wv, wo_out, wo):
    first = info[1] == 0
    low = low_lanes((96, SEG))
    for at in range(8):
        rows = slice(at * 96, (at + 1) * 96)
        a, b = own[at, :96].astype(F32), oth[at, :96].astype(F32)
        a, b = jnp.where(first, a, b), jnp.where(first, b, a)
        a = [a[:, n * SEG : (n + 1) * SEG] for n in range(4)]
        b = [b[:, n * SEG : (n + 1) * SEG] for n in range(4)]
        at_turn = [pltpu.roll(v, HD, 1) for v in a]
        turned = [pltpu.roll(v, HD, 1) for v in b]
        wq[rows, :SEG] = a[0]
        wq[rows, SEG : 2 * SEG] = jnp.where(low, a[1], turned[0])
        wq[rows, 2 * SEG :] = jnp.where(low, turned[0], turned[1])
        wk[rows] = jnp.where(low, a[3], turned[3])
        wv[rows] = jnp.where(low, at_turn[3], b[3])
        wo[rows, :SEG] = a[2]
        wo[rows, SEG : 2 * SEG] = jnp.where(low, at_turn[1], turned[2])
        wo[rows, 2 * SEG :] = jnp.where(low, turned[2], b[1])
    wo_out[...] = wo[...].T


def smem():
    return pl.BlockSpec(memory_space=SMEM)


def whole():
    return None


def each(*shape):
    return pl.BlockSpec((1, *shape), lambda e: (e,) + (0,) * len(shape))


def fixed(*shape):
    return pl.BlockSpec(shape, lambda e: (0,) * len(shape))


def shape_of(shape, dtype):
    return jax.ShapeDtypeStruct(shape, dtype)


def cost(us):
    return pl.CostEstimate(flops=int(us * 3.3e9), bytes_accessed=int(us * 1e7), transcendentals=0)


def run(kernel, name, us, ins, in_specs, outs, out_specs, scratch=(), grid=(1,), mib=60):
    def block(spec, v):
        return fixed(*v.shape) if spec is None else spec

    return pl.pallas_call(
        kernel,
        name=name,
        grid=grid,
        in_specs=[block(spec, v) for spec, v in zip(in_specs, ins, strict=True)],
        out_specs=[block(spec, v) for spec, v in zip(out_specs, outs, strict=True)],
        out_shape=outs,
        scratch_shapes=list(scratch),
        cost_estimate=cost(us),
        compiler_params=pltpu.CompilerParams(vmem_limit_bytes=mib * 2**20),
    )(*ins)


def angle_tables():
    freq = 10000.0 ** (-np.arange(0, HD, 2) / HD)
    freq = np.tile(freq, 4)[None, :]
    coarse = np.arange(32)[:, None] * SEG * freq
    fine = np.arange(SEG)[:, None] * freq
    return tuple(
        jnp.asarray(v.astype(np.float32))
        for v in (np.cos(coarse), np.sin(coarse), np.cos(fine), np.sin(fine))
    )


def per_device(
    x,
    gain_attn,
    w_query,
    w_key,
    w_value,
    w_out,
    gain_moe,
    expert_gate,
    expert_up,
    expert_down,
    routes,
    route_gates,
    layout,
    g,
):
    s = lax.axis_index("shard")
    c = lax.axis_index("core")
    info = jnp.stack(
        [s, c, lax.axis_index("z"), lax.axis_index("xh"), lax.axis_index("tensor")]
    ).astype(jnp.int32)
    first = c == 0
    tables = angle_tables()

    def mine(v, axis):
        width = v.shape[axis] // 2
        return jnp.where(
            first,
            lax.slice_in_dim(v, 0, width, axis=axis),
            lax.slice_in_dim(v, width, 2 * width, axis=axis),
        )

    def both_cores(own, oth, axis):
        return jnp.where(
            first, jnp.concatenate([own, oth], axis), jnp.concatenate([oth, own], axis)
        )

    packed = jnp.concatenate(
        [mine(w_query, 1), mine(w_key, 1), jnp.zeros((HALF, HD), B16), mine(w_value, 1)], axis=1
    )
    wa, wb = packed[:384], packed[384:]
    ra, rb = to_x(wa, 1), to_x(wb, -1)
    x_t = other_core(x)
    wo = mine(after(w_out, wa, wb), 0)
    wo_up, wo_down = to_x(wo[:96], 1), to_x(wo[96:], -1)
    gains = jnp.stack([gain_attn, gain_moe])
    gains_t = to_x(gains, 1)
    g1o, g1t, g2o, g2t = gains[0:1], gains_t[0:1], gains[1:2], gains_t[1:2]
    a, q, kv = run(
        qkv_kernel,
        "qkv",
        0.02,
        (info, layout, x, x_t, g1o, g1t, wa, wb, ra, rb, *tables),
        [smem(), smem()] + [whole()] * 12,
        (shape_of((512, D), B16), shape_of((3, 512, 128), B16), shape_of((8, 512, 128), B16)),
        [whole()] * 3,
    )
    slots = lax.all_to_all(kv, ("z", "xh"), 0, 0, tiled=True)
    wo, wo_up, wo_down, _ = lax.optimization_barrier((wo, wo_up, wo_down, kv))
    wo_both = jnp.stack([wo, jnp.concatenate([wo_up, wo_down], axis=0)])
    wo_own = lax.all_gather(wo_both, "tensor")
    down_c = lax.dynamic_slice_in_dim(after(expert_down, kv), c * OWN, OWN, 0)
    gate_c = lax.dynamic_slice_in_dim(after(expert_gate, kv), c * OWN, OWN, 0)
    up_c = lax.dynamic_slice_in_dim(after(expert_up, kv), c * OWN, OWN, 0)
    down_a, down_b = down_c[:, :64], down_c[:, 64:]
    down_ra, down_rb = to_x(down_a, 1), to_x(down_b, -1)
    gate_t, up_t = to_x(gate_c, 1), to_x(up_c, -1)
    g_t = other_core(after(g, kv))
    ids = jnp.arange(EXPERTS, dtype=jnp.int32)
    share = jnp.sum(
        jnp.where(routes[:, :, None] == ids[None, None, :], route_gates[:, :, None], 0.0), axis=1
    )
    share = after(share, kv)
    share = jnp.concatenate([share, other_core(share)], axis=0)
    share = jnp.where(first, share[:, :OWN], share[:, OWN:])
    o, o_send, lse, ks, kst = run(
        attend_kernel,
        "attend",
        14,
        (info, layout, after(q, share, g_t, gate_c, up_c, down_c, down_a, down_b), slots),
        [smem(), smem()] + [whole()] * 2,
        (
            shape_of((512, 256), B16),
            shape_of((256, 256), B16),
            shape_of((4, 1, ROWS), F32),
            shape_of((4096, 128), B16),
            shape_of((128, 4096), B16),
        ),
        [whole()] * 5,
    )
    o_send = after(o_send, gate_t, up_t)
    o_got = other_core(o_send)
    wo_oth = other_core(after(wo_own, o_got))
    o_all = jnp.concatenate([o[:256], o_got], axis=1)
    o_tok = over_y(o_all.reshape(4, 64, 512))
    h, b64 = run(
        token_kernel,
        "token",
        0.02,
        (info, x, o_tok, wo_own, wo_oth, g2o, g2t),
        [smem()] + [whole()] * 6,
        (shape_of((64, D), F32), shape_of((64, D), B16)),
        [whole()] * 2,
    )
    lifted, g_roll = run(
        lift_kernel,
        "lift",
        6,
        (info, after(g, b64), g_t, down_c, down_ra, down_rb),
        [smem(), fixed(256, D), fixed(256, D), each(FC, HALF), each(64, HALF), each(64, HALF)],
        (shape_of((OWN, 512, FC), F32), shape_of((512, D), B16)),
        [each(512, FC), fixed(512, D)],
        grid=(OWN,),
    )
    b_own = [b64, *from_each_y(b64)]
    b_own = b_own[:1] + [after(v, lifted) for v in b_own[1:]]
    b_oth = [other_core(v) for v in b_own]
    out_own, out_oth, hw, dgu, b = run(
        expert_kernel,
        "expert",
        0.02,
        (info, *b_own, *b_oth, share, lifted, gate_c, gate_t, up_c, up_t, down_c, down_ra, down_rb),
        [smem()]
        + [whole()] * 9
        + [each(512, FC)]
        + [each(HALF, FC)] * 4
        + [each(FC, HALF), each(64, HALF), each(64, HALF)],
        (
            shape_of((512, D), B16),
            shape_of((512, D), B16),
            shape_of((OWN, 512, FC), B16),
            shape_of((OWN, 512, 2 * FC), B16),
            shape_of((512, D), B16),
        ),
        [whole(), whole(), each(512, FC), each(512, 2 * FC), whole()],
        scratch=[
            VMEM((HALF, 2 * FC * OWN), B16),
            VMEM((HALF, 2 * FC * OWN), B16),
            VMEM((FC * OWN, HALF), B16),
            VMEM((FC * OWN, HALF), B16),
            VMEM((512, 2 * FC * OWN), B16),
            VMEM((512, FC * OWN), B16),
        ],
        grid=(OWN,),
    )

    def to_tokens(own, oth, name):
        outs = (shape_of((64, D), F32),) + (shape_of((64, D), B16),) * 3
        if own.shape[0] > 256:
            outs += (shape_of((4, 64, D), B16),)
        return run(
            fold_kernel,
            name,
            2,
            (info, own, other_core(oth)),
            [smem()] + [whole()] * 2,
            outs,
            [whole()] * len(outs),
        )

    def over_pieces(parts):
        return [parts[0]] + [to_y(parts[k], k) for k in range(1, 4)]

    *db, moe = to_tokens(out_own, out_oth, "fold_b")
    halves = shape_of((2, 3, OWN, 48, FC), B16)
    quarter = shape_of((4, 3, OWN, 48, FC), B16)

    def by_expert(n):
        return pl.BlockSpec((n, 3, 1, 48, FC), lambda e: (0, 0, e, 0, 0))

    sent = run(
        expert_grad_kernel,
        "expert_grad",
        9,
        (info, after(b, db[1]), g_roll, hw, dgu),
        [smem(), fixed(512, D), fixed(512, D), each(512, FC), each(512, 2 * FC)],
        (quarter, quarter, halves, halves, quarter) * 2,
        [by_expert(4), by_expert(4), by_expert(2), by_expert(2), by_expert(4)] * 2,
        scratch=[VMEM((HALF, 2 * FC), B16), VMEM((FC, HALF), B16)],
        grid=(OWN,),
    )
    flat = (3 * OWN * 48, FC)
    sent = [v.reshape(-1, *flat) for v in sent]
    xs, zs = sent[:5], sent[5:]
    db = over_pieces(db)
    db[0] = after(db[0], *sent)
    dh, both, do_tok, gsum_moe = run(
        token_back_kernel,
        "token_back",
        0.02,
        (info, h, *db, moe, g, wo_own, wo_oth, g2o, g2t),
        [smem()] + [whole()] * 11,
        (
            shape_of((64, D), F32),
            shape_of((4, 128, D), B16),
            shape_of((4, 64, 512), B16),
            shape_of((1, D), F32),
        ),
        [whole()] * 4,
    )
    xs[2], xs[3], zs[2], zs[3], _ = lax.optimization_barrier((xs[2], xs[3], zs[2], zs[3], dh))
    passing = (to_x(xs[2], 1), to_x(xs[3], -1), to_z(zs[2], 1), to_z(zs[3], -1))
    do = over_y(do_tok).reshape(256, 512)
    do_oth = other_core(do)
    four = shape_of((4, *flat), B16)
    def half(n):
        return pl.BlockSpec((2, *flat), lambda e: (n, 0, 0))

    x_up, x_down, z_up, z_down = pl.pallas_call(
        pass_on_kernel,
        name="pass_on",
        grid=(1,),
        in_specs=[half(0), half(1), half(0), half(0)] * 2,
        out_specs=[half(0), half(1)] * 2,
        out_shape=(four,) * 4,
        input_output_aliases={0: 0, 1: 1, 4: 2, 5: 3},
        cost_estimate=cost(0.02),
        compiler_params=pltpu.CompilerParams(vmem_limit_bytes=60 * 2**20),
    )(xs[1], xs[4], *passing[:2], zs[1], zs[4], *passing[2:])
    got = (to_x(x_up, 1), to_x(x_down, -1), to_z(z_up, 1), to_z(z_down, -1))

    do = after(do, x_up)
    both = over_y(after(both, do))
    dq, dkv = run(
        attend_back_kernel,
        "attend_back",
        16,
        (info, layout, q, do, do_oth, o, lse, *tables, ks, kst),
        [smem(), smem()] + [whole()] * 11,
        (shape_of((512, 256), B16), shape_of((8, 512, 128), B16)),
        [whole()] * 2,
        scratch=[VMEM((4096, 128), F32)],
    )
    dkv = lax.all_to_all(after(dkv, *got, both), ("z", "xh"), 0, 0, tiled=True)

    one, one32 = shape_of(flat, B16), shape_of(flat, F32)
    xz = run(
        gather_sum_kernel,
        "plane_sum",
        0.02,
        (after(xs[0], dq), *got[:2], zs[0], *got[2:]),
        [whole()] * 6,
        (one32, one, one, one) * 2,
        [whole()] * 8,
    )
    both_oth = other_core(after(both, xz[1]))
    early, gain_q = run(
        early_grad_kernel,
        "early_grad",
        1,
        (info, a, after(dq, xz[1]), both, both_oth, o, wa, wb, ra, rb),
        [smem()] + [whole()] * 9,
        (shape_of((16, 96, 384), B16), shape_of((1, D), F32)),
        [whole()] * 2,
    )
    xz = list(xz)
    xz[2], xz[6], _ = lax.optimization_barrier((xz[2], xz[6], gain_q))
    second = [xz[0]] + [to_z(xz[k], k) for k in range(1, 4)]
    second += [xz[4]] + [to_x(xz[4 + k], k) for k in range(1, 4)]
    early = lax.all_to_all(after(early, dkv), PLANE, 0, 0, tiled=True)
    dkv = after(dkv, gain_q)
    dqkv, da_own, da_oth = run(
        qkv_back_kernel,
        "qkv_back",
        6,
        (info, layout, dq, dkv, wa, wb, ra, rb, *tables),
        [smem(), smem()] + [whole()] * 10,
        (shape_of((512, 384), B16), shape_of((256, D), B16), shape_of((256, D), B16)),
        [whole()] * 3,
    )
    ea, eb = run(
        sum_kernel, "plane_sum2", 1, (after(second[0], dqkv), *second[1:]), [whole()] * 8, (one, one), [whole()] * 2
    )

    def stacked(arrays, name):
        n = len(arrays)
        return run(
            functools.partial(stack_kernel, n),
            name,
            1,
            (info, *arrays),
            [smem()] + [whole()] * n,
            (shape_of((n, *flat), B16),),
            [whole()],
        )[0]

    eb_pair = stacked([eb, to_x(eb, 2)], "along_x")
    da = over_pieces(to_tokens(da_own, da_oth, "fold_a"))
    late = run(
        late_grad_kernel,
        "late_grad",
        0.02,
        (info, a, after(dqkv, ea, eb, early, eb_pair, da[1], da[2], da[3]), gain_q, gsum_moe, wa, wb, ra, rb),
        [smem()] + [whole()] * 8,
        (shape_of((16, 112, 128), B16),),
        [whole()],
    )[0]
    grads_in = late
    late = lax.all_to_all(late, PLANE, 0, 0, tiled=True)
    ea = lax.all_gather(ea, ("xh", "z"))
    e_own = [ea, eb_pair] + [to_z(eb_pair, 4 - k) for k in range(1, 4)]
    da[0] = after(da[0], eb_pair)

    ig = run(
        input_back_kernel,
        "input_back",
        0.02,
        (info, dh, *da, x, g1o, g1t, h, both),
        [smem()] + [whole()] * 10,
        (shape_of((128, D), B16),),
        [whole()],
    )[0]


    late = after(late, ig, *e_own[2:])
    grads = run(
        sum_grads_kernel,
        "sum_grads",
        0.02,
        (early, late),
        [whole()] * 2,
        (shape_of((8, 112, 512), B16),),
        [whole()],
    )[0]
    ig_parts = from_each_y(ig)
    e_own[0] = after(e_own[0], grads, ig_parts[0])
    e_own = [v.reshape(-1, 3, OWN, 48, FC) for v in e_own]
    e_oth = [other_core(v) for v in e_own]
    expert_grads = pl.pallas_call(
        assemble_kernel,
        name="assemble",
        grid_spec=pltpu.PrefetchScalarGridSpec(
            num_scalar_prefetch=1,
            grid=(2,),
            in_specs=[
                pl.BlockSpec((n, 3, OWN, 48, FC), lambda q, info: (0, 0, 0, 0, 0))
                for n in (8, 2, 2, 2, 2) * 2
            ],
            out_specs=[
                pl.BlockSpec((OWN, *shape), lambda q, info: ((info[1] + q) & 1, 0, 0))
                for shape in ((HALF, FC), (HALF, FC), (FC, HALF))
            ],
        ),
        out_shape=(
            shape_of((EXPERTS, HALF, FC), F32),
            shape_of((EXPERTS, HALF, FC), F32),
            shape_of((EXPERTS, FC, HALF), F32),
        ),
        cost_estimate=cost(0.02),
        compiler_params=pltpu.CompilerParams(vmem_limit_bytes=60 * 2**20),
    )(info, *e_own, *e_oth)
    input_grad, output = run(
        place_kernel,
        "place",
        0.02,
        (info, after(ig, expert_grads[0]), *ig_parts),
        [smem()] + [whole()] * 4,
        (shape_of((256, D), F32), shape_of((256, D), B16)),
        [whole()] * 2,
    )

    grads = lax.all_to_all(
        grads, ("xh", "z"), 0, 0, tiled=True
    )
    grads = after(grads, input_grad)
    grads_t = other_core(grads)
    gsum = grads[:, 96:98, 384:480].astype(F32).transpose(1, 0, 2).reshape(2, HALF)
    gsum = gsum + sum(from_each_y(gsum))
    gsum = gsum + other_core(gsum)

    wq_grad, wk_grad, wv_grad, wo_grad = run(
        finish_kernel,
        "finish",
        0.02,
        (info, grads, after(grads_t, expert_grads[0])),
        [smem()] + [whole()] * 2,
        tuple(shape_of(v, F32) for v in ((HALF, 384), (HALF, 128), (HALF, 128), (384, HALF))),
        [whole()] * 4,
        scratch=[VMEM((HALF, 384), F32)],
    )
    return (
        output,
        input_grad,
        gsum[0] / gain_attn.astype(F32),
        wq_grad,
        wk_grad,
        wv_grad,
        wo_grad,
        gsum[1],
        *expert_grads,
    )


def solution(mesh):
    fine = Mesh(
        mesh.devices.reshape(2, 4, 2, 2, 4), ("shard", "z", "xh", "core", "tensor")
    )
    rows = P(("shard", "z", "xh", "core"), None)
    placed = (
        rows,
        P("shard"),
        P("shard", "tensor"),
        P("shard", "tensor"),
        P("shard", "tensor"),
        P("tensor", "shard"),
        P("shard"),
        P(None, "shard", "tensor"),
        P(None, "shard", "tensor"),
        P(None, "tensor", "shard"),
        rows,
        rows,
        P(),
        rows,
    )
    return jax.shard_map(
        per_device,
        mesh=fine,
        in_specs=placed,
        out_specs=(
            rows,
            rows,
            P("shard"),
            P("shard", "tensor"),
            P("shard", "tensor"),
            P("shard", "tensor"),
            P("tensor", "shard"),
            P("shard"),
            P(None, "shard", "tensor"),
            P(None, "shard", "tensor"),
            P(None, "tensor", "shard"),
        ),
        check_vma=False,
    )
```
